128 devices in a mesh: tok: 8 (over x, y_hi), voc: 16 (over y_lo, z, core).
Axes of the slice: x: 4, y: 4 (y_hi: 2, y_lo: 2; y = y_hi * 2 + y_lo), z: 4, core: 2. Of those that a mesh axis runs over, the one named last changes fastest.
Arguments:
- teacher_hidden: bfloat16 [256, 4096], P(None, 'tok'), may hold values from -70 to 70
- teacher_head: bfloat16 [4096, 8, 12288], P('tok', None, 'voc')
- student_hidden: bfloat16 [256, 2, 2560], P(('tok', 'voc')), may hold values from -60 to 60
- student_head: bfloat16 [2560, 98304], P(None, ('tok', 'voc'))
- target_ids: int32 [256, 2], replicated, may hold values from 0 to 98303
Outputs:
- sample_objective: float32 [256, 2], replicated
- grad_hidden: bfloat16 [256, 2, 2560], P(('tok', 'voc'))
- grad_head: bfloat16 [2560, 98304], P(None, ('tok', 'voc'))
The draws below stay inside these ranges and needn't reach their ends.
All inputs are finite; a program needn't handle non-finite values.
Results may differ from the reference program's by a relative error of at most 0.0044.
Values may be sent and summed in bfloat16 or wider, within the bound.
No kernel may reach another device: no remote copies, remote signals or barrier semaphores. Data moves between devices by JAX's collectives and lax.ppermute only.
A program may use at most 128 MiB of HBM per device.

```python
import math
import jax
import jax.numpy as jnp
import numpy as np
from jax import lax

D = 4096
DS = 2560
VOCAB = 98304
ROWS = 256
N_TOK = 8


def log_factors(scale_key, extent, lowest, highest):
    return jnp.exp(jax.random.uniform(scale_key, extent, minval=math.log(lowest), maxval=math.log(highest)))


def mixed_factors(scale_key, extent, flat_low, flat_high, peak_low, peak_high):
    pick_key, flat_key, peak_key = jax.random.split(scale_key, 3)
    flat_part = log_factors(flat_key, extent, flat_low, flat_high)
    peak_part = log_factors(peak_key, extent, peak_low, peak_high)
    chosen = jax.random.bernoulli(pick_key, 0.125, extent)
    return jnp.where(chosen, peak_part, flat_part)


def draw_teacher_hidden(key, part):
    key = jax.random.fold_in(key, 11)
    scale_key, value_key = jax.random.split(key)
    factors = mixed_factors(scale_key, (ROWS, 1), 0.6, 2.0, 2.0, 10.0)
    values = jnp.clip(jax.random.normal(value_key, (ROWS, D)), -4.0, 4.0)
    return (values * factors).astype(jnp.bfloat16)


def draw_student_hidden(key, part):
    key = jax.random.fold_in(key, 23)
    scale_key, value_key = jax.random.split(key)
    factors = mixed_factors(scale_key, (ROWS, 2, 1), 0.7, 1.8, 1.8, 8.0)
    values = jnp.clip(jax.random.normal(value_key, (ROWS, 2, DS)), -4.0, 4.0)
    return (values * factors).astype(jnp.bfloat16)


def draw_teacher_head(key, part):
    key = jax.random.fold_in(key, 37)
    scale_key, value_key = jax.random.split(key)
    factors = log_factors(scale_key, (1, N_TOK, VOCAB // N_TOK), 0.4, 2.5)
    values = jnp.clip(jax.random.normal(value_key, (D, N_TOK, VOCAB // N_TOK)), -4.0, 4.0)
    return (values * factors * (3.0 / math.sqrt(D))).astype(jnp.bfloat16)


def draw_student_head(key, part):
    key = jax.random.fold_in(key, 41)
    scale_key, value_key = jax.random.split(key)
    factors = log_factors(scale_key, (1, VOCAB), 0.5, 2.0)
    values = jnp.clip(jax.random.normal(value_key, (DS, VOCAB)), -4.0, 4.0)
    return (values * factors * (3.0 / math.sqrt(DS))).astype(jnp.bfloat16)


def plant(entries, key, smallest, largest):
    spot = [jax.random.randint(jax.random.fold_in(key, axis), (), 0, length) for axis, length in enumerate(entries.shape)]
    longest = entries.shape.index(max(entries.shape))
    beside = spot[:longest] + [(spot[longest] + 1) % entries.shape[longest]] + spot[longest + 1:]
    return entries.at[tuple(spot)].set(smallest).at[tuple(beside)].set(largest)


def skewed_wide(rng, dims, number_of, skew):
    portions = [min(1 << octave, number_of + 1 - (1 << octave)) * (1 << 20) // math.isqrt((1 << octave) ** skew) + 1 for octave in range((number_of + 1).bit_length()) if 1 << octave <= number_of]
    width = 1 + sum(portions) // (1 << 30)
    listing = np.cumsum(np.array([max(1, weight // width) for weight in portions]))
    pick = jax.random.randint(jax.random.fold_in(rng, 1), dims, 0, int(listing[len(portions) - 1]))
    start = jnp.left_shift(1, jnp.searchsorted(jnp.asarray(listing, jnp.int32), pick, side="right").astype(jnp.int32))
    grade = start - 1 + jax.random.randint(jax.random.fold_in(rng, 4), dims, 0, 1 << 30) % jnp.minimum(start, number_of + 1 - start)
    return jax.random.permutation(jax.random.fold_in(rng, 2), number_of)[grade].astype(jnp.int32)


def setup_inputs(seed: int = 0) -> dict:
    streams_of = jax.random.split(jax.random.key(seed), 6)
    teacher_hidden = draw_teacher_hidden(jax.random.fold_in(streams_of[5], 71), 0)
    teacher_head = draw_teacher_head(jax.random.fold_in(streams_of[5], 71), 0)
    student_hidden = draw_student_hidden(jax.random.fold_in(streams_of[5], 71), 0)
    student_head = draw_student_head(jax.random.fold_in(streams_of[5], 71), 0)
    target_ids = plant(skewed_wide(streams_of[4], (ROWS, 2), VOCAB, 2), jax.random.fold_in(streams_of[4], 3), 0, VOCAB - 1).astype(jnp.int32)
    return {"teacher_hidden": teacher_hidden, "teacher_head": teacher_head, "student_hidden": student_hidden, "student_head": student_head, "target_ids": target_ids}


smoothing_scale = 2.0
distill_coefficient = 0.5


def shift_rows(values, fill):
    return jnp.concatenate([values[1:], jnp.full_like(values[:1], fill)], axis=0)


def reference(teacher_hidden, teacher_head, student_hidden, student_head, target_ids):
    flat_head = teacher_head.reshape(D, VOCAB)
    tutor_scores = jnp.dot(teacher_hidden, flat_head, preferred_element_type=jnp.float32)
    scaled_scores = tutor_scores / smoothing_scale
    maxima = jnp.max(scaled_scores, axis=1, keepdims=True)
    teacher_logprob = scaled_scores - (maxima + jnp.log(jnp.sum(jnp.exp(scaled_scores - maxima), axis=1, keepdims=True)))
    correct_class_logscore = jnp.stack([teacher_logprob, shift_rows(teacher_logprob, 0.0)], axis=1)
    pupil_scores = jnp.dot(student_hidden.reshape(ROWS * 2, DS), student_head,
                             preferred_element_type=jnp.float32).reshape(ROWS, 2, VOCAB)
    pupil_peak_score = jnp.max(pupil_scores, axis=2)
    shifted_scores = pupil_scores - pupil_peak_score[:, :, None]
    exp_one = jnp.exp(shifted_scores)
    scaled_exponential = jnp.exp(shifted_scores / smoothing_scale)
    sum_one = jnp.sum(exp_one, axis=2)
    scaled_accumulation = jnp.sum(scaled_exponential, axis=2)
    tutor_likelihood = jnp.exp(correct_class_logscore)
    mixed_expectation = jnp.sum(tutor_likelihood * (correct_class_logscore - pupil_scores / smoothing_scale), axis=2)
    columns = lax.broadcasted_iota(jnp.int32, (1, 1, VOCAB), 2)
    matches = columns == target_ids[:, :, None]
    target_logit = jnp.sum(jnp.where(matches, pupil_scores, 0.0), axis=2)
    lse_one = pupil_peak_score + jnp.log(sum_one)
    scaled_normalizer = pupil_peak_score / smoothing_scale + jnp.log(scaled_accumulation)
    row_index = lax.broadcasted_iota(jnp.int32, (ROWS, 2), 0)
    head_index = lax.broadcasted_iota(jnp.int32, (ROWS, 2), 1)
    sample_coefficient = jnp.where((head_index == 1) & (row_index == ROWS - 1), 0.0, 1.0).astype(jnp.float32)
    sample_objective = sample_coefficient * (distill_coefficient * smoothing_scale ** 2 * (mixed_expectation + scaled_normalizer)
                             + (1.0 - distill_coefficient) * (lse_one - target_logit))
    score_derivative = (sample_coefficient[:, :, None] * (distill_coefficient * smoothing_scale * (scaled_exponential / scaled_accumulation[:, :, None] - tutor_likelihood)
                                            + (1.0 - distill_coefficient) * (exp_one / sum_one[:, :, None] - matches.astype(jnp.float32)))).astype(jnp.bfloat16)
    grad_flat = score_derivative.reshape(ROWS * 2, VOCAB)
    grad_hidden = lax.dot_general(grad_flat, student_head, (((1,), (1,)), ((), ())),
                                  preferred_element_type=jnp.float32).reshape(ROWS, 2, DS).astype(jnp.bfloat16)
    grad_head = lax.dot_general(student_hidden.reshape(ROWS * 2, DS), grad_flat, (((0,), (0,)), ((), ())),
                                preferred_element_type=jnp.float32).astype(jnp.bfloat16)
    return sample_objective, grad_hidden, grad_head
```

```python
import jax
import jax.numpy as jnp
from jax import lax
from jax.sharding import Mesh
from jax.sharding import PartitionSpec as P

TOK = ("x", "yh")
VOC = ("yl", "z", "c")
CHIPS = ("x", "yh", "yl", "z")
SIZES = (4, 2, 2, 4, 2)


def encode(partial):
    stripes, rows, width = partial.shape
    half = width // 2
    peak = jnp.maximum(jnp.max(jnp.abs(partial), axis=2), 1e-30)
    level = jnp.ceil(jnp.log2(peak) * 256.0)
    scale = jnp.exp2(-level / 256.0) * 32766.0
    code = jnp.clip(jnp.round(partial * scale[:, :, None]), -32767.0, 32767.0).astype(jnp.int32)
    words = (code[:, :, :half] << 16) | (code[:, :, half:] & 0xFFFF)
    tail = jnp.zeros((stripes, 8, half), jnp.int32).at[:, 0, :rows].set(level.astype(jnp.int32))
    return jnp.concatenate([words, tail], axis=1)


def decode(words, rows):
    level = words[:, rows, :rows].astype(jnp.float32)
    scale = (jnp.exp2(level / 256.0) * (0.5 / 32766.0))[:, :, None]
    body = words[:, :rows]
    high = (body >> 16).astype(jnp.float32)
    low = ((body << 16) >> 16).astype(jnp.float32)
    return jnp.concatenate([jnp.sum(high * scale, axis=0), jnp.sum(low * scale, axis=0)], axis=1)


def merge(parts):
    tp, tz, sp, s1, s2, cross, target = [parts[:, i] for i in range(7)]
    tm = jnp.max(tp, axis=0)
    sm = jnp.max(sp, axis=0)
    te = jnp.exp(tp - tm)
    se = jnp.exp((sp - sm) * 0.5)
    return jnp.stack(
        [
            tm,
            jnp.sum(tz * te, axis=0),
            sm,
            jnp.sum(s1 * (se * se), axis=0),
            jnp.sum(s2 * se, axis=0),
            jnp.sum(cross * te, axis=0),
            jnp.sum(target, axis=0),
        ]
    )


def everywhere(value, axes, count):
    copies = jnp.broadcast_to(value, (count,) + value.shape)
    return lax.all_to_all(copies, axes, 0, 0, tiled=True)


def local(teacher_hidden, teacher_head, student_hidden, student_head, target_ids):
    core = lax.axis_index("c")
    chips = lax.axis_size(CHIPS)
    stripes = teacher_head.shape[1]
    voc = teacher_head.shape[2]
    rows = teacher_hidden.shape[0]
    width = student_head.shape[0]
    base = lax.axis_index(TOK + VOC) * voc
    pair = [(0, 1), (1, 0)]

    partial = jnp.einsum("rd,dsv->srv", teacher_hidden, teacher_head, preferred_element_type=jnp.float32)
    words = lax.all_to_all(encode(partial), TOK, 0, 0, tiled=True)

    mine = jnp.swapaxes(student_hidden, 0, 1).reshape(4, width)
    own = everywhere(mine, CHIPS, chips).reshape(rows, width)
    other = lax.ppermute(own, "c", pair)
    hidden = jnp.concatenate([own, other], axis=0)
    scores = jnp.dot(hidden, student_head, preferred_element_type=jnp.float32)

    place = lax.broadcasted_iota(jnp.int32, (2 * rows, 1), 0)
    side = place // rows
    place = place % rows
    chip, head, inner = place // 4, (place // 2) % 2, place % 2
    row = chip * 4 + jnp.where(side == 0, core, 1 - core) * 2 + inner
    weight = jnp.where((head == 1) & (row == rows - 1), 0.0, 1.0).astype(jnp.float32)
    teacher_row = jnp.minimum(row + head, rows - 1)
    order = target_ids.reshape(chips, 2, 2, 2)
    order = jnp.transpose(order, (1, 0, 3, 2)).reshape(2, rows)
    ids = jnp.where(core == 0, order, order[::-1]).reshape(2 * rows, 1)
    match = lax.broadcasted_iota(jnp.int32, (1, voc), 1) + base == ids

    pick = (lax.broadcasted_iota(jnp.int32, (1, rows), 1) == teacher_row).astype(jnp.float32)
    teacher = jnp.dot(pick, decode(words, rows), precision=lax.Precision.HIGHEST)

    t_peak = jnp.max(teacher, axis=1, keepdims=True)
    t_exp = jnp.exp(teacher - t_peak)
    s_peak = jnp.max(scores, axis=1, keepdims=True)
    s_exp = jnp.exp((scores - s_peak) * 0.5)
    stats = jnp.stack(
        [
            t_peak[:, 0],
            jnp.sum(t_exp, axis=1),
            s_peak[:, 0],
            jnp.sum(s_exp * s_exp, axis=1),
            jnp.sum(s_exp, axis=1),
            jnp.sum(t_exp * (teacher - scores * 0.5), axis=1),
            jnp.sum(jnp.where(match, scores, 0.0), axis=1),
        ]
    )
    stats = jnp.where(core == 0, stats, jnp.roll(stats, rows, axis=1))
    stats = merge(everywhere(stats, VOC, lax.axis_size(VOC)))
    stats = merge(everywhere(stats, TOK, lax.axis_size(TOK)))
    tm, tz, sm, s1, s2, cross, target = [stats[i] for i in range(7)]
    t_lse = tm + jnp.log(tz)
    s_one = sm + jnp.log(s1)
    s_tau = sm * 0.5 + jnp.log(s2)
    objective = 2.0 * (cross / tz - t_lse + s_tau) + 0.5 * (s_one - target)
    objective = jnp.transpose(objective.reshape(2, chips, 2, 2), (1, 0, 3, 2)).reshape(rows, 2)
    last = (lax.broadcasted_iota(jnp.int32, (rows, 2), 0) == rows - 1) & (
        lax.broadcasted_iota(jnp.int32, (rows, 2), 1) == 1
    )
    objective = jnp.where(last, 0.0, objective)

    norms = jnp.stack([t_lse, s_one, s_tau])
    norms = jnp.where(core == 0, norms, jnp.roll(norms, rows, axis=1))[:, :, None]
    grad = weight * (
        jnp.exp(scores * 0.5 - norms[2])
        - jnp.exp(teacher - norms[0])
        + 0.5 * (jnp.exp(scores - norms[1]) - match.astype(jnp.float32))
    )
    grad = grad.astype(jnp.bfloat16)

    contract = (((1,), (1,)), ((), ()))
    give = lax.dot_general(grad[rows:], student_head, contract, preferred_element_type=jnp.float32)
    taken = lax.ppermute(give, "c", pair)
    keep = lax.dot_general(grad[:rows], student_head, contract, preferred_element_type=jnp.float32)
    grad_head = lax.dot_general(
        hidden, grad, (((0,), (0,)), ((), ())), preferred_element_type=jnp.float32
    ).astype(jnp.bfloat16)
    share = (keep + taken).astype(jnp.bfloat16).reshape(chips, 4, width)
    share = lax.all_to_all(share, CHIPS, 0, 0, tiled=True)
    grad_hidden = jnp.sum(share.astype(jnp.float32), axis=0).astype(jnp.bfloat16)
    grad_hidden = jnp.swapaxes(grad_hidden.reshape(2, 2, width), 0, 1)
    return objective, grad_hidden, grad_head


def solution(mesh):
    fine = Mesh(mesh.devices.reshape(SIZES), CHIPS + ("c",))
    return jax.shard_map(
        local,
        mesh=fine,
        in_specs=(
            P(None, TOK),
            P(TOK, None, VOC),
            P(TOK + VOC, None, None),
            P(None, TOK + VOC),
            P(),
        ),
        out_specs=(P(), P(TOK + VOC, None, None), P(None, TOK + VOC)),
        check_vma=False,
    )
```

```python
import jax
import jax.numpy as jnp
from jax import lax
from jax.sharding import Mesh
from jax.sharding import PartitionSpec as P

TOK = ("x", "yh")
VOC = ("yl", "z", "c")
CHIPS = ("x", "yh", "yl", "z")
SIZES = (4, 2, 2, 4, 2)
WALK = ("z", "yh", "yl", "x")


def encode(partial):
    stripes, rows, width = partial.shape
    half = width // 2
    peak = jnp.maximum(jnp.max(jnp.abs(partial), axis=2), 1e-30)
    level = jnp.ceil(jnp.log2(peak) * 256.0)
    scale = jnp.exp2(-level / 256.0) * 32766.0
    code = jnp.clip(jnp.round(partial * scale[:, :, None]), -32767.0, 32767.0).astype(jnp.int32)
    words = (code[:, :, :half] << 16) | (code[:, :, half:] & 0xFFFF)
    tail = jnp.zeros((stripes, 8, half), jnp.int32).at[:, 0, :rows].set(level.astype(jnp.int32))
    return jnp.concatenate([words, tail], axis=1)


def decode(words, rows):
    level = words[:, rows, :rows].astype(jnp.float32)
    scale = (jnp.exp2(level / 256.0) * (0.5 / 32766.0))[:, :, None]
    body = words[:, :rows]
    high = (body >> 16).astype(jnp.float32)
    low = ((body << 16) >> 16).astype(jnp.float32)
    return jnp.concatenate([jnp.sum(high * scale, axis=0), jnp.sum(low * scale, axis=0)], axis=1)


def merge(parts):
    tp, tz, sp, s1, s2, cross, target = [parts[:, i] for i in range(7)]
    tm = jnp.max(tp, axis=0)
    sm = jnp.max(sp, axis=0)
    te = jnp.exp(tp - tm)
    se = jnp.exp((sp - sm) * 0.5)
    return jnp.stack(
        [
            tm,
            jnp.sum(tz * te, axis=0),
            sm,
            jnp.sum(s1 * (se * se), axis=0),
            jnp.sum(s2 * se, axis=0),
            jnp.sum(cross * te, axis=0),
            jnp.sum(target, axis=0),
        ]
    )


def ring_gather(block, axes):
    size = lax.axis_size(axes)
    here = lax.axis_index(axes)
    whole = jnp.zeros((size,) + block.shape, block.dtype)
    whole = lax.dynamic_update_index_in_dim(whole, block, here, 0)
    for step in range(1, size):
        taken = lax.ppermute(block, axes, [(i, (i + step) % size) for i in range(size)])
        whole = lax.dynamic_update_index_in_dim(whole, taken, (here + size - step) % size, 0)
    return whole.reshape((size * block.shape[0],) + block.shape[1:])


def everywhere(value, axes, count):
    copies = jnp.broadcast_to(value, (count,) + value.shape)
    return lax.all_to_all(copies, axes, 0, 0, tiled=True)


def local(teacher_hidden, teacher_head, student_hidden, student_head, target_ids):
    core = lax.axis_index("c")
    chips = lax.axis_size(CHIPS)
    stripes = teacher_head.shape[1]
    voc = teacher_head.shape[2]
    rows = teacher_hidden.shape[0]
    width = student_head.shape[0]
    base = lax.axis_index(TOK + VOC) * voc
    pair = [(0, 1), (1, 0)]

    partial = jnp.einsum("rd,dsv->srv", teacher_hidden, teacher_head, preferred_element_type=jnp.float32)
    words = lax.all_to_all(encode(partial), TOK, 0, 0, tiled=True)

    own = jnp.swapaxes(student_hidden, 0, 1).reshape(4, width)
    for axes in ("x", ("yh", "yl"), "z"):
        own = ring_gather(own, axes)
    other = lax.ppermute(own, "c", pair)
    hidden = jnp.concatenate([own, other], axis=0)
    scores = jnp.dot(hidden, student_head, preferred_element_type=jnp.float32)

    place = lax.broadcasted_iota(jnp.int32, (2 * rows, 1), 0)
    side = place // rows
    place = place % rows
    head, inner = (place // 2) % 2, place % 2
    chip = (place // 4) % 4 * 16 + (place // 16) % 4 * 4 + place // 64
    row = chip * 4 + jnp.where(side == 0, core, 1 - core) * 2 + inner
    weight = jnp.where((head == 1) & (row == rows - 1), 0.0, 1.0).astype(jnp.float32)
    teacher_row = jnp.minimum(row + head, rows - 1)
    order = target_ids.reshape(4, 4, 4, 2, 2, 2)
    order = jnp.transpose(order, (3, 2, 1, 0, 5, 4)).reshape(2, rows)
    ids = jnp.where(core == 0, order, order[::-1]).reshape(2 * rows, 1)
    match = lax.broadcasted_iota(jnp.int32, (1, voc), 1) + base == ids

    pick = (lax.broadcasted_iota(jnp.int32, (1, rows), 1) == teacher_row).astype(jnp.float32)
    teacher = jnp.dot(pick, decode(words, rows), precision=lax.Precision.HIGHEST)

    t_peak = jnp.max(teacher, axis=1, keepdims=True)
    t_exp = jnp.exp(teacher - t_peak)
    s_peak = jnp.max(scores, axis=1, keepdims=True)
    s_exp = jnp.exp((scores - s_peak) * 0.5)
    stats = jnp.stack(
        [
            t_peak[:, 0],
            jnp.sum(t_exp, axis=1),
            s_peak[:, 0],
            jnp.sum(s_exp * s_exp, axis=1),
            jnp.sum(s_exp, axis=1),
            jnp.sum(t_exp * (teacher - scores * 0.5), axis=1),
            jnp.sum(jnp.where(match, scores, 0.0), axis=1),
        ]
    )
    stats = jnp.where(core == 0, stats, jnp.roll(stats, rows, axis=1))
    stats = merge(everywhere(stats, VOC, lax.axis_size(VOC)))
    stats = merge(everywhere(stats, TOK, lax.axis_size(TOK)))
    tm, tz, sm, s1, s2, cross, target = [stats[i] for i in range(7)]
    t_lse = tm + jnp.log(tz)
    s_one = sm + jnp.log(s1)
    s_tau = sm * 0.5 + jnp.log(s2)
    objective = 2.0 * (cross / tz - t_lse + s_tau) + 0.5 * (s_one - target)
    objective = objective.reshape(2, 4, 4, 4, 2, 2)
    objective = jnp.transpose(objective, (3, 2, 1, 0, 5, 4)).reshape(rows, 2)
    last = (lax.broadcasted_iota(jnp.int32, (rows, 2), 0) == rows - 1) & (
        lax.broadcasted_iota(jnp.int32, (rows, 2), 1) == 1
    )
    objective = jnp.where(last, 0.0, objective)

    norms = jnp.stack([t_lse, s_one, s_tau])
    norms = jnp.where(core == 0, norms, jnp.roll(norms, rows, axis=1))[:, :, None]
    grad = weight * (
        jnp.exp(scores * 0.5 - norms[2])
        - jnp.exp(teacher - norms[0])
        + 0.5 * (jnp.exp(scores - norms[1]) - match.astype(jnp.float32))
    )
    grad = grad.astype(jnp.bfloat16)

    contract = (((1,), (1,)), ((), ()))
    give = lax.dot_general(grad[rows:], student_head, contract, preferred_element_type=jnp.float32)
    taken = lax.ppermute(give, "c", pair)
    keep = lax.dot_general(grad[:rows], student_head, contract, preferred_element_type=jnp.float32)
    grad_head = lax.dot_general(
        hidden, grad, (((0,), (0,)), ((), ())), preferred_element_type=jnp.float32
    ).astype(jnp.bfloat16)
    share = (keep + taken).astype(jnp.bfloat16).reshape(chips, 4, width)
    share = lax.all_to_all(share, WALK, 0, 0, tiled=True)
    grad_hidden = jnp.sum(share.astype(jnp.float32), axis=0).astype(jnp.bfloat16)
    grad_hidden = jnp.swapaxes(grad_hidden.reshape(2, 2, width), 0, 1)
    return objective, grad_hidden, grad_head


def solution(mesh):
    fine = Mesh(mesh.devices.reshape(SIZES), CHIPS + ("c",))
    return jax.shard_map(
        local,
        mesh=fine,
        in_specs=(
            P(None, TOK),
            P(TOK, None, VOC),
            P(TOK + VOC, None, None),
            P(None, TOK + VOC),
            P(),
        ),
        out_specs=(P(), P(TOK + VOC, None, None), P(None, TOK + VOC)),
        check_vma=False,
    )
```

```python
import jax
import jax.numpy as jnp
from jax import lax
from jax.sharding import Mesh
from jax.sharding import PartitionSpec as P

TOK = ("x", "yh")
VOC = ("yl", "z", "c")
CHIPS = ("x", "yh", "yl", "z")
SIZES = (4, 2, 2, 4, 2)
WALK = ("z", "yh", "yl", "x")


def encode(partial):
    stripes, rows, width = partial.shape
    half = width // 2
    peak = jnp.maximum(jnp.max(jnp.abs(partial), axis=2), 1e-30)
    level = jnp.ceil(jnp.log2(peak) * 256.0)
    scale = jnp.exp2(-level / 256.0) * 32766.0
    code = jnp.clip(jnp.round(partial * scale[:, :, None]), -32767.0, 32767.0).astype(jnp.int32)
    words = (code[:, :, :half] << 16) | (code[:, :, half:] & 0xFFFF)
    tail = jnp.zeros((stripes, 8, half), jnp.int32).at[:, 0, :rows].set(level.astype(jnp.int32))
    return jnp.concatenate([words, tail], axis=1)


def decode(words, rows):
    level = words[:, rows, :rows].astype(jnp.float32)
    scale = (jnp.exp2(level / 256.0) * (0.5 / 32766.0))[:, :, None]
    body = words[:, :rows]
    high = (body >> 16).astype(jnp.float32)
    low = ((body << 16) >> 16).astype(jnp.float32)
    return jnp.concatenate([jnp.sum(high * scale, axis=0), jnp.sum(low * scale, axis=0)], axis=1)


def merge(parts):
    tp, tz, sp, s1, s2, cross, target = [parts[:, i] for i in range(7)]
    tm = jnp.max(tp, axis=0)
    sm = jnp.max(sp, axis=0)
    te = jnp.exp(tp - tm)
    se = jnp.exp((sp - sm) * 0.5)
    return jnp.stack(
        [
            tm,
            jnp.sum(tz * te, axis=0),
            sm,
            jnp.sum(s1 * (se * se), axis=0),
            jnp.sum(s2 * se, axis=0),
            jnp.sum(cross * te, axis=0),
            jnp.sum(target, axis=0),
        ]
    )


def ring_gather(block, axes):
    size = lax.axis_size(axes)
    here = lax.axis_index(axes)
    whole = jnp.zeros((size,) + block.shape, block.dtype)
    whole = lax.dynamic_update_index_in_dim(whole, block, here, 0)
    for step in range(1, size):
        taken = lax.ppermute(block, axes, [(i, (i + step) % size) for i in range(size)])
        whole = lax.dynamic_update_index_in_dim(whole, taken, (here + size - step) % size, 0)
    return whole.reshape((size * block.shape[0],) + block.shape[1:])


def everywhere(value, axes, count):
    copies = jnp.broadcast_to(value, (count,) + value.shape)
    return lax.all_to_all(copies, axes, 0, 0, tiled=True)


def local(teacher_hidden, teacher_head, student_hidden, student_head, target_ids):
    core = lax.axis_index("c")
    chips = lax.axis_size(CHIPS)
    stripes = teacher_head.shape[1]
    voc = teacher_head.shape[2]
    rows = teacher_hidden.shape[0]
    width = student_head.shape[0]
    base = lax.axis_index(TOK + VOC) * voc
    pair = [(0, 1), (1, 0)]

    partial = jnp.einsum("rd,dsv->srv", teacher_hidden, teacher_head, preferred_element_type=jnp.float32)
    words = lax.all_to_all(encode(partial), TOK, 0, 0, tiled=True)

    own = jnp.swapaxes(student_hidden, 0, 1).reshape(4, width)
    own = everywhere(own, ("yh", "yl", "x"), 16).reshape(64, width)
    own = ring_gather(own, "z")
    other = lax.ppermute(own, "c", pair)
    hidden = jnp.concatenate([own, other], axis=0)
    scores = jnp.dot(hidden, student_head, preferred_element_type=jnp.float32)

    place = lax.broadcasted_iota(jnp.int32, (2 * rows, 1), 0)
    side = place // rows
    place = place % rows
    head, inner = (place // 2) % 2, place % 2
    chip = (place // 4) % 4 * 16 + (place // 16) % 4 * 4 + place // 64
    row = chip * 4 + jnp.where(side == 0, core, 1 - core) * 2 + inner
    weight = jnp.where((head == 1) & (row == rows - 1), 0.0, 1.0).astype(jnp.float32)
    teacher_row = jnp.minimum(row + head, rows - 1)
    order = target_ids.reshape(4, 4, 4, 2, 2, 2)
    order = jnp.transpose(order, (3, 2, 1, 0, 5, 4)).reshape(2, rows)
    ids = jnp.where(core == 0, order, order[::-1]).reshape(2 * rows, 1)
    match = lax.broadcasted_iota(jnp.int32, (1, voc), 1) + base == ids

    pick = (lax.broadcasted_iota(jnp.int32, (1, rows), 1) == teacher_row).astype(jnp.float32)
    teacher = jnp.dot(pick, decode(words, rows), precision=lax.Precision.HIGHEST)

    t_peak = jnp.max(teacher, axis=1, keepdims=True)
    t_exp = jnp.exp(teacher - t_peak)
    s_peak = jnp.max(scores, axis=1, keepdims=True)
    s_exp = jnp.exp((scores - s_peak) * 0.5)
    stats = jnp.stack(
        [
            t_peak[:, 0],
            jnp.sum(t_exp, axis=1),
            s_peak[:, 0],
            jnp.sum(s_exp * s_exp, axis=1),
            jnp.sum(s_exp, axis=1),
            jnp.sum(t_exp * (teacher - scores * 0.5), axis=1),
            jnp.sum(jnp.where(match, scores, 0.0), axis=1),
        ]
    )
    stats = jnp.where(core == 0, stats, jnp.roll(stats, rows, axis=1))
    stats = merge(everywhere(stats, VOC, lax.axis_size(VOC)))
    stats = merge(everywhere(stats, TOK, lax.axis_size(TOK)))
    tm, tz, sm, s1, s2, cross, target = [stats[i] for i in range(7)]
    t_lse = tm + jnp.log(tz)
    s_one = sm + jnp.log(s1)
    s_tau = sm * 0.5 + jnp.log(s2)
    objective = 2.0 * (cross / tz - t_lse + s_tau) + 0.5 * (s_one - target)
    objective = objective.reshape(2, 4, 4, 4, 2, 2)
    objective = jnp.transpose(objective, (3, 2, 1, 0, 5, 4)).reshape(rows, 2)
    last = (lax.broadcasted_iota(jnp.int32, (rows, 2), 0) == rows - 1) & (
        lax.broadcasted_iota(jnp.int32, (rows, 2), 1) == 1
    )
    objective = jnp.where(last, 0.0, objective)

    norms = jnp.stack([t_lse, s_one, s_tau])
    norms = jnp.where(core == 0, norms, jnp.roll(norms, rows, axis=1))[:, :, None]
    grad = weight * (
        jnp.exp(scores * 0.5 - norms[2])
        - jnp.exp(teacher - norms[0])
        + 0.5 * (jnp.exp(scores - norms[1]) - match.astype(jnp.float32))
    )
    grad = grad.astype(jnp.bfloat16)

    contract = (((1,), (1,)), ((), ()))
    give = lax.dot_general(grad[rows:], student_head, contract, preferred_element_type=jnp.float32)
    taken = lax.ppermute(give, "c", pair)
    keep = lax.dot_general(grad[:rows], student_head, contract, preferred_element_type=jnp.float32)
    grad_head = lax.dot_general(
        hidden, grad, (((0,), (0,)), ((), ())), preferred_element_type=jnp.float32
    ).astype(jnp.bfloat16)
    share = (keep + taken).astype(jnp.bfloat16).reshape(chips, 4, width)
    share = lax.all_to_all(share, WALK, 0, 0, tiled=True)
    grad_hidden = jnp.sum(share.astype(jnp.float32), axis=0).astype(jnp.bfloat16)
    grad_hidden = jnp.swapaxes(grad_hidden.reshape(2, 2, width), 0, 1)
    return objective, grad_hidden, grad_head


def solution(mesh):
    fine = Mesh(mesh.devices.reshape(SIZES), CHIPS + ("c",))
    return jax.shard_map(
        local,
        mesh=fine,
        in_specs=(
            P(None, TOK),
            P(TOK, None, VOC),
            P(TOK + VOC, None, None),
            P(None, TOK + VOC),
            P(),
        ),
        out_specs=(P(), P(TOK + VOC, None, None), P(None, TOK + VOC)),
        check_vma=False,
    )
```

```python
import jax
import jax.numpy as jnp
from jax import lax
from jax.sharding import Mesh
from jax.sharding import PartitionSpec as P

TOK = ("xh", "xl", "yh")
VOC = ("yl", "z", "c")
SIZES = (2, 2, 2, 2, 4, 2)
STRIPES = ("yh", "xl", "xh")
WALK = ("z", "yh", "yl", "xh", "xl")


def encode(partial):
    stripes, rows, width = partial.shape
    half = width // 2
    peak = jnp.maximum(jnp.max(jnp.abs(partial), axis=2), 1e-30)
    level = jnp.ceil(jnp.log2(peak) * 256.0)
    scale = jnp.exp2(-level / 256.0) * 32766.0
    code = jnp.clip(jnp.round(partial * scale[:, :, None]), -32767.0, 32767.0).astype(jnp.int32)
    words = (code[:, :, :half] << 16) | (code[:, :, half:] & 0xFFFF)
    tail = jnp.zeros((stripes, 8, half), jnp.int32).at[:, 0, :rows].set(level.astype(jnp.int32))
    return jnp.concatenate([words, tail], axis=1)


def decode(words, rows):
    level = words[:, rows, :rows].astype(jnp.float32)
    scale = (jnp.exp2(level / 256.0) * (0.5 / 32766.0))[:, :, None]
    body = words[:, :rows]
    high = (body >> 16).astype(jnp.float32)
    low = ((body << 16) >> 16).astype(jnp.float32)
    return jnp.concatenate([jnp.sum(high * scale, axis=0), jnp.sum(low * scale, axis=0)], axis=1)


def merge(parts):
    tp, tz, sp, s1, s2, cross, target = [parts[:, i] for i in range(7)]
    tm = jnp.max(tp, axis=0)
    sm = jnp.max(sp, axis=0)
    te = jnp.exp(tp - tm)
    se = jnp.exp((sp - sm) * 0.5)
    return jnp.stack(
        [
            tm,
            jnp.sum(tz * te, axis=0),
            sm,
            jnp.sum(s1 * (se * se), axis=0),
            jnp.sum(s2 * se, axis=0),
            jnp.sum(cross * te, axis=0),
            jnp.sum(target, axis=0),
        ]
    )


def ring_gather(block, axes):
    size = lax.axis_size(axes)
    here = lax.axis_index(axes)
    whole = jnp.zeros((size,) + block.shape, block.dtype)
    whole = lax.dynamic_update_index_in_dim(whole, block, here, 0)
    for step in range(1, size):
        taken = lax.ppermute(block, axes, [(i, (i + step) % size) for i in range(size)])
        whole = lax.dynamic_update_index_in_dim(whole, taken, (here + size - step) % size, 0)
    return whole.reshape((size * block.shape[0],) + block.shape[1:])


def everywhere(value, axes, count):
    copies = jnp.broadcast_to(value, (count,) + value.shape)
    return lax.all_to_all(copies, axes, 0, 0, tiled=True)


def local(teacher_hidden, teacher_head, student_hidden, student_head, target_ids):
    core = lax.axis_index("c")
    chips = lax.axis_size(WALK)
    stripes = teacher_head.shape[1]
    voc = teacher_head.shape[2]
    rows = teacher_hidden.shape[0]
    width = student_head.shape[0]
    base = lax.axis_index(TOK + VOC) * voc
    pair = [(0, 1), (1, 0)]

    partial = jnp.einsum("rd,dsv->srv", teacher_hidden, teacher_head, preferred_element_type=jnp.float32)
    words = encode(partial)
    words = words.reshape((2, 2, 2) + words.shape[1:]).transpose(2, 1, 0, 3, 4).reshape(words.shape)
    words = lax.all_to_all(words, STRIPES, 0, 0, tiled=True)

    own = jnp.swapaxes(student_hidden, 0, 1).reshape(4, width)
    own = everywhere(own, ("yh", "yl", "xh", "xl"), 16).reshape(64, width)
    own = ring_gather(own, "z")
    other = lax.ppermute(own, "c", pair)
    hidden = jnp.concatenate([own, other], axis=0)
    scores = jnp.dot(hidden, student_head, preferred_element_type=jnp.float32)

    place = lax.broadcasted_iota(jnp.int32, (2 * rows, 1), 0)
    side = place // rows
    place = place % rows
    head, inner = (place // 2) % 2, place % 2
    chip = (place // 4) % 4 * 16 + (place // 16) % 4 * 4 + place // 64
    row = chip * 4 + jnp.where(side == 0, core, 1 - core) * 2 + inner
    weight = jnp.where((head == 1) & (row == rows - 1), 0.0, 1.0).astype(jnp.float32)
    teacher_row = jnp.minimum(row + head, rows - 1)
    order = target_ids.reshape(4, 4, 4, 2, 2, 2)
    order = jnp.transpose(order, (3, 2, 1, 0, 5, 4)).reshape(2, rows)
    ids = jnp.where(core == 0, order, order[::-1]).reshape(2 * rows, 1)
    match = lax.broadcasted_iota(jnp.int32, (1, voc), 1) + base == ids

    pick = (lax.broadcasted_iota(jnp.int32, (1, rows), 1) == teacher_row).astype(jnp.float32)
    teacher = jnp.dot(pick, decode(words, rows), precision=lax.Precision.HIGHEST)

    t_peak = jnp.max(teacher, axis=1, keepdims=True)
    t_exp = jnp.exp(teacher - t_peak)
    s_peak = jnp.max(scores, axis=1, keepdims=True)
    s_exp = jnp.exp((scores - s_peak) * 0.5)
    stats = jnp.stack(
        [
            t_peak[:, 0],
            jnp.sum(t_exp, axis=1),
            s_peak[:, 0],
            jnp.sum(s_exp * s_exp, axis=1),
            jnp.sum(s_exp, axis=1),
            jnp.sum(t_exp * (teacher - scores * 0.5), axis=1),
            jnp.sum(jnp.where(match, scores, 0.0), axis=1),
        ]
    )
    stats = jnp.where(core == 0, stats, jnp.roll(stats, rows, axis=1))
    stats = merge(everywhere(stats, VOC, lax.axis_size(VOC)))
    stats = merge(everywhere(stats, TOK, lax.axis_size(TOK)))
    tm, tz, sm, s1, s2, cross, target = [stats[i] for i in range(7)]
    t_lse = tm + jnp.log(tz)
    s_one = sm + jnp.log(s1)
    s_tau = sm * 0.5 + jnp.log(s2)
    objective = 2.0 * (cross / tz - t_lse + s_tau) + 0.5 * (s_one - target)
    objective = objective.reshape(2, 4, 4, 4, 2, 2)
    objective = jnp.transpose(objective, (3, 2, 1, 0, 5, 4)).reshape(rows, 2)
    last = (lax.broadcasted_iota(jnp.int32, (rows, 2), 0) == rows - 1) & (
        lax.broadcasted_iota(jnp.int32, (rows, 2), 1) == 1
    )
    objective = jnp.where(last, 0.0, objective)

    norms = jnp.stack([t_lse, s_one, s_tau])
    norms = jnp.where(core == 0, norms, jnp.roll(norms, rows, axis=1))[:, :, None]
    grad = weight * (
        jnp.exp(scores * 0.5 - norms[2])
        - jnp.exp(teacher - norms[0])
        + 0.5 * (jnp.exp(scores - norms[1]) - match.astype(jnp.float32))
    )
    grad = grad.astype(jnp.bfloat16)

    contract = (((1,), (1,)), ((), ()))
    give = lax.dot_general(grad[rows:], student_head, contract, preferred_element_type=jnp.float32)
    taken = lax.ppermute(give, "c", pair)
    keep = lax.dot_general(grad[:rows], student_head, contract, preferred_element_type=jnp.float32)
    grad_head = lax.dot_general(
        hidden, grad, (((0,), (0,)), ((), ())), preferred_element_type=jnp.float32
    ).astype(jnp.bfloat16)
    share = (keep + taken).astype(jnp.bfloat16).reshape(chips, 4, width)
    share, grad_head = lax.optimization_barrier((share, grad_head))
    share = lax.all_to_all(share, WALK, 0, 0, tiled=True)
    grad_hidden = jnp.sum(share.astype(jnp.float32), axis=0).astype(jnp.bfloat16)
    grad_hidden = jnp.swapaxes(grad_hidden.reshape(2, 2, width), 0, 1)
    return objective, grad_hidden, grad_head


def solution(mesh):
    fine = Mesh(mesh.devices.reshape(SIZES), TOK + VOC)
    return jax.shard_map(
        local,
        mesh=fine,
        in_specs=(
            P(None, TOK),
            P(TOK, None, VOC),
            P(TOK + VOC, None, None),
            P(None, TOK + VOC),
            P(),
        ),
        out_specs=(P(), P(TOK + VOC, None, None), P(None, TOK + VOC)),
        check_vma=False,
    )
```

```python
import jax
import jax.numpy as jnp
from jax import lax
from jax.sharding import Mesh
from jax.sharding import PartitionSpec as P

TOK = ("xh", "xl", "yh")
VOC = ("yl", "z", "c")
SIZES = (2, 2, 2, 2, 4, 2)
STEPS = ((2, 1), (1, 1), (3, 1), (2, 0), (0, 1), (1, 0), (3, 0))
WALK = ("z", "yh", "yl", "xh", "xl")


def encode(partial, level):
    rows, width = partial.shape
    half = width // 2
    scale = jnp.exp2(level * (-1.0 / 256.0)) * 32766.0
    code = jnp.clip(jnp.round(partial * scale[:, None]), -32767.0, 32767.0).astype(jnp.int32)
    words = (code[:, :half] << 16) | (code[:, half:] & 0xFFFF)
    tail = jnp.pad(level.astype(jnp.int32)[None], ((0, 7), (0, half - rows)))
    return jnp.concatenate([words, tail], axis=0)


def decode(words, rows):
    level = words[rows, :rows].astype(jnp.float32)
    scale = (jnp.exp2(level * (1.0 / 256.0)) * (0.5 / 32766.0))[:, None]
    body = words[:rows]
    high = (body >> 16).astype(jnp.float32)
    low = ((body << 16) >> 16).astype(jnp.float32)
    return high * scale, low * scale


def merge(parts):
    tp, tz, sp, s1, s2, cross, target = [parts[:, i] for i in range(7)]
    tm = jnp.max(tp, axis=0)
    sm = jnp.max(sp, axis=0)
    te = jnp.exp(tp - tm)
    se = jnp.exp((sp - sm) * 0.5)
    return jnp.stack(
        [
            tm,
            jnp.sum(tz * te, axis=0),
            sm,
            jnp.sum(s1 * (se * se), axis=0),
            jnp.sum(s2 * se, axis=0),
            jnp.sum(cross * te, axis=0),
            jnp.sum(target, axis=0),
        ]
    )


def ring_gather(block, axes):
    size = lax.axis_size(axes)
    here = lax.axis_index(axes)
    whole = jnp.zeros((size,) + block.shape, block.dtype)
    whole = lax.dynamic_update_index_in_dim(whole, block, here, 0)
    for step in range(1, size):
        taken = lax.ppermute(block, axes, [(i, (i + step) % size) for i in range(size)])
        whole = lax.dynamic_update_index_in_dim(whole, taken, (here + size - step) % size, 0)
    return whole.reshape((size * block.shape[0],) + block.shape[1:])


def everywhere(value, axes, count):
    copies = jnp.broadcast_to(value, (count,) + value.shape)
    return lax.all_to_all(copies, axes, 0, 0, tiled=True)


def local(teacher_hidden, teacher_head, student_hidden, student_head, target_ids):
    core = lax.axis_index("c")
    chips = lax.axis_size(WALK)
    stripes = teacher_head.shape[1]
    voc = teacher_head.shape[2]
    rows = teacher_hidden.shape[0]
    width = student_head.shape[0]
    base = lax.axis_index(TOK + VOC) * voc
    pair = [(0, 1), (1, 0)]

    partial = jnp.einsum("rd,dsv->srv", teacher_hidden, teacher_head, preferred_element_type=jnp.float32)
    peak = jnp.maximum(jnp.max(jnp.abs(partial), axis=2), 1e-30)
    level = jnp.ceil(jnp.log2(peak) * 256.0)
    tok = lax.axis_index(TOK)

    def move(index, step):
        return (index // 2 + step[0]) % 4 * 2 + (index % 2 + step[1]) % 2

    arrived = []
    for step in STEPS:
        to = move(tok, step)
        words = encode(
            lax.dynamic_index_in_dim(partial, to, 0, False), lax.dynamic_index_in_dim(level, to, 0, False)
        )
        arrived.append(lax.ppermute(words, TOK, [(i, move(i, step)) for i in range(stripes)]))

    own = jnp.swapaxes(student_hidden, 0, 1).reshape(4, width)
    own = everywhere(own, ("yh", "yl", "xh", "xl"), 16).reshape(64, width)
    own = ring_gather(own, "z")
    other = lax.ppermute(own, "c", pair)
    hidden = jnp.concatenate([own, other], axis=0)
    scores = jnp.dot(hidden, student_head, preferred_element_type=jnp.float32)

    place = lax.broadcasted_iota(jnp.int32, (2 * rows, 1), 0)
    side = place // rows
    place = place % rows
    head, inner = (place // 2) % 2, place % 2
    chip = (place // 4) % 4 * 16 + (place // 16) % 4 * 4 + place // 64
    row = chip * 4 + jnp.where(side == 0, core, 1 - core) * 2 + inner
    weight = jnp.where((head == 1) & (row == rows - 1), 0.0, 1.0).astype(jnp.float32)
    teacher_row = jnp.minimum(row + head, rows - 1)
    order = target_ids.reshape(4, 4, 4, 2, 2, 2)
    order = jnp.transpose(order, (3, 2, 1, 0, 5, 4)).reshape(2, rows)
    ids = jnp.where(core == 0, order, order[::-1]).reshape(2 * rows, 1)
    match = lax.broadcasted_iota(jnp.int32, (1, voc), 1) + base == ids

    pick = (lax.broadcasted_iota(jnp.int32, (1, rows), 1) == teacher_row).astype(jnp.float32)
    parts = [decode(words, rows) for words in arrived]
    whole = jnp.concatenate([sum(p[0] for p in parts), sum(p[1] for p in parts)], axis=1)
    whole = whole + 0.5 * lax.dynamic_index_in_dim(partial, tok, 0, False)
    teacher = jnp.dot(pick, whole, precision=lax.Precision.HIGHEST)

    t_peak = jnp.max(teacher, axis=1, keepdims=True)
    t_exp = jnp.exp(teacher - t_peak)
    s_peak = jnp.max(scores, axis=1, keepdims=True)
    s_exp = jnp.exp((scores - s_peak) * 0.5)
    stats = jnp.stack(
        [
            t_peak[:, 0],
            jnp.sum(t_exp, axis=1),
            s_peak[:, 0],
            jnp.sum(s_exp * s_exp, axis=1),
            jnp.sum(s_exp, axis=1),
            jnp.sum(t_exp * (teacher - scores * 0.5), axis=1),
            jnp.sum(jnp.where(match, scores, 0.0), axis=1),
        ]
    )
    stats = jnp.where(core == 0, stats, jnp.roll(stats, rows, axis=1))
    stats = merge(everywhere(stats, VOC, lax.axis_size(VOC)))
    stats = merge(everywhere(stats, TOK, lax.axis_size(TOK)))
    tm, tz, sm, s1, s2, cross, target = [stats[i] for i in range(7)]
    t_lse = tm + jnp.log(tz)
    s_one = sm + jnp.log(s1)
    s_tau = sm * 0.5 + jnp.log(s2)
    objective = 2.0 * (cross / tz - t_lse + s_tau) + 0.5 * (s_one - target)
    objective = objective.reshape(2, 4, 4, 4, 2, 2)
    objective = jnp.transpose(objective, (3, 2, 1, 0, 5, 4)).reshape(rows, 2)
    last = (lax.broadcasted_iota(jnp.int32, (rows, 2), 0) == rows - 1) & (
        lax.broadcasted_iota(jnp.int32, (rows, 2), 1) == 1
    )
    objective = jnp.where(last, 0.0, objective)

    norms = jnp.stack([t_lse, s_one, s_tau])
    norms = jnp.where(core == 0, norms, jnp.roll(norms, rows, axis=1))[:, :, None]
    grad = weight * (
        jnp.exp(scores * 0.5 - norms[2])
        - jnp.exp(teacher - norms[0])
        + 0.5 * (jnp.exp(scores - norms[1]) - match.astype(jnp.float32))
    )
    grad = grad.astype(jnp.bfloat16)

    contract = (((1,), (1,)), ((), ()))
    give = lax.dot_general(grad[rows:], student_head, contract, preferred_element_type=jnp.float32)
    taken = lax.ppermute(give, "c", pair)
    keep = lax.dot_general(grad[:rows], student_head, contract, preferred_element_type=jnp.float32)
    grad_head = lax.dot_general(
        hidden, grad, (((0,), (0,)), ((), ())), preferred_element_type=jnp.float32
    ).astype(jnp.bfloat16)
    share = (keep + taken).astype(jnp.bfloat16).reshape(chips, 4, width)
    share, grad_head, objective = lax.optimization_barrier((share, grad_head, objective))
    share = lax.all_to_all(share, WALK, 0, 0, tiled=True)
    grad_hidden = jnp.sum(share.astype(jnp.float32), axis=0).astype(jnp.bfloat16)
    grad_hidden = jnp.swapaxes(grad_hidden.reshape(2, 2, width), 0, 1)
    return objective, grad_hidden, grad_head


def solution(mesh):
    fine = Mesh(mesh.devices.reshape(SIZES), TOK + VOC)
    return jax.shard_map(
        local,
        mesh=fine,
        in_specs=(
            P(None, TOK),
            P(TOK, None, VOC),
            P(TOK + VOC, None, None),
            P(None, TOK + VOC),
            P(),
        ),
        out_specs=(P(), P(TOK + VOC, None, None), P(None, TOK + VOC)),
        check_vma=False,
    )
```

```python
import jax
import jax.numpy as jnp
from jax import lax
from jax.experimental import pallas as pl
from jax.experimental.pallas import tpu as pltpu
from jax.sharding import Mesh
from jax.sharding import PartitionSpec as P

TOK = ("xh", "xl", "yh")
VOC = ("yl", "z", "c")
SIZES = (2, 2, 2, 2, 4, 2)
STEPS = ((2, 1), (1, 1), (3, 1), (2, 0), (0, 1), (1, 0), (3, 0))
WALK = ("z", "yh", "yl", "xh", "xl")
EXCHANGE = ("z", "yh", "xh", "yl", "xl", "c")


def encode(partial, level):
    rows, width = partial.shape
    half = width // 2
    scale = jnp.exp2(level * (-1.0 / 256.0)) * 32766.0
    code = jnp.clip(jnp.round(partial * scale[:, None]), -32767.0, 32767.0).astype(jnp.int32)
    words = (code[:, :half] << 16) | (code[:, half:] & 0xFFFF)
    tail = jnp.pad(level.astype(jnp.int32)[None], ((0, 7), (0, half - rows)))
    return jnp.concatenate([words, tail], axis=0)


def row_of(place, core):
    head = (place >> 1) & 1
    row = ((place >> 2) & 3) * 64 + ((place >> 4) & 3) * 16 + (place >> 6) * 4 + core * 2 + (place & 1)
    return row, head


def teacher_kernel(core_ref, *refs):
    words, (own_ref, mine_ref, theirs_ref, mine_out, theirs_out, stats_out, sum_ref) = refs[:7], refs[7:]
    rows, width = sum_ref.shape
    half = width // 2
    step = 32
    level = jnp.concatenate([w[rows : rows + 1, :rows] for w in words] + [words[0][rows : rows + 1, :rows]], axis=0)
    scale = jnp.transpose(jnp.exp2(level.astype(jnp.float32) * (1.0 / 256.0)) * (0.5 / 32766.0))
    peaks, totals = [], []
    for at in range(0, rows, step):
        here = pl.ds(at, step)
        low = 0.5 * own_ref[0, here, half:]
        high = 0.5 * own_ref[0, here, :half]
        for j, w in enumerate(words):
            body = w[here, :]
            by = scale[at : at + step, j : j + 1]
            high = high + (body >> 16).astype(jnp.float32) * by
            low = low + ((body << 16) >> 16).astype(jnp.float32) * by
        sum_ref[here, :half] = high
        sum_ref[here, half:] = low
        peak = jnp.maximum(jnp.max(high, axis=1, keepdims=True), jnp.max(low, axis=1, keepdims=True))
        total = jnp.sum(jnp.exp(high - peak), axis=1, keepdims=True)
        total = total + jnp.sum(jnp.exp(low - peak), axis=1, keepdims=True)
        peaks.append(peak)
        totals.append(total)
    peak = jnp.concatenate(peaks, axis=0)
    total = jnp.concatenate(totals, axis=0)
    lane = lax.broadcasted_iota(jnp.int32, (rows, rows), 1)
    place = lax.broadcasted_iota(jnp.int32, (rows, rows), 0)
    eye = lane == place
    first = sum_ref[...].astype(jnp.bfloat16)
    rest = sum_ref[...] - first.astype(jnp.float32)
    second = rest.astype(jnp.bfloat16)
    third = (rest - second.astype(jnp.float32)).astype(jnp.bfloat16)
    crosses = [jnp.zeros((1, rows), jnp.float32), jnp.zeros((1, rows), jnp.float32)]
    for side, scores, out in ((0, mine_ref, mine_out), (1, theirs_ref, theirs_out)):
        core = jnp.where(side == 0, core_ref[0], 1 - core_ref[0])
        row, head = row_of(place, core)
        chosen = lane == jnp.minimum(row + head, rows - 1)
        pick = jnp.where(chosen, 1.0, 0.0).astype(jnp.bfloat16)
        moved = jnp.dot(pick, first, preferred_element_type=jnp.float32)
        moved = moved + jnp.dot(pick, second, preferred_element_type=jnp.float32)
        out[...] = moved + jnp.dot(pick, third, preferred_element_type=jnp.float32)
        parts = []
        for at in range(0, rows, step):
            here = pl.ds(at, step)
            logits = out[here, :]
            weight = jnp.exp(logits - jnp.max(logits, axis=1, keepdims=True))
            parts.append(jnp.sum(weight * (logits - 0.5 * scores[here, :]), axis=1, keepdims=True))
        cross = jnp.concatenate(parts, axis=0)
        for k in (0, 1):
            inside = chosen & (head == k) & (row + k < rows)
            crosses[k] = crosses[k] + jnp.sum(jnp.where(inside, cross, 0.0), axis=0, keepdims=True)
    stats_out[0:1, :] = jnp.sum(jnp.where(eye, peak, 0.0), axis=0, keepdims=True)
    stats_out[1:2, :] = jnp.sum(jnp.where(eye, total, 0.0), axis=0, keepdims=True)
    stats_out[2:3, :] = crosses[0]
    stats_out[3:4, :] = crosses[1]
    stats_out[4:8, :] = jnp.zeros((4, rows), jnp.float32)


def teacher_sum(core, tok, words, partial, mine, theirs):
    rows, width = mine.shape
    whole = lambda a: pl.BlockSpec(a.shape, lambda i, c, t: (0,) * a.ndim)
    shape = jax.ShapeDtypeStruct
    flops = 12 * rows * rows * width
    return pl.pallas_call(
        lambda core_ref, tok_ref, *refs: teacher_kernel(core_ref, *refs),
        out_shape=(
            shape((rows, width), jnp.float32),
            shape((rows, width), jnp.float32),
            shape((8, rows), jnp.float32),
        ),
        grid_spec=pltpu.PrefetchScalarGridSpec(
            num_scalar_prefetch=2,
            grid=(1,),
            in_specs=[whole(w) for w in words]
            + [pl.BlockSpec((1, rows, width), lambda i, c, t: (t[0], 0, 0)), whole(mine), whole(theirs)],
            out_specs=(whole(mine), whole(mine), pl.BlockSpec((8, rows), lambda i, c, t: (0, 0))),
            scratch_shapes=[pltpu.VMEM((rows, width), jnp.float32)],
        ),
        compiler_params=pltpu.CompilerParams(vmem_limit_bytes=40 * 1024 * 1024),
        cost_estimate=pl.CostEstimate(flops=flops, bytes_accessed=10 * rows * width * 4, transcendentals=3 * rows * width),
    )(core, tok, *words, partial, mine, theirs)


def merge(parts):
    peak = jnp.max(parts[:, 0], axis=0)
    scale = jnp.exp((parts[:, 0] - peak) * 0.5)
    return jnp.stack(
        [
            peak,
            jnp.sum(parts[:, 1] * (scale * scale), axis=0),
            jnp.sum(parts[:, 2] * scale, axis=0),
            jnp.sum(parts[:, 3], axis=0),
        ]
    )


def ring_gather(block, axes):
    size = lax.axis_size(axes)
    here = lax.axis_index(axes)
    whole = jnp.zeros((size,) + block.shape, block.dtype)
    whole = lax.dynamic_update_index_in_dim(whole, block, here, 0)
    for step in range(1, size):
        taken = lax.ppermute(block, axes, [(i, (i + step) % size) for i in range(size)])
        whole = lax.dynamic_update_index_in_dim(whole, taken, (here + size - step) % size, 0)
    return whole.reshape((size * block.shape[0],) + block.shape[1:])


def everywhere(value, axes, count):
    copies = jnp.broadcast_to(value, (count,) + value.shape)
    return lax.all_to_all(copies, axes, 0, 0, tiled=True)


def local(teacher_hidden, teacher_head, student_hidden, student_head, target_ids):
    core = lax.axis_index("c")
    chips = lax.axis_size(WALK)
    devices = lax.axis_size(EXCHANGE)
    stripes = teacher_head.shape[1]
    voc = teacher_head.shape[2]
    rows = teacher_hidden.shape[0]
    width = student_head.shape[0]
    base = lax.axis_index(TOK + VOC) * voc
    tok = lax.axis_index(TOK)
    pair = [(0, 1), (1, 0)]

    plane = jnp.swapaxes(student_hidden, 0, 1).reshape(4, width)
    plane = everywhere(plane, ("yh", "yl", "xh", "xl"), 16).reshape(64, width)

    partial = jnp.einsum("rd,dsv->srv", teacher_hidden, teacher_head, preferred_element_type=jnp.float32)
    peak = jnp.maximum(jnp.max(jnp.abs(partial), axis=2), 1e-30)
    level = jnp.ceil(jnp.log2(peak) * 256.0)
    level, plane = lax.optimization_barrier((level, plane))

    def move(index, step):
        return (index // 2 + step[0]) % 4 * 2 + (index % 2 + step[1]) % 2

    arrived = []
    for step in STEPS:
        to = move(tok, step)
        words = encode(
            lax.dynamic_index_in_dim(partial, to, 0, False), lax.dynamic_index_in_dim(level, to, 0, False)
        )
        if len(arrived) == 1:
            words, plane = lax.optimization_barrier((words, plane))
        arrived.append(lax.ppermute(words, TOK, [(i, move(i, step)) for i in range(stripes)]))

    own = ring_gather(plane, "z")
    other = lax.ppermute(own, "c", pair)

    order = target_ids.reshape(4, 4, 4, 2, 2, 2)
    order = jnp.transpose(order, (3, 2, 1, 0, 5, 4)).reshape(2, rows, 1)
    place = lax.broadcasted_iota(jnp.int32, (rows, 1), 0)
    columns = lax.broadcasted_iota(jnp.int32, (1, voc), 1) + base

    def student(hidden, side):
        scores = jnp.dot(hidden, student_head, preferred_element_type=jnp.float32)
        match = columns == jnp.where(side == 0, order[0], order[1])
        top = jnp.max(scores, axis=1, keepdims=True)
        powers = jnp.exp((scores - top) * 0.5)
        stats = jnp.stack(
            [
                top[:, 0],
                jnp.sum(powers * powers, axis=1),
                jnp.sum(powers, axis=1),
                jnp.sum(jnp.where(match, scores, 0.0), axis=1),
            ]
        )
        return scores, match, stats

    own_scores, own_match, own_stats = student(own, core)
    other_scores, other_match, other_stats = student(other, 1 - core)
    stats = jnp.stack(
        [jnp.where(core == 0, own_stats, other_stats), jnp.where(core == 0, other_stats, own_stats)], axis=1
    ).reshape(4, 2 * rows)
    around = [stats] + [lax.ppermute(stats, "z", [(i, (i + j) % 4) for i in range(4)]) for j in (1, 2, 3)]
    stats = merge(jnp.stack(around)).reshape(4, 4, rows // 2)
    stats = lax.dynamic_index_in_dim(stats, lax.axis_index("z"), 1, False)

    own_teacher, other_teacher, teacher_stats = teacher_sum(
        core[None], tok[None], arrived, partial, own_scores, other_scores
    )

    shares = jnp.concatenate([teacher_stats[:4].reshape(1, -1), stats.reshape(1, -1)], axis=1)
    shares = everywhere(shares, EXCHANGE, devices)
    cut = 4 * rows
    t_parts = shares[:, 0, :cut].reshape(devices, 4, rows)
    s_parts = shares[:, 0, cut:].reshape(4, devices // 4, 4, rows // 2)
    t_peak = jnp.max(t_parts[:, 0], axis=0)
    t_scale = jnp.exp(t_parts[:, 0] - t_peak)
    t_total = jnp.sum(t_parts[:, 1] * t_scale, axis=0)
    t_lse = t_peak + jnp.log(t_total)
    cross = jnp.sum(t_parts[:, 2:] * t_scale[:, None], axis=0) / t_total
    sm, s1, s2, target = [a.reshape(2, rows) for a in jax.vmap(merge, out_axes=1)(s_parts)]
    s_one = sm + jnp.log(s1)
    s_tau = sm * 0.5 + jnp.log(s2)

    own_first = lambda a: jnp.where(core == 0, a, a[::-1])
    s_one_here, s_tau_here = own_first(s_one), own_first(s_tau)

    def slope(side, scores, teacher, match, one, tau):
        row, head = row_of(place, side)
        picked = lax.broadcasted_iota(jnp.int32, (1, rows), 1) == jnp.minimum(row + head, rows - 1)
        lse = jnp.sum(jnp.where(picked, t_lse[None], 0.0), axis=1, keepdims=True)
        weight = jnp.where((head == 1) & (row == rows - 1), 0.0, 1.0).astype(jnp.float32)
        grad = weight * (
            jnp.exp(scores * 0.5 - tau[:, None])
            - jnp.exp(teacher - lse)
            + 0.5 * (jnp.exp(scores - one[:, None]) - match.astype(jnp.float32))
        )
        return grad.astype(jnp.bfloat16)

    contract = (((1,), (1,)), ((), ()))
    other_grad = slope(1 - core, other_scores, other_teacher, other_match, s_one_here[1], s_tau_here[1])
    give = lax.dot_general(other_grad, student_head, contract, preferred_element_type=jnp.float32)
    taken = lax.ppermute(give, "c", pair)
    own_grad = slope(core, own_scores, own_teacher, own_match, s_one_here[0], s_tau_here[0])
    keep = lax.dot_general(own_grad, student_head, contract, preferred_element_type=jnp.float32)
    hidden = jnp.concatenate([own, other], axis=0)
    grad = jnp.concatenate([own_grad, other_grad], axis=0)
    grad_head = lax.dot_general(
        hidden, grad, (((0,), (0,)), ((), ())), preferred_element_type=jnp.float32
    ).astype(jnp.bfloat16)

    def natural(a):
        return jnp.transpose(a.reshape(2, 4, 4, 4, 2, 2), (3, 2, 1, 0, 5, 4)).reshape(rows, 2)

    after = lambda a: jnp.concatenate([a[1:], a[-1:]])
    both = lambda a, b: jnp.stack([a, after(b)], axis=1)
    objective = 2.0 * (both(cross[0], cross[1]) - both(t_lse, t_lse) + natural(s_tau)) + 0.5 * natural(s_one - target)
    last = (lax.broadcasted_iota(jnp.int32, (rows, 2), 0) == rows - 1) & (
        lax.broadcasted_iota(jnp.int32, (rows, 2), 1) == 1
    )
    objective = jnp.where(last, 0.0, objective)

    share = (keep + taken).astype(jnp.bfloat16).reshape(chips, 4, width)
    share, grad_head, objective = lax.optimization_barrier((share, grad_head, objective))
    share = lax.all_to_all(share, WALK, 0, 0, tiled=True)
    grad_hidden = jnp.sum(share.astype(jnp.float32), axis=0).astype(jnp.bfloat16)
    grad_hidden = jnp.swapaxes(grad_hidden.reshape(2, 2, width), 0, 1)
    return objective, grad_hidden, grad_head


def solution(mesh):
    fine = Mesh(mesh.devices.reshape(SIZES), TOK + VOC)
    return jax.shard_map(
        local,
        mesh=fine,
        in_specs=(
            P(None, TOK),
            P(TOK, None, VOC),
            P(TOK + VOC, None, None),
            P(None, TOK + VOC),
            P(),
        ),
        out_specs=(P(), P(TOK + VOC, None, None), P(None, TOK + VOC)),
        check_vma=False,
    )
```

```python
import jax
import jax.numpy as jnp
from jax import lax
from jax.experimental import pallas as pl
from jax.experimental.pallas import tpu as pltpu
from jax.sharding import Mesh
from jax.sharding import PartitionSpec as P

TOK = ("xh", "xl", "yh")
VOC = ("yl", "z", "c")
SIZES = (2, 2, 2, 2, 4, 2)
STRIPES = ("yh", "xl", "xh")
WALK = ("z", "yh", "yl", "xh", "xl")
EXCHANGE = ("z", "yh", "xh", "yl", "xl", "c")


def encode(partial):
    stripes, rows, width = partial.shape
    half = width // 2
    peak = jnp.maximum(jnp.max(jnp.abs(partial), axis=2), 1e-30)
    level = jnp.ceil(jnp.log2(peak) * 256.0)
    scale = jnp.exp2(-level / 256.0) * 32766.0
    code = jnp.clip(jnp.round(partial * scale[:, :, None]), -32767.0, 32767.0).astype(jnp.int32)
    words = (code[:, :, :half] << 16) | (code[:, :, half:] & 0xFFFF)
    tail = jnp.zeros((stripes, 8, half), jnp.int32).at[:, 0, :rows].set(level.astype(jnp.int32))
    return jnp.concatenate([words, tail], axis=1)


def row_of(place, core):
    head = (place >> 1) & 1
    row = ((place >> 2) & 3) * 64 + ((place >> 4) & 3) * 16 + (place >> 6) * 4 + core * 2 + (place & 1)
    return row, head


def teacher_kernel(core_ref, words_ref, mine_ref, theirs_ref, stats_ref, mine_out, theirs_out, copies_out, sum_ref):
    rows, width = sum_ref.shape
    senders = words_ref.shape[0]
    half = width // 2
    step = 32
    level = jnp.concatenate([words_ref[j, rows : rows + 1, :rows] for j in range(senders)], axis=0)
    scale = jnp.transpose(jnp.exp2(level.astype(jnp.float32) * (1.0 / 256.0)) * (0.5 / 32766.0))
    peaks, totals = [], []
    for at in range(0, rows, step):
        here = pl.ds(at, step)
        low = jnp.zeros((step, half), jnp.float32)
        high = jnp.zeros((step, half), jnp.float32)
        for j in range(senders):
            body = words_ref[j, here, :]
            by = scale[at : at + step, j : j + 1]
            high = high + (body >> 16).astype(jnp.float32) * by
            low = low + ((body << 16) >> 16).astype(jnp.float32) * by
        sum_ref[here, :half] = high
        sum_ref[here, half:] = low
        peak = jnp.maximum(jnp.max(high, axis=1, keepdims=True), jnp.max(low, axis=1, keepdims=True))
        total = jnp.sum(jnp.exp(high - peak), axis=1, keepdims=True)
        total = total + jnp.sum(jnp.exp(low - peak), axis=1, keepdims=True)
        peaks.append(peak)
        totals.append(total)
    peak = jnp.concatenate(peaks, axis=0)
    total = jnp.concatenate(totals, axis=0)
    lane = lax.broadcasted_iota(jnp.int32, (rows, rows), 1)
    place = lax.broadcasted_iota(jnp.int32, (rows, rows), 0)
    eye = lane == place
    first = sum_ref[...].astype(jnp.bfloat16)
    rest = sum_ref[...] - first.astype(jnp.float32)
    second = rest.astype(jnp.bfloat16)
    third = (rest - second.astype(jnp.float32)).astype(jnp.bfloat16)
    crosses = [jnp.zeros((1, rows), jnp.float32), jnp.zeros((1, rows), jnp.float32)]
    for side, scores, out in ((0, mine_ref, mine_out), (1, theirs_ref, theirs_out)):
        core = jnp.where(side == 0, core_ref[0], 1 - core_ref[0])
        row, head = row_of(place, core)
        chosen = lane == jnp.minimum(row + head, rows - 1)
        pick = jnp.where(chosen, 1.0, 0.0).astype(jnp.bfloat16)
        moved = jnp.dot(pick, first, preferred_element_type=jnp.float32)
        moved = moved + jnp.dot(pick, second, preferred_element_type=jnp.float32)
        out[...] = moved + jnp.dot(pick, third, preferred_element_type=jnp.float32)
        parts = []
        for at in range(0, rows, step):
            here = pl.ds(at, step)
            logits = out[here, :]
            weight = jnp.exp(logits - jnp.max(logits, axis=1, keepdims=True))
            parts.append(jnp.sum(weight * (logits - 0.5 * scores[here, :]), axis=1, keepdims=True))
        cross = jnp.concatenate(parts, axis=0)
        for k in (0, 1):
            inside = chosen & (head == k) & (row + k < rows)
            crosses[k] = crosses[k] + jnp.sum(jnp.where(inside, cross, 0.0), axis=0, keepdims=True)
    lines = [jnp.sum(jnp.where(eye, column, 0.0), axis=0, keepdims=True) for column in (peak, total)] + crosses
    edge = rows // 2
    tile = jnp.concatenate([line[:, at : at + edge] for line in lines for at in (0, edge)], axis=0)
    rest = jnp.concatenate([stats_ref[...], jnp.zeros((4, edge), jnp.float32)], axis=0)
    copies_out[:, 0:8, :] = jnp.broadcast_to(tile[None], (copies_out.shape[0], 8, edge))
    copies_out[:, 8:16, :] = jnp.broadcast_to(rest[None], (copies_out.shape[0], 8, edge))


def whole(shape):
    return pl.BlockSpec(shape, lambda *_: (0,) * len(shape))


def teacher_sum(core, words, mine, theirs, stats, devices):
    rows, width = mine.shape
    shape = jax.ShapeDtypeStruct
    copies = (devices, 16, rows // 2)
    return pl.pallas_call(
        teacher_kernel,
        out_shape=(
            shape(mine.shape, jnp.float32),
            shape(mine.shape, jnp.float32),
            shape(copies, jnp.float32),
        ),
        grid_spec=pltpu.PrefetchScalarGridSpec(
            num_scalar_prefetch=1,
            grid=(1,),
            in_specs=[whole(words.shape), whole(mine.shape), whole(theirs.shape), whole(stats.shape)],
            out_specs=(whole(mine.shape), whole(mine.shape), whole(copies)),
            scratch_shapes=[pltpu.VMEM((rows, width), jnp.float32)],
        ),
        compiler_params=pltpu.CompilerParams(vmem_limit_bytes=40 * 1024 * 1024),
        cost_estimate=pl.CostEstimate(
            flops=12 * rows * rows * width, bytes_accessed=10 * rows * width * 4, transcendentals=3 * rows * width
        ),
    )(core, words, mine, theirs, stats)


def slope_kernel(core_ref, shares_ref, ids_ref, mine_ref, theirs_ref, mine_t_ref, theirs_t_ref, mine_out, theirs_out, objective_out):
    devices = shares_ref.shape[0]
    rows, width = mine_ref.shape
    edge = rows // 2
    step = 32
    batch = 16
    four = lambda a: jnp.concatenate([a, a, a, a], axis=1)
    top = jnp.max(shares_ref[0:batch, 0:8, :], axis=0)
    for at in range(batch, devices, batch):
        top = jnp.maximum(top, jnp.max(shares_ref[at : at + batch, 0:8, :], axis=0))
    top = jnp.concatenate([top[0:2]] * 4, axis=0)
    sums = jnp.zeros((8, edge), jnp.float32)
    for at in range(0, devices, batch):
        part = shares_ref[at : at + batch, 0:8, :]
        sums = sums + jnp.sum(jnp.exp(four(part[:, 0:2]) - top[None]) * part, axis=0)
    line = lambda a: jnp.concatenate([a[0:1], a[1:2]], axis=1)
    t_total = sums[2:4]
    t_lse = line(top[0:2] + jnp.log(t_total))
    cross = [line(sums[4:6] / t_total), line(sums[6:8] / t_total)]

    ones, taus, targets = [], [], []
    quarter = devices // 4
    kind = lax.broadcasted_iota(jnp.int32, (batch, 8, edge), 1)
    for q in range(4):
        peak = jnp.max(shares_ref[q * quarter : (q + 1) * quarter, 8:16, :], axis=0)[0:1]
        total = jnp.zeros((8, edge), jnp.float32)
        for at in range(q * quarter, (q + 1) * quarter, batch):
            part = shares_ref[at : at + batch, 8:16, :]
            scale = jnp.exp(0.5 * (part[:, 0:1] - peak[None]))
            scale = jnp.broadcast_to(scale, part.shape)
            scale = jnp.where(kind == 1, scale * scale, jnp.where(kind == 2, scale, 1.0))
            total = total + jnp.sum(scale * part, axis=0)
        ones.append(peak + jnp.log(total[1:2]))
        taus.append(0.5 * peak + jnp.log(total[2:3]))
        targets.append(total[3:4])
    norms = jnp.transpose(jnp.concatenate(ones + taus + targets + targets, axis=0))

    lane = lax.broadcasted_iota(jnp.int32, (rows, rows), 1)
    place = lax.broadcasted_iota(jnp.int32, (rows, rows), 0)
    objective = [jnp.zeros((1, rows), jnp.float32), jnp.zeros((1, rows), jnp.float32)]
    base = core_ref[1]
    columns = lax.broadcasted_iota(jnp.int32, (step, width), 1) + base
    for side, scores, teacher, out in ((0, mine_ref, mine_t_ref, mine_out), (1, theirs_ref, theirs_t_ref, theirs_out)):
        first = (core_ref[0] == 0) == (side == 0)
        core = jnp.where(first, 0, 1)

        def column(n):
            low = jnp.concatenate([norms[:, n : n + 1], norms[:, n + 1 : n + 2]], axis=0)
            high = jnp.concatenate([norms[:, n + 2 : n + 3], norms[:, n + 3 : n + 4]], axis=0)
            return jnp.where(first, low, high)

        one, tau, target = column(0), column(4), column(8)
        row, head = row_of(place, core)
        chosen = lane == jnp.minimum(row + head, rows - 1)
        lse = jnp.sum(jnp.where(chosen, t_lse, 0.0), axis=1, keepdims=True)
        mixed = jnp.where(head == 0, cross[0], cross[1])
        mixed = jnp.sum(jnp.where(chosen, mixed, 0.0), axis=1, keepdims=True)
        weight = jnp.where((head[:, 0:1] == 1) & (row[:, 0:1] == rows - 1), 0.0, 1.0)
        loss = weight * (2.0 * (mixed - lse + tau) + 0.5 * (one - target))
        for k in (0, 1):
            inside = (lane == row) & (head == k)
            objective[k] = objective[k] + jnp.sum(jnp.where(inside, loss, 0.0), axis=0, keepdims=True)
        ids = jnp.where(first, ids_ref[0], ids_ref[1])
        for at in range(0, rows, step):
            here = pl.ds(at, step)
            part = slice(at, at + step)
            score = scores[here, :]
            grad = jnp.exp(0.5 * score - tau[part]) - jnp.exp(teacher[here, :] - lse[part])
            hit = jnp.where(columns == ids[part], 1.0, 0.0)
            grad = weight[part] * (grad + 0.5 * (jnp.exp(score - one[part]) - hit))
            out[here, :] = grad.astype(jnp.bfloat16)
    objective_out[...] = jnp.concatenate(objective + [jnp.zeros((6, rows), jnp.float32)], axis=0)


def slopes(core, base, shares, ids, mine, theirs, mine_t, theirs_t):
    rows, width = mine.shape
    shape = jax.ShapeDtypeStruct
    operands = (shares, ids, mine, theirs, mine_t, theirs_t)
    return pl.pallas_call(
        slope_kernel,
        out_shape=(
            shape(mine.shape, jnp.bfloat16),
            shape(mine.shape, jnp.bfloat16),
            shape((8, rows), jnp.float32),
        ),
        grid_spec=pltpu.PrefetchScalarGridSpec(
            num_scalar_prefetch=1,
            grid=(1,),
            in_specs=[whole(a.shape) for a in operands],
            out_specs=(whole(mine.shape), whole(mine.shape), whole((8, rows))),
        ),
        compiler_params=pltpu.CompilerParams(vmem_limit_bytes=40 * 1024 * 1024),
        cost_estimate=pl.CostEstimate(
            flops=40 * rows * width, bytes_accessed=6 * rows * width * 4, transcendentals=6 * rows * width
        ),
    )(jnp.stack([core, base]), *operands)


def merge(parts):
    peak = jnp.max(parts[:, 0], axis=0)
    scale = jnp.exp((parts[:, 0] - peak) * 0.5)
    return jnp.stack(
        [
            peak,
            jnp.sum(parts[:, 1] * (scale * scale), axis=0),
            jnp.sum(parts[:, 2] * scale, axis=0),
            jnp.sum(parts[:, 3], axis=0),
        ]
    )


def ring_gather(block, axes):
    size = lax.axis_size(axes)
    here = lax.axis_index(axes)
    whole = jnp.zeros((size,) + block.shape, block.dtype)
    whole = lax.dynamic_update_index_in_dim(whole, block, here, 0)
    for step in range(1, size):
        taken = lax.ppermute(block, axes, [(i, (i + step) % size) for i in range(size)])
        whole = lax.dynamic_update_index_in_dim(whole, taken, (here + size - step) % size, 0)
    return whole.reshape((size * block.shape[0],) + block.shape[1:])


def everywhere(value, axes, count):
    copies = jnp.broadcast_to(value, (count,) + value.shape)
    return lax.all_to_all(copies, axes, 0, 0, tiled=True)


def local(teacher_hidden, teacher_head, student_hidden, student_head, target_ids):
    core = lax.axis_index("c")
    chips = lax.axis_size(WALK)
    devices = lax.axis_size(EXCHANGE)
    stripes = teacher_head.shape[1]
    voc = teacher_head.shape[2]
    rows = teacher_hidden.shape[0]
    width = student_head.shape[0]
    base = lax.axis_index(TOK + VOC) * voc
    pair = [(0, 1), (1, 0)]

    plane = jnp.swapaxes(student_hidden, 0, 1).reshape(4, width)
    plane = everywhere(plane, ("yh", "yl", "xh", "xl"), 16).reshape(64, width)

    partial = jnp.einsum("rd,dsv->srv", teacher_hidden, teacher_head, preferred_element_type=jnp.float32)
    words = encode(partial)
    words = words.reshape((2, 2, 2) + words.shape[1:]).transpose(2, 1, 0, 3, 4).reshape(words.shape)
    words = lax.all_to_all(words, STRIPES, 0, 0, tiled=True)

    own = ring_gather(plane, "z")
    other = lax.ppermute(own, "c", pair)

    order = target_ids.reshape(4, 4, 4, 2, 2, 2)
    order = jnp.transpose(order, (3, 2, 1, 0, 5, 4)).reshape(2, rows, 1)
    columns = lax.broadcasted_iota(jnp.int32, (1, voc), 1) + base

    def student(hidden, side):
        scores = jnp.dot(hidden, student_head, preferred_element_type=jnp.float32)
        match = columns == jnp.where(side == 0, order[0], order[1])
        top = jnp.max(scores, axis=1, keepdims=True)
        powers = jnp.exp((scores - top) * 0.5)
        stats = jnp.stack(
            [
                top[:, 0],
                jnp.sum(powers * powers, axis=1),
                jnp.sum(powers, axis=1),
                jnp.sum(jnp.where(match, scores, 0.0), axis=1),
            ]
        )
        return scores, stats

    own_scores, own_stats = student(own, core)
    other_scores, other_stats = student(other, 1 - core)
    stats = jnp.stack(
        [jnp.where(core == 0, own_stats, other_stats), jnp.where(core == 0, other_stats, own_stats)], axis=1
    ).reshape(4, 2 * rows)
    around = [stats] + [lax.ppermute(stats, "z", [(i, (i + j) % 4) for i in range(4)]) for j in (1, 2, 3)]
    stats = merge(jnp.stack(around)).reshape(4, 4, rows // 2)
    stats = lax.dynamic_index_in_dim(stats, lax.axis_index("z"), 1, False)

    own_teacher, other_teacher, copies = teacher_sum(core[None], words, own_scores, other_scores, stats, devices)
    hidden = jnp.concatenate([own, other], axis=0)
    copies, hidden, order = lax.optimization_barrier((copies, hidden, order))
    shares = lax.all_to_all(copies, EXCHANGE, 0, 0, tiled=True)
    own_grad, other_grad, objective = slopes(
        core, base, shares, order, own_scores, other_scores, own_teacher, other_teacher
    )

    contract = (((1,), (1,)), ((), ()))
    give = lax.dot_general(other_grad, student_head, contract, preferred_element_type=jnp.float32)
    taken = lax.ppermute(give, "c", pair)
    keep = lax.dot_general(own_grad, student_head, contract, preferred_element_type=jnp.float32)
    grad = jnp.concatenate([own_grad, other_grad], axis=0)
    grad_head = lax.dot_general(
        hidden, grad, (((0,), (0,)), ((), ())), preferred_element_type=jnp.float32
    ).astype(jnp.bfloat16)
    objective = objective[:2].T

    share = (keep + taken).astype(jnp.bfloat16).reshape(chips, 4, width)
    share, grad_head, objective = lax.optimization_barrier((share, grad_head, objective))
    share = lax.all_to_all(share, WALK, 0, 0, tiled=True)
    grad_hidden = jnp.sum(share.astype(jnp.float32), axis=0).astype(jnp.bfloat16)
    grad_hidden = jnp.swapaxes(grad_hidden.reshape(2, 2, width), 0, 1)
    return objective, grad_hidden, grad_head


def solution(mesh):
    fine = Mesh(mesh.devices.reshape(SIZES), TOK + VOC)
    return jax.shard_map(
        local,
        mesh=fine,
        in_specs=(
            P(None, TOK),
            P(TOK, None, VOC),
            P(TOK + VOC, None, None),
            P(None, TOK + VOC),
            P(),
        ),
        out_specs=(P(), P(TOK + VOC, None, None), P(None, TOK + VOC)),
        check_vma=False,
    )
```

```python
import jax
import jax.numpy as jnp
from jax import lax
from jax.experimental import pallas as pl
from jax.experimental.pallas import tpu as pltpu
from jax.sharding import Mesh
from jax.sharding import PartitionSpec as P

TOK = ("xh", "xl", "yh")
VOC = ("yl", "z", "c")
SIZES = (2, 2, 2, 2, 4, 2)
STRIPES = ("yh", "xl", "xh")
WALK = ("z", "yh", "yl", "xh", "xl")
EXCHANGE = ("z", "yh", "xh", "yl", "xl", "c")


def encode(partial):
    stripes, rows, width = partial.shape
    half = width // 2
    peak = jnp.maximum(jnp.max(jnp.abs(partial), axis=2), 1e-30)
    level = jnp.ceil(jnp.log2(peak) * 256.0)
    scale = jnp.exp2(-level / 256.0) * 32766.0
    code = jnp.clip(jnp.round(partial * scale[:, :, None]), -32767.0, 32767.0).astype(jnp.int32)
    words = (code[:, :, :half] << 16) | (code[:, :, half:] & 0xFFFF)
    tail = jnp.zeros((stripes, 8, half), jnp.int32).at[:, 0, :rows].set(level.astype(jnp.int32))
    return jnp.concatenate([words, tail], axis=1)


def row_of(place, core):
    head = (place >> 1) & 1
    row = ((place >> 2) & 3) * 64 + ((place >> 4) & 3) * 16 + (place >> 6) * 4 + core * 2 + (place & 1)
    return row, head


def teacher_kernel(core_ref, words_ref, mine_out, theirs_out, lines_out, sum_ref):
    rows, width = sum_ref.shape
    senders = words_ref.shape[0]
    half = width // 2
    step = 32
    level = jnp.concatenate([words_ref[j, rows : rows + 1, :rows] for j in range(senders)], axis=0)
    scale = jnp.transpose(jnp.exp2(level.astype(jnp.float32) * (1.0 / 256.0)) * (0.5 / 32766.0))
    peaks, totals = [], []
    for at in range(0, rows, step):
        here = pl.ds(at, step)
        low = jnp.zeros((step, half), jnp.float32)
        high = jnp.zeros((step, half), jnp.float32)
        for j in range(senders):
            body = words_ref[j, here, :]
            by = scale[at : at + step, j : j + 1]
            high = high + (body >> 16).astype(jnp.float32) * by
            low = low + ((body << 16) >> 16).astype(jnp.float32) * by
        sum_ref[here, :half] = high
        sum_ref[here, half:] = low
        peak = jnp.maximum(jnp.max(high, axis=1, keepdims=True), jnp.max(low, axis=1, keepdims=True))
        total = jnp.sum(jnp.exp(high - peak), axis=1, keepdims=True)
        total = total + jnp.sum(jnp.exp(low - peak), axis=1, keepdims=True)
        peaks.append(peak)
        totals.append(total)
    peak = jnp.concatenate(peaks, axis=0)
    total = jnp.concatenate(totals, axis=0)
    lane = lax.broadcasted_iota(jnp.int32, (rows, rows), 1)
    place = lax.broadcasted_iota(jnp.int32, (rows, rows), 0)
    eye = lane == place
    first = sum_ref[...].astype(jnp.bfloat16)
    rest = sum_ref[...] - first.astype(jnp.float32)
    second = rest.astype(jnp.bfloat16)
    third = (rest - second.astype(jnp.float32)).astype(jnp.bfloat16)
    for side, out in ((0, mine_out), (1, theirs_out)):
        core = jnp.where(side == 0, core_ref[0], 1 - core_ref[0])
        row, head = row_of(place, core)
        chosen = lane == jnp.minimum(row + head, rows - 1)
        pick = jnp.where(chosen, 1.0, 0.0).astype(jnp.bfloat16)
        moved = jnp.dot(pick, first, preferred_element_type=jnp.float32)
        moved = moved + jnp.dot(pick, second, preferred_element_type=jnp.float32)
        out[...] = moved + jnp.dot(pick, third, preferred_element_type=jnp.float32)
    lines = [jnp.sum(jnp.where(eye, column, 0.0), axis=0, keepdims=True) for column in (peak, total)]
    lines_out[...] = jnp.concatenate(lines + [jnp.zeros((6, rows), jnp.float32)], axis=0)


def cross_kernel(
    core_ref, lines_ref, mine_t_ref, theirs_t_ref, mine_ref, theirs_ref, stats_ref, ids_ref, copies_out, ids_out
):
    rows = mine_ref.shape[0]
    edge = rows // 2
    step = 32
    lane = lax.broadcasted_iota(jnp.int32, (rows, rows), 1)
    place = lax.broadcasted_iota(jnp.int32, (rows, rows), 0)
    ids_out[...] = ids_ref[...]
    crosses = [jnp.zeros((1, rows), jnp.float32), jnp.zeros((1, rows), jnp.float32)]
    for side, teacher, scores in ((0, mine_t_ref, mine_ref), (1, theirs_t_ref, theirs_ref)):
        core = jnp.where(side == 0, core_ref[0], 1 - core_ref[0])
        row, head = row_of(place, core)
        parts = []
        for at in range(0, rows, step):
            here = pl.ds(at, step)
            logits = teacher[here, :]
            weight = jnp.exp(logits - jnp.max(logits, axis=1, keepdims=True))
            parts.append(jnp.sum(weight * (logits - 0.5 * scores[here, :]), axis=1, keepdims=True))
        cross = jnp.concatenate(parts, axis=0)
        for k in (0, 1):
            inside = (lane == row + k) & (head == k)
            crosses[k] = crosses[k] + jnp.sum(jnp.where(inside, cross, 0.0), axis=0, keepdims=True)
    lines = [lines_ref[0:1, :], lines_ref[1:2, :]] + crosses
    tile = jnp.concatenate([line[:, at : at + edge] for line in lines for at in (0, edge)], axis=0)
    rest = jnp.concatenate([stats_ref[...], jnp.zeros((4, edge), jnp.float32)], axis=0)
    copies_out[:, 0:8, :] = jnp.broadcast_to(tile[None], (copies_out.shape[0], 8, edge))
    copies_out[:, 8:16, :] = jnp.broadcast_to(rest[None], (copies_out.shape[0], 8, edge))


def whole(shape):
    return pl.BlockSpec(shape, lambda *_: (0,) * len(shape), pipeline_mode=pl.Buffered(1))


def call(kernel, scalars, operands, results, grant, cost, scratch=()):
    return pl.pallas_call(
        kernel,
        out_shape=tuple(results),
        grid_spec=pltpu.PrefetchScalarGridSpec(
            num_scalar_prefetch=1,
            grid=(1,),
            in_specs=[whole(a.shape) for a in operands],
            out_specs=tuple(whole(a.shape) for a in results),
            scratch_shapes=scratch,
        ),
        compiler_params=pltpu.CompilerParams(vmem_limit_bytes=grant << 20),
        cost_estimate=pl.CostEstimate(flops=cost[0], bytes_accessed=cost[1], transcendentals=cost[2]),
    )(scalars, *operands)


def teacher_sum(scalars, words, rows, width):
    half = jax.ShapeDtypeStruct((rows, width), jnp.float32)
    lines = jax.ShapeDtypeStruct((8, rows), jnp.float32)
    area = rows * width
    scratch = [pltpu.VMEM((rows, width), jnp.float32)]
    return call(teacher_kernel, scalars, (words,), (half, half, lines), 12, (12 * rows * area, 32 * area, area), scratch)


def cross_terms(scalars, operands, devices):
    lines, ids = operands[0], operands[-1]
    copies = jax.ShapeDtypeStruct((devices, 16, lines.shape[1] // 2), jnp.float32)
    area = operands[1].size
    return call(cross_kernel, scalars, operands, (copies, jax.ShapeDtypeStruct(ids.shape, ids.dtype)), 9, (16 * area, 20 * area, 2 * area))


def slope_kernel(core_ref, shares_ref, ids_ref, mine_ref, theirs_ref, mine_t_ref, theirs_t_ref, mine_out, theirs_out, objective_out):
    devices = shares_ref.shape[0]
    rows, width = mine_ref.shape
    edge = rows // 2
    step = 32
    batch = 16
    four = lambda a: jnp.concatenate([a, a, a, a], axis=1)
    top = jnp.max(shares_ref[0:batch, 0:8, :], axis=0)
    for at in range(batch, devices, batch):
        top = jnp.maximum(top, jnp.max(shares_ref[at : at + batch, 0:8, :], axis=0))
    top = jnp.concatenate([top[0:2]] * 4, axis=0)
    sums = jnp.zeros((8, edge), jnp.float32)
    for at in range(0, devices, batch):
        part = shares_ref[at : at + batch, 0:8, :]
        sums = sums + jnp.sum(jnp.exp(four(part[:, 0:2]) - top[None]) * part, axis=0)
    line = lambda a: jnp.concatenate([a[0:1], a[1:2]], axis=1)
    t_total = sums[2:4]
    t_lse = line(top[0:2] + jnp.log(t_total))
    cross = [line(sums[4:6] / t_total), line(sums[6:8] / t_total)]

    ones, taus, targets = [], [], []
    quarter = devices // 4
    kind = lax.broadcasted_iota(jnp.int32, (batch, 8, edge), 1)
    for q in range(4):
        peak = jnp.max(shares_ref[q * quarter : (q + 1) * quarter, 8:16, :], axis=0)[0:1]
        total = jnp.zeros((8, edge), jnp.float32)
        for at in range(q * quarter, (q + 1) * quarter, batch):
            part = shares_ref[at : at + batch, 8:16, :]
            scale = jnp.exp(0.5 * (part[:, 0:1] - peak[None]))
            scale = jnp.broadcast_to(scale, part.shape)
            scale = jnp.where(kind == 1, scale * scale, jnp.where(kind == 2, scale, 1.0))
            total = total + jnp.sum(scale * part, axis=0)
        ones.append(peak + jnp.log(total[1:2]))
        taus.append(0.5 * peak + jnp.log(total[2:3]))
        targets.append(total[3:4])
    norms = jnp.transpose(jnp.concatenate(ones + taus + targets + targets, axis=0))

    lane = lax.broadcasted_iota(jnp.int32, (rows, rows), 1)
    place = lax.broadcasted_iota(jnp.int32, (rows, rows), 0)
    objective = [jnp.zeros((1, rows), jnp.float32), jnp.zeros((1, rows), jnp.float32)]
    base = core_ref[1]
    columns = lax.broadcasted_iota(jnp.int32, (step, width), 1) + base
    for side, scores, teacher, out in ((0, mine_ref, mine_t_ref, mine_out), (1, theirs_ref, theirs_t_ref, theirs_out)):
        first = (core_ref[0] == 0) == (side == 0)
        core = jnp.where(first, 0, 1)

        def column(n):
            low = jnp.concatenate([norms[:, n : n + 1], norms[:, n + 1 : n + 2]], axis=0)
            high = jnp.concatenate([norms[:, n + 2 : n + 3], norms[:, n + 3 : n + 4]], axis=0)
            return jnp.where(first, low, high)

        one, tau, target = column(0), column(4), column(8)
        row, head = row_of(place, core)
        chosen = lane == jnp.minimum(row + head, rows - 1)
        lse = jnp.sum(jnp.where(chosen, t_lse, 0.0), axis=1, keepdims=True)
        mixed = jnp.where(head == 0, cross[0], cross[1])
        mixed = jnp.sum(jnp.where(chosen, mixed, 0.0), axis=1, keepdims=True)
        weight = jnp.where((head[:, 0:1] == 1) & (row[:, 0:1] == rows - 1), 0.0, 1.0)
        loss = weight * (2.0 * (mixed - lse + tau) + 0.5 * (one - target))
        for k in (0, 1):
            inside = (lane == row) & (head == k)
            objective[k] = objective[k] + jnp.sum(jnp.where(inside, loss, 0.0), axis=0, keepdims=True)
        ids = jnp.where(first, ids_ref[0], ids_ref[1])
        for at in range(0, rows, step):
            here = pl.ds(at, step)
            part = slice(at, at + step)
            score = scores[here, :]
            grad = jnp.exp(0.5 * score - tau[part]) - jnp.exp(teacher[here, :] - lse[part])
            hit = jnp.where(columns == ids[part], 1.0, 0.0)
            grad = weight[part] * (grad + 0.5 * (jnp.exp(score - one[part]) - hit))
            out[here, :] = grad.astype(jnp.bfloat16)
    objective_out[...] = jnp.concatenate(objective + [jnp.zeros((6, rows), jnp.float32)], axis=0)


def slopes(scalars, *operands):
    half = jax.ShapeDtypeStruct(operands[2].shape, jnp.bfloat16)
    lines = jax.ShapeDtypeStruct((8, half.shape[0]), jnp.float32)
    area = operands[2].size
    return call(slope_kernel, scalars, operands, (half, half, lines), 9, (40 * area, 24 * area, 6 * area))


def merge(parts):
    peak = jnp.max(parts[:, 0], axis=0)
    scale = jnp.exp((parts[:, 0] - peak) * 0.5)
    return jnp.stack(
        [
            peak,
            jnp.sum(parts[:, 1] * (scale * scale), axis=0),
            jnp.sum(parts[:, 2] * scale, axis=0),
            jnp.sum(parts[:, 3], axis=0),
        ]
    )


def ring_gather(block, axes):
    size = lax.axis_size(axes)
    here = lax.axis_index(axes)
    whole = jnp.zeros((size,) + block.shape, block.dtype)
    whole = lax.dynamic_update_index_in_dim(whole, block, here, 0)
    for step in range(1, size):
        taken = lax.ppermute(block, axes, [(i, (i + step) % size) for i in range(size)])
        whole = lax.dynamic_update_index_in_dim(whole, taken, (here + size - step) % size, 0)
    return whole.reshape((size * block.shape[0],) + block.shape[1:])


def everywhere(value, axes, count):
    copies = jnp.broadcast_to(value, (count,) + value.shape)
    return lax.all_to_all(copies, axes, 0, 0, tiled=True)


def local(teacher_hidden, teacher_head, student_hidden, student_head, target_ids):
    core = lax.axis_index("c")
    chips = lax.axis_size(WALK)
    devices = lax.axis_size(EXCHANGE)
    stripes = teacher_head.shape[1]
    voc = teacher_head.shape[2]
    rows = teacher_hidden.shape[0]
    width = student_head.shape[0]
    base = lax.axis_index(TOK + VOC) * voc
    pair = [(0, 1), (1, 0)]

    partial = jnp.einsum("rd,dsv->srv", teacher_hidden, teacher_head, preferred_element_type=jnp.float32)
    words = encode(partial)
    words = words.reshape((2, 2, 2) + words.shape[1:]).transpose(2, 1, 0, 3, 4).reshape(words.shape)
    words = lax.all_to_all(words, STRIPES, 0, 0, tiled=True)

    plane = jnp.swapaxes(student_hidden, 0, 1).reshape(4, width)
    plane = everywhere(plane, ("yh", "yl", "xh", "xl"), 16).reshape(64, width)

    own = ring_gather(plane, "z")
    other = lax.ppermute(own, "c", pair)

    order = target_ids.reshape(4, 4, 4, 2, 2, 2)
    order = jnp.transpose(order, (3, 2, 1, 0, 5, 4)).reshape(2, rows, 1)
    columns = lax.broadcasted_iota(jnp.int32, (1, voc), 1) + base

    def student(hidden, side):
        scores = jnp.dot(hidden, student_head, preferred_element_type=jnp.float32)
        match = columns == jnp.where(side == 0, order[0], order[1])
        top = jnp.max(scores, axis=1, keepdims=True)
        powers = jnp.exp((scores - top) * 0.5)
        stats = jnp.stack(
            [
                top[:, 0],
                jnp.sum(powers * powers, axis=1),
                jnp.sum(powers, axis=1),
                jnp.sum(jnp.where(match, scores, 0.0), axis=1),
            ]
        )
        return scores, stats

    own_scores, own_stats = student(own, core)
    other_scores, other_stats = student(other, 1 - core)
    stats = jnp.stack(
        [jnp.where(core == 0, own_stats, other_stats), jnp.where(core == 0, other_stats, own_stats)], axis=1
    ).reshape(4, 2 * rows)
    stats = stats + 0.0 * words[0, 0, 0].astype(jnp.float32)
    around = [stats] + [lax.ppermute(stats, "z", [(i, (i + j) % 4) for i in range(4)]) for j in (1, 2, 3)]
    stats = merge(jnp.stack(around)).reshape(4, 4, rows // 2)
    stats = lax.dynamic_index_in_dim(stats, lax.axis_index("z"), 1, False)

    scalars = jnp.stack([core, base])
    own_teacher, other_teacher, lines = teacher_sum(scalars, words, rows, voc)
    copies, order = cross_terms(
        scalars, (lines, own_teacher, other_teacher, own_scores, other_scores, stats, order), devices
    )
    hidden = jnp.concatenate([own, other], axis=0)
    copies, hidden, order = lax.optimization_barrier((copies, hidden, order))
    shares = lax.all_to_all(copies, EXCHANGE, 0, 0, tiled=True)
    own_grad, other_grad, objective = slopes(
        scalars, shares, order, own_scores, other_scores, own_teacher, other_teacher
    )

    contract = (((1,), (1,)), ((), ()))
    give = lax.dot_general(other_grad, student_head, contract, preferred_element_type=jnp.float32)
    taken = lax.ppermute(give, "c", pair)
    keep = lax.dot_general(own_grad, student_head, contract, preferred_element_type=jnp.float32)
    grad = jnp.concatenate([own_grad, other_grad], axis=0)
    grad_head = lax.dot_general(
        hidden, grad, (((0,), (0,)), ((), ())), preferred_element_type=jnp.float32
    ).astype(jnp.bfloat16)
    objective = objective[:2].T

    share = (keep + taken).astype(jnp.bfloat16).reshape(chips, 4, width)
    share, grad_head, objective = lax.optimization_barrier((share, grad_head, objective))
    share = lax.all_to_all(share, WALK, 0, 0, tiled=True)
    grad_hidden = jnp.sum(share.astype(jnp.float32), axis=0).astype(jnp.bfloat16)
    grad_hidden = jnp.swapaxes(grad_hidden.reshape(2, 2, width), 0, 1)
    return objective, grad_hidden, grad_head


def solution(mesh):
    fine = Mesh(mesh.devices.reshape(SIZES), TOK + VOC)
    return jax.shard_map(
        local,
        mesh=fine,
        in_specs=(
            P(None, TOK),
            P(TOK, None, VOC),
            P(TOK + VOC, None, None),
            P(None, TOK + VOC),
            P(),
        ),
        out_specs=(P(), P(TOK + VOC, None, None), P(None, TOK + VOC)),
        check_vma=False,
    )
```

```python
import functools

import jax
import jax.numpy as jnp
from jax import lax
from jax.experimental import pallas as pl
from jax.experimental.pallas import tpu as pltpu
from jax.sharding import Mesh
from jax.sharding import PartitionSpec as P

TOK = ("xh", "xl", "yh")
VOC = ("yl", "z", "c")
SIZES = (2, 2, 2, 2, 4, 2)
GRANT = 14
STRIPES = ("yh", "xl", "xh")
WALK = ("z", "yh", "yl", "xh", "xl")
EXCHANGE = ("z", "yh", "xh", "yl", "xl")


def encode(partial):
    stripes, rows, width = partial.shape
    half = width // 2
    peak = jnp.maximum(jnp.max(jnp.abs(partial), axis=2), 1e-30)
    level = jnp.ceil(jnp.log2(peak) * 256.0)
    scale = jnp.exp2(-level / 256.0) * 32766.0
    code = jnp.clip(jnp.round(partial * scale[:, :, None]), -32767.0, 32767.0).astype(jnp.int32)
    words = (code[:, :, :half] << 16) | (code[:, :, half:] & 0xFFFF)
    tail = jnp.zeros((stripes, 8, half), jnp.int32).at[:, 0, :rows].set(level.astype(jnp.int32))
    return jnp.concatenate([words, tail], axis=1)


def row_of(place, core):
    head = (place >> 1) & 1
    row = ((place >> 2) & 3) * 64 + ((place >> 4) & 3) * 16 + (place >> 6) * 4 + core * 2 + (place & 1)
    return row, head


def teacher_kernel(core_ref, words_ref, mine_ref, theirs_ref, mine_out, theirs_out, tile_out, sum_ref):
    rows, width = sum_ref.shape
    senders = words_ref.shape[0]
    half = width // 2
    step = 32
    level = jnp.concatenate([words_ref[j, rows : rows + 1, :rows] for j in range(senders)], axis=0)
    scale = jnp.transpose(jnp.exp2(level.astype(jnp.float32) * (1.0 / 256.0)) * (0.5 / 32766.0))
    peaks, totals = [], []
    for at in range(0, rows, step):
        here = pl.ds(at, step)
        low = jnp.zeros((step, half), jnp.float32)
        high = jnp.zeros((step, half), jnp.float32)
        for j in range(senders):
            body = words_ref[j, here, :]
            by = scale[at : at + step, j : j + 1]
            high = high + (body >> 16).astype(jnp.float32) * by
            low = low + ((body << 16) >> 16).astype(jnp.float32) * by
        sum_ref[here, :half] = high
        sum_ref[here, half:] = low
        peak = jnp.maximum(jnp.max(high, axis=1, keepdims=True), jnp.max(low, axis=1, keepdims=True))
        total = jnp.sum(jnp.exp(high - peak), axis=1, keepdims=True)
        total = total + jnp.sum(jnp.exp(low - peak), axis=1, keepdims=True)
        peaks.append(peak)
        totals.append(total)
    peak = jnp.concatenate(peaks, axis=0)
    total = jnp.concatenate(totals, axis=0)
    lane = lax.broadcasted_iota(jnp.int32, (rows, rows), 1)
    place = lax.broadcasted_iota(jnp.int32, (rows, rows), 0)
    eye = lane == place
    first = sum_ref[...].astype(jnp.bfloat16)
    rest = sum_ref[...] - first.astype(jnp.float32)
    second = rest.astype(jnp.bfloat16)
    third = (rest - second.astype(jnp.float32)).astype(jnp.bfloat16)
    crosses = [jnp.zeros((1, rows), jnp.float32), jnp.zeros((1, rows), jnp.float32)]
    for side, scores, out in ((0, mine_ref, mine_out), (1, theirs_ref, theirs_out)):
        core = jnp.where(side == 0, core_ref[0], 1 - core_ref[0])
        row, head = row_of(place, core)
        chosen = lane == jnp.minimum(row + head, rows - 1)
        pick = jnp.where(chosen, 1.0, 0.0).astype(jnp.bfloat16)
        moved = jnp.dot(pick, first, preferred_element_type=jnp.float32)
        moved = moved + jnp.dot(pick, second, preferred_element_type=jnp.float32)
        out[...] = moved + jnp.dot(pick, third, preferred_element_type=jnp.float32)
        parts = []
        for at in range(0, rows, step):
            here = pl.ds(at, step)
            logits = out[here, :]
            weight = jnp.exp(logits - jnp.max(logits, axis=1, keepdims=True))
            parts.append(jnp.sum(weight * (logits - 0.5 * scores[here, :]), axis=1, keepdims=True))
        cross = jnp.concatenate(parts, axis=0)
        for k in (0, 1):
            inside = (lane == row + k) & (head == k)
            crosses[k] = crosses[k] + jnp.sum(jnp.where(inside, cross, 0.0), axis=0, keepdims=True)
    lines = [jnp.sum(jnp.where(eye, column, 0.0), axis=0, keepdims=True) for column in (peak, total)] + crosses
    edge = rows // 2
    tile_out[...] = jnp.concatenate([line[:, at : at + edge] for line in lines for at in (0, edge)], axis=0)


def chosen_id(ids_ref, place, row, head):
    lane = lax.broadcasted_iota(jnp.int32, place.shape, 1)
    ids = jnp.where(head == 0, ids_ref[0:1, :], ids_ref[1:2, :])
    return jnp.sum(jnp.where(lane == row, ids, 0.0), axis=1, keepdims=True)


def student_kernel(side, core_ref, hidden_ref, head_ref, ids_ref, scores_out, lines_out):
    rows, width = scores_out.shape
    step = 32
    for at in range(0, width, 256):
        scores_out[:, at : at + 256] = jnp.dot(
            hidden_ref[...], head_ref[:, at : at + 256], preferred_element_type=jnp.float32
        )
    lane = lax.broadcasted_iota(jnp.int32, (rows, rows), 1)
    place = lax.broadcasted_iota(jnp.int32, (rows, rows), 0)
    core = jnp.where(side == 0, core_ref[0], 1 - core_ref[0])
    row, head = row_of(place, core)
    ids = chosen_id(ids_ref, place, row, head)
    columns = (lax.broadcasted_iota(jnp.int32, (step, width), 1) + core_ref[1]).astype(jnp.float32)
    found = [[], [], [], []]
    for at in range(0, rows, step):
        scores = scores_out[at : at + step, :]
        peak = jnp.max(scores, axis=1, keepdims=True)
        power = jnp.exp((scores - peak) * 0.5)
        found[0].append(peak)
        found[1].append(jnp.sum(power * power, axis=1, keepdims=True))
        found[2].append(jnp.sum(power, axis=1, keepdims=True))
        found[3].append(jnp.sum(jnp.where(columns == ids[at : at + step], scores, 0.0), axis=1, keepdims=True))
    eye = lane == place
    lines = [jnp.sum(jnp.where(eye, jnp.concatenate(f, axis=0), 0.0), axis=0, keepdims=True) for f in found]
    lines_out[...] = jnp.concatenate(lines + [jnp.zeros((4, rows), jnp.float32)], axis=0)


def copy_kernel(core_ref, mine_ref, theirs_ref, stats_ref, copies_out):
    mine, theirs = mine_ref[...], theirs_ref[...]
    top = jnp.maximum(mine[0:2], theirs[0:2])
    both = [jnp.exp(a[0:2] - top) for a in (mine, theirs)]
    both = [jnp.concatenate([b, b, b, b], axis=0) for b in both]
    tile = mine * both[0] + theirs * both[1]
    tile = jnp.concatenate([top, tile[2:8]], axis=0)
    rest = jnp.concatenate([stats_ref[...], jnp.zeros_like(stats_ref)], axis=0)
    copies_out[:, 0:8, :] = jnp.broadcast_to(tile[None], copies_out[:, 0:8, :].shape)
    copies_out[:, 8:16, :] = jnp.broadcast_to(rest[None], copies_out[:, 8:16, :].shape)


def whole(shape):
    return pl.BlockSpec(shape, lambda *_: (0,) * len(shape), pipeline_mode=pl.Buffered(1))


def call(kernel, scalars, operands, results, grant, cost, scratch=()):
    return pl.pallas_call(
        kernel,
        out_shape=tuple(results),
        grid_spec=pltpu.PrefetchScalarGridSpec(
            num_scalar_prefetch=1,
            grid=(1,),
            in_specs=[whole(a.shape) for a in operands],
            out_specs=tuple(whole(a.shape) for a in results),
            scratch_shapes=scratch,
        ),
        compiler_params=pltpu.CompilerParams(vmem_limit_bytes=grant << 20),
        cost_estimate=pl.CostEstimate(flops=cost[0], bytes_accessed=cost[1], transcendentals=cost[2]),
    )(scalars, *operands)


def teacher_sum(scalars, words, mine, theirs):
    rows, width = mine.shape
    area = rows * width
    tile = jax.ShapeDtypeStruct((8, rows // 2), jnp.float32)
    half = jax.ShapeDtypeStruct(mine.shape, jnp.float32)
    scratch = [pltpu.VMEM((rows, width), jnp.float32)]
    operands = (words, mine, theirs)
    return call(teacher_kernel, scalars, operands, (half, half, tile), GRANT, (12 * rows * area, 40 * area, 3 * area), scratch)


def student_half(side, scalars, hidden, head, ids):
    rows, width = hidden.shape[0], head.shape[1]
    area = rows * width
    results = (jax.ShapeDtypeStruct((rows, width), jnp.float32), jax.ShapeDtypeStruct((8, rows), jnp.float32))
    cost = (2 * area * hidden.shape[1], 4 * area + 2 * head.size, area)
    return call(functools.partial(student_kernel, side), scalars, (hidden, head, ids), results, GRANT, cost)


def chip_copies(scalars, mine, theirs, stats, chips):
    copies = jax.ShapeDtypeStruct((chips, 16, mine.shape[1]), jnp.float32)
    return call(copy_kernel, scalars, (mine, theirs, stats), (copies,), GRANT, (mine.size, 4 * copies.size, mine.size))[0]


def slope_kernel(core_ref, shares_ref, ids_ref, mine_ref, theirs_ref, mine_t_ref, theirs_t_ref, mine_out, theirs_out, objective_out):
    devices = shares_ref.shape[0]
    rows, width = mine_ref.shape
    edge = rows // 2
    step = 32
    batch = 16
    four = lambda a: jnp.concatenate([a, a, a, a], axis=1)
    top = jnp.max(shares_ref[0:batch, 0:8, :], axis=0)
    for at in range(batch, devices, batch):
        top = jnp.maximum(top, jnp.max(shares_ref[at : at + batch, 0:8, :], axis=0))
    top = jnp.concatenate([top[0:2]] * 4, axis=0)
    sums = jnp.zeros((8, edge), jnp.float32)
    for at in range(0, devices, batch):
        part = shares_ref[at : at + batch, 0:8, :]
        sums = sums + jnp.sum(jnp.exp(four(part[:, 0:2]) - top[None]) * part, axis=0)
    line = lambda a: jnp.concatenate([a[0:1], a[1:2]], axis=1)
    t_total = sums[2:4]
    t_lse = line(top[0:2] + jnp.log(t_total))
    cross = [line(sums[4:6] / t_total), line(sums[6:8] / t_total)]

    ones, taus, targets = [], [], []
    quarter = devices // 4
    kind = lax.broadcasted_iota(jnp.int32, (batch, 8, edge), 1)
    for q in range(4):
        peak = jnp.max(shares_ref[q * quarter : (q + 1) * quarter, 8:16, :], axis=0)[0:1]
        total = jnp.zeros((8, edge), jnp.float32)
        for at in range(q * quarter, (q + 1) * quarter, batch):
            part = shares_ref[at : at + batch, 8:16, :]
            scale = jnp.exp(0.5 * (part[:, 0:1] - peak[None]))
            scale = jnp.broadcast_to(scale, part.shape)
            scale = jnp.where(kind == 1, scale * scale, jnp.where(kind == 2, scale, 1.0))
            total = total + jnp.sum(scale * part, axis=0)
        ones.append(peak + jnp.log(total[1:2]))
        taus.append(0.5 * peak + jnp.log(total[2:3]))
        targets.append(total[3:4])
    norms = jnp.transpose(jnp.concatenate(ones + taus + targets + targets, axis=0))

    lane = lax.broadcasted_iota(jnp.int32, (rows, rows), 1)
    place = lax.broadcasted_iota(jnp.int32, (rows, rows), 0)
    objective = [jnp.zeros((1, rows), jnp.float32), jnp.zeros((1, rows), jnp.float32)]
    base = core_ref[1]
    columns = (lax.broadcasted_iota(jnp.int32, (step, width), 1) + base).astype(jnp.float32)
    for side, scores, teacher, out in ((0, mine_ref, mine_t_ref, mine_out), (1, theirs_ref, theirs_t_ref, theirs_out)):
        first = (core_ref[0] == 0) == (side == 0)
        core = jnp.where(first, 0, 1)

        def column(n):
            low = jnp.concatenate([norms[:, n : n + 1], norms[:, n + 1 : n + 2]], axis=0)
            high = jnp.concatenate([norms[:, n + 2 : n + 3], norms[:, n + 3 : n + 4]], axis=0)
            return jnp.where(first, low, high)

        one, tau, target = column(0), column(4), column(8)
        row, head = row_of(place, core)
        chosen = lane == jnp.minimum(row + head, rows - 1)
        lse = jnp.sum(jnp.where(chosen, t_lse, 0.0), axis=1, keepdims=True)
        mixed = jnp.where(head == 0, cross[0], cross[1])
        mixed = jnp.sum(jnp.where(chosen, mixed, 0.0), axis=1, keepdims=True)
        weight = jnp.where((head[:, 0:1] == 1) & (row[:, 0:1] == rows - 1), 0.0, 1.0)
        loss = weight * (2.0 * (mixed - lse + tau) + 0.5 * (one - target))
        for k in (0, 1):
            inside = (lane == row) & (head == k)
            objective[k] = objective[k] + jnp.sum(jnp.where(inside, loss, 0.0), axis=0, keepdims=True)
        ids = chosen_id(ids_ref, place, row, head)
        for at in range(0, rows, step):
            here = pl.ds(at, step)
            part = slice(at, at + step)
            score = scores[here, :]
            grad = jnp.exp(0.5 * score - tau[part]) - jnp.exp(teacher[here, :] - lse[part])
            hit = jnp.where(columns == ids[part], 1.0, 0.0)
            grad = weight[part] * (grad + 0.5 * (jnp.exp(score - one[part]) - hit))
            out[here, :] = grad.astype(jnp.bfloat16)
    objective_out[...] = jnp.concatenate(objective + [jnp.zeros((6, rows), jnp.float32)], axis=0)


def slopes(scalars, *operands):
    half = jax.ShapeDtypeStruct(operands[2].shape, jnp.bfloat16)
    lines = jax.ShapeDtypeStruct((8, half.shape[0]), jnp.float32)
    area = operands[2].size
    return call(slope_kernel, scalars, operands, (half, half, lines), GRANT, (40 * area, 24 * area, 6 * area))


def merge(parts):
    peak = jnp.max(parts[:, 0], axis=0)
    scale = jnp.exp((parts[:, 0] - peak) * 0.5)
    return jnp.stack(
        [
            peak,
            jnp.sum(parts[:, 1] * (scale * scale), axis=0),
            jnp.sum(parts[:, 2] * scale, axis=0),
            jnp.sum(parts[:, 3], axis=0),
        ]
    )


def ring_gather(block, axes):
    size = lax.axis_size(axes)
    here = lax.axis_index(axes)
    whole = jnp.zeros((size,) + block.shape, block.dtype)
    whole = lax.dynamic_update_index_in_dim(whole, block, here, 0)
    for step in range(1, size):
        taken = lax.ppermute(block, axes, [(i, (i + step) % size) for i in range(size)])
        whole = lax.dynamic_update_index_in_dim(whole, taken, (here + size - step) % size, 0)
    return whole.reshape((size * block.shape[0],) + block.shape[1:])


def everywhere(value, axes, count):
    copies = jnp.broadcast_to(value, (count,) + value.shape)
    return lax.all_to_all(copies, axes, 0, 0, tiled=True)


def local(teacher_hidden, teacher_head, student_hidden, student_head, target_ids):
    core = lax.axis_index("c")
    chips = lax.axis_size(WALK)
    stripes = teacher_head.shape[1]
    voc = teacher_head.shape[2]
    rows = teacher_hidden.shape[0]
    width = student_head.shape[0]
    base = lax.axis_index(TOK + VOC) * voc
    pair = [(0, 1), (1, 0)]

    partial = jnp.einsum("rd,dsv->srv", teacher_hidden, teacher_head, preferred_element_type=jnp.float32)
    words = encode(partial)
    words = words.reshape((2, 2, 2) + words.shape[1:]).transpose(2, 1, 0, 3, 4).reshape(words.shape)
    words = lax.all_to_all(words, STRIPES, 0, 0, tiled=True)

    plane = jnp.swapaxes(student_hidden, 0, 1).reshape(4, width)
    plane = everywhere(plane, ("yh", "yl", "xh", "xl"), 16).reshape(64, width)

    own = ring_gather(plane, "z")
    other = lax.ppermute(own, "c", pair)

    scalars = jnp.stack([core, base])
    ids = target_ids.T.astype(jnp.float32)
    own_scores, own_stats = student_half(0, scalars, own, student_head, ids)
    other_scores, other_stats = student_half(1, scalars, other, student_head, ids)
    own_stats, other_stats = own_stats[:4], other_stats[:4]
    stats = jnp.stack(
        [jnp.where(core == 0, own_stats, other_stats), jnp.where(core == 0, other_stats, own_stats)], axis=1
    ).reshape(4, 2 * rows)
    around = [stats] + [lax.ppermute(stats, "z", [(i, (i + j) % 4) for i in range(4)]) for j in (1, 2, 3)]
    stats = merge(jnp.stack(around)).reshape(4, 4, rows // 2)
    stats = lax.dynamic_index_in_dim(stats, lax.axis_index("z"), 1, False)
    stats = stats + 0.0 * words[0, 0, 0].astype(jnp.float32)
    stats = merge(jnp.stack([stats, lax.ppermute(stats, "c", pair)]))

    own_teacher, other_teacher, tile = teacher_sum(scalars, words, own_scores, other_scores)
    copies = chip_copies(scalars, tile, lax.ppermute(tile, "c", pair), stats, chips)
    hidden = jnp.concatenate([own, other], axis=0)
    copies, hidden = lax.optimization_barrier((copies, hidden))
    shares = lax.all_to_all(copies, EXCHANGE, 0, 0, tiled=True)
    own_grad, other_grad, objective = slopes(
        scalars, shares, ids, own_scores, other_scores, own_teacher, other_teacher
    )

    contract = (((1,), (1,)), ((), ()))
    give = lax.dot_general(other_grad, student_head, contract, preferred_element_type=jnp.float32)
    taken = lax.ppermute(give, "c", pair)
    keep = lax.dot_general(own_grad, student_head, contract, preferred_element_type=jnp.float32)
    grad = jnp.concatenate([own_grad, other_grad], axis=0)
    grad_head = lax.dot_general(
        hidden, grad, (((0,), (0,)), ((), ())), preferred_element_type=jnp.float32
    ).astype(jnp.bfloat16)
    objective = objective[:2].T

    share = (keep + taken).astype(jnp.bfloat16).reshape(chips, 4, width)
    share, grad_head, objective = lax.optimization_barrier((share, grad_head, objective))
    share = lax.all_to_all(share, WALK, 0, 0, tiled=True)
    grad_hidden = jnp.sum(share.astype(jnp.float32), axis=0).astype(jnp.bfloat16)
    grad_hidden = jnp.swapaxes(grad_hidden.reshape(2, 2, width), 0, 1)
    return objective, grad_hidden, grad_head


def solution(mesh):
    fine = Mesh(mesh.devices.reshape(SIZES), TOK + VOC)
    return jax.shard_map(
        local,
        mesh=fine,
        in_specs=(
            P(None, TOK),
            P(TOK, None, VOC),
            P(TOK + VOC, None, None),
            P(None, TOK + VOC),
            P(),
        ),
        out_specs=(P(), P(TOK + VOC, None, None), P(None, TOK + VOC)),
        check_vma=False,
    )
```

```python
import functools

import jax
import jax.numpy as jnp
from jax import lax
from jax.experimental import pallas as pl
from jax.experimental.pallas import tpu as pltpu
from jax.sharding import Mesh
from jax.sharding import PartitionSpec as P

TOK = ("xh", "xl", "yh")
VOC = ("yl", "z", "c")
SIZES = (2, 2, 2, 2, 4, 2)
GRANT = 14
STRIPES = ("yh", "xl", "xh")
WALK = ("z", "yh", "yl", "xh", "xl")
EXCHANGE = ("z", "yh", "xh", "yl", "xl")


def encode(partial):
    stripes, rows, width = partial.shape
    half = width // 2
    peak = jnp.maximum(jnp.max(jnp.abs(partial), axis=2), 1e-30)
    level = jnp.ceil(jnp.log2(peak) * 256.0)
    scale = jnp.exp2(-level / 256.0) * 32766.0
    code = jnp.clip(jnp.round(partial * scale[:, :, None]), -32767.0, 32767.0).astype(jnp.int32)
    words = (code[:, :, :half] << 16) | (code[:, :, half:] & 0xFFFF)
    tail = jnp.zeros((stripes, 8, half), jnp.int32).at[:, 0, :rows].set(level.astype(jnp.int32))
    return jnp.concatenate([words, tail], axis=1)


def row_of(place, core):
    head = (place >> 1) & 1
    row = ((place >> 2) & 3) * 64 + ((place >> 4) & 3) * 16 + (place >> 6) * 4 + core * 2 + (place & 1)
    return row, head


def teacher_kernel(core_ref, words_ref, mine_ref, theirs_ref, mine_out, theirs_out, tile_out, sum_ref):
    rows, width = sum_ref.shape
    senders = words_ref.shape[0]
    half = width // 2
    step = 32
    level = jnp.concatenate([words_ref[j, rows : rows + 1, :rows] for j in range(senders)], axis=0)
    scale = jnp.transpose(jnp.exp2(level.astype(jnp.float32) * (1.0 / 256.0)) * (0.5 / 32766.0))
    peaks, totals = [], []
    for at in range(0, rows, step):
        here = pl.ds(at, step)
        low = jnp.zeros((step, half), jnp.float32)
        high = jnp.zeros((step, half), jnp.float32)
        for j in range(senders):
            body = words_ref[j, here, :]
            by = scale[at : at + step, j : j + 1]
            high = high + (body >> 16).astype(jnp.float32) * by
            low = low + ((body << 16) >> 16).astype(jnp.float32) * by
        sum_ref[here, :half] = high
        sum_ref[here, half:] = low
        peak = jnp.maximum(jnp.max(high, axis=1, keepdims=True), jnp.max(low, axis=1, keepdims=True))
        total = jnp.sum(jnp.exp(high - peak), axis=1, keepdims=True)
        total = total + jnp.sum(jnp.exp(low - peak), axis=1, keepdims=True)
        peaks.append(peak)
        totals.append(total)
    peak = jnp.concatenate(peaks, axis=0)
    total = jnp.concatenate(totals, axis=0)
    lane = lax.broadcasted_iota(jnp.int32, (rows, rows), 1)
    place = lax.broadcasted_iota(jnp.int32, (rows, rows), 0)
    eye = lane == place
    first = sum_ref[...].astype(jnp.bfloat16)
    rest = sum_ref[...] - first.astype(jnp.float32)
    second = rest.astype(jnp.bfloat16)
    third = (rest - second.astype(jnp.float32)).astype(jnp.bfloat16)
    crosses = [jnp.zeros((1, rows), jnp.float32), jnp.zeros((1, rows), jnp.float32)]
    for side, scores, out in ((0, mine_ref, mine_out), (1, theirs_ref, theirs_out)):
        core = jnp.where(side == 0, core_ref[0], 1 - core_ref[0])
        row, head = row_of(place, core)
        chosen = lane == jnp.minimum(row + head, rows - 1)
        pick = jnp.where(chosen, 1.0, 0.0).astype(jnp.bfloat16)
        moved = jnp.dot(pick, first, preferred_element_type=jnp.float32)
        moved = moved + jnp.dot(pick, second, preferred_element_type=jnp.float32)
        out[...] = moved + jnp.dot(pick, third, preferred_element_type=jnp.float32)
        parts = []
        for at in range(0, rows, step):
            here = pl.ds(at, step)
            logits = out[here, :]
            weight = jnp.exp(logits - jnp.max(logits, axis=1, keepdims=True))
            parts.append(jnp.sum(weight * (logits - 0.5 * scores[here, :]), axis=1, keepdims=True))
        cross = jnp.concatenate(parts, axis=0)
        for k in (0, 1):
            inside = (lane == row + k) & (head == k)
            crosses[k] = crosses[k] + jnp.sum(jnp.where(inside, cross, 0.0), axis=0, keepdims=True)
    lines = [jnp.sum(jnp.where(eye, column, 0.0), axis=0, keepdims=True) for column in (peak, total)] + crosses
    edge = rows // 2
    tile_out[...] = jnp.concatenate([line[:, at : at + edge] for line in lines for at in (0, edge)], axis=0)


def chosen_id(ids_ref, place, row, head):
    lane = lax.broadcasted_iota(jnp.int32, place.shape, 1)
    ids = jnp.where(head == 0, ids_ref[0:1, :], ids_ref[1:2, :])
    return jnp.sum(jnp.where(lane == row, ids, 0.0), axis=1, keepdims=True)


def student_kernel(side, core_ref, hidden_ref, head_ref, ids_ref, scores_out, lines_out):
    rows, width = scores_out.shape
    step = 32
    for at in range(0, width, 256):
        scores_out[:, at : at + 256] = jnp.dot(
            hidden_ref[...], head_ref[:, at : at + 256], preferred_element_type=jnp.float32
        )
    lane = lax.broadcasted_iota(jnp.int32, (rows, rows), 1)
    place = lax.broadcasted_iota(jnp.int32, (rows, rows), 0)
    core = jnp.where(side == 0, core_ref[0], 1 - core_ref[0])
    row, head = row_of(place, core)
    ids = chosen_id(ids_ref, place, row, head)
    columns = (lax.broadcasted_iota(jnp.int32, (step, width), 1) + core_ref[1]).astype(jnp.float32)
    found = [[], [], [], []]
    for at in range(0, rows, step):
        scores = scores_out[at : at + step, :]
        peak = jnp.max(scores, axis=1, keepdims=True)
        power = jnp.exp((scores - peak) * 0.5)
        found[0].append(peak)
        found[1].append(jnp.sum(power * power, axis=1, keepdims=True))
        found[2].append(jnp.sum(power, axis=1, keepdims=True))
        found[3].append(jnp.sum(jnp.where(columns == ids[at : at + step], scores, 0.0), axis=1, keepdims=True))
    eye = lane == place
    lines = [jnp.sum(jnp.where(eye, jnp.concatenate(f, axis=0), 0.0), axis=0, keepdims=True) for f in found]
    lines_out[...] = jnp.concatenate(lines + [jnp.zeros((4, rows), jnp.float32)], axis=0)


def copy_kernel(core_ref, mine_ref, theirs_ref, stats_ref, copies_out):
    mine, theirs = mine_ref[...], theirs_ref[...]
    top = jnp.maximum(mine[0:2], theirs[0:2])
    both = [jnp.exp(a[0:2] - top) for a in (mine, theirs)]
    both = [jnp.concatenate([b, b, b, b], axis=0) for b in both]
    tile = mine * both[0] + theirs * both[1]
    tile = jnp.concatenate([top, tile[2:8]], axis=0)
    rest = jnp.concatenate([stats_ref[...], jnp.zeros_like(stats_ref)], axis=0)
    copies_out[:, 0:8, :] = jnp.broadcast_to(tile[None], copies_out[:, 0:8, :].shape)
    copies_out[:, 8:16, :] = jnp.broadcast_to(rest[None], copies_out[:, 8:16, :].shape)


def whole(shape):
    return pl.BlockSpec(shape, lambda *_: (0,) * len(shape), pipeline_mode=pl.Buffered(1))


def call(kernel, scalars, operands, results, grant, cost, scratch=()):
    return pl.pallas_call(
        kernel,
        out_shape=tuple(results),
        grid_spec=pltpu.PrefetchScalarGridSpec(
            num_scalar_prefetch=1,
            grid=(1,),
            in_specs=[whole(a.shape) for a in operands],
            out_specs=tuple(whole(a.shape) for a in results),
            scratch_shapes=scratch,
        ),
        compiler_params=pltpu.CompilerParams(vmem_limit_bytes=grant << 20),
        cost_estimate=pl.CostEstimate(flops=cost[0], bytes_accessed=cost[1], transcendentals=cost[2]),
    )(scalars, *operands)


def teacher_sum(scalars, words, mine, theirs):
    rows, width = mine.shape
    area = rows * width
    tile = jax.ShapeDtypeStruct((8, rows // 2), jnp.float32)
    half = jax.ShapeDtypeStruct(mine.shape, jnp.float32)
    scratch = [pltpu.VMEM((rows, width), jnp.float32)]
    operands = (words, mine, theirs)
    return call(teacher_kernel, scalars, operands, (half, half, tile), GRANT, (12 * rows * area, 40 * area, 3 * area), scratch)


def student_half(side, scalars, hidden, head, ids):
    rows, width = hidden.shape[0], head.shape[1]
    area = rows * width
    results = (jax.ShapeDtypeStruct((rows, width), jnp.float32), jax.ShapeDtypeStruct((8, rows), jnp.float32))
    cost = (2 * area * hidden.shape[1], 4 * area + 2 * head.size, area)
    return call(functools.partial(student_kernel, side), scalars, (hidden, head, ids), results, GRANT, cost)


def chip_copies(scalars, mine, theirs, stats, chips):
    copies = jax.ShapeDtypeStruct((chips, 16, mine.shape[1]), jnp.float32)
    return call(copy_kernel, scalars, (mine, theirs, stats), (copies,), GRANT, (mine.size, 4 * copies.size, mine.size))[0]


def slope_kernel(core_ref, shares_ref, ids_ref, mine_ref, theirs_ref, mine_t_ref, theirs_t_ref, mine_out, theirs_out, objective_out):
    devices = shares_ref.shape[0]
    rows, width = mine_ref.shape
    edge = rows // 2
    step = 32
    batch = 16
    four = lambda a: jnp.concatenate([a, a, a, a], axis=1)
    top = jnp.max(shares_ref[0:batch, 0:8, :], axis=0)
    for at in range(batch, devices, batch):
        top = jnp.maximum(top, jnp.max(shares_ref[at : at + batch, 0:8, :], axis=0))
    top = jnp.concatenate([top[0:2]] * 4, axis=0)
    sums = jnp.zeros((8, edge), jnp.float32)
    for at in range(0, devices, batch):
        part = shares_ref[at : at + batch, 0:8, :]
        sums = sums + jnp.sum(jnp.exp(four(part[:, 0:2]) - top[None]) * part, axis=0)
    line = lambda a: jnp.concatenate([a[0:1], a[1:2]], axis=1)
    t_total = sums[2:4]
    t_lse = line(top[0:2] + jnp.log(t_total))
    cross = [line(sums[4:6] / t_total), line(sums[6:8] / t_total)]

    ones, taus, targets = [], [], []
    quarter = devices // 4
    kind = lax.broadcasted_iota(jnp.int32, (batch, 8, edge), 1)
    for q in range(4):
        peak = jnp.max(shares_ref[q * quarter : (q + 1) * quarter, 8:16, :], axis=0)[0:1]
        total = jnp.zeros((8, edge), jnp.float32)
        for at in range(q * quarter, (q + 1) * quarter, batch):
            part = shares_ref[at : at + batch, 8:16, :]
            scale = jnp.exp(0.5 * (part[:, 0:1] - peak[None]))
            scale = jnp.broadcast_to(scale, part.shape)
            scale = jnp.where(kind == 1, scale * scale, jnp.where(kind == 2, scale, 1.0))
            total = total + jnp.sum(scale * part, axis=0)
        ones.append(peak + jnp.log(total[1:2]))
        taus.append(0.5 * peak + jnp.log(total[2:3]))
        targets.append(total[3:4])
    norms = jnp.transpose(jnp.concatenate(ones + taus + targets + targets, axis=0))

    lane = lax.broadcasted_iota(jnp.int32, (rows, rows), 1)
    place = lax.broadcasted_iota(jnp.int32, (rows, rows), 0)
    objective = [jnp.zeros((1, rows), jnp.float32), jnp.zeros((1, rows), jnp.float32)]
    base = core_ref[1]
    columns = (lax.broadcasted_iota(jnp.int32, (step, width), 1) + base).astype(jnp.float32)
    for side, scores, teacher, out in ((0, mine_ref, mine_t_ref, mine_out), (1, theirs_ref, theirs_t_ref, theirs_out)):
        first = (core_ref[0] == 0) == (side == 0)
        core = jnp.where(first, 0, 1)

        def column(n):
            low = jnp.concatenate([norms[:, n : n + 1], norms[:, n + 1 : n + 2]], axis=0)
            high = jnp.concatenate([norms[:, n + 2 : n + 3], norms[:, n + 3 : n + 4]], axis=0)
            return jnp.where(first, low, high)

        one, tau, target = column(0), column(4), column(8)
        row, head = row_of(place, core)
        chosen = lane == jnp.minimum(row + head, rows - 1)
        lse = jnp.sum(jnp.where(chosen, t_lse, 0.0), axis=1, keepdims=True)
        mixed = jnp.where(head == 0, cross[0], cross[1])
        mixed = jnp.sum(jnp.where(chosen, mixed, 0.0), axis=1, keepdims=True)
        weight = jnp.where((head[:, 0:1] == 1) & (row[:, 0:1] == rows - 1), 0.0, 1.0)
        loss = weight * (2.0 * (mixed - lse + tau) + 0.5 * (one - target))
        for k in (0, 1):
            inside = (lane == row) & (head == k)
            objective[k] = objective[k] + jnp.sum(jnp.where(inside, loss, 0.0), axis=0, keepdims=True)
        ids = chosen_id(ids_ref, place, row, head)
        for at in range(0, rows, step):
            here = pl.ds(at, step)
            part = slice(at, at + step)
            score = scores[here, :]
            grad = jnp.exp(0.5 * score - tau[part]) - jnp.exp(teacher[here, :] - lse[part])
            hit = jnp.where(columns == ids[part], 1.0, 0.0)
            grad = weight[part] * (grad + 0.5 * (jnp.exp(score - one[part]) - hit))
            out[here, :] = grad.astype(jnp.bfloat16)
    objective_out[...] = jnp.concatenate(objective + [jnp.zeros((6, rows), jnp.float32)], axis=0)


def slopes(scalars, *operands):
    half = jax.ShapeDtypeStruct(operands[2].shape, jnp.bfloat16)
    lines = jax.ShapeDtypeStruct((8, half.shape[0]), jnp.float32)
    area = operands[2].size
    return call(slope_kernel, scalars, operands, (half, half, lines), GRANT, (40 * area, 24 * area, 6 * area))


def merge(parts):
    peak = jnp.max(parts[:, 0], axis=0)
    scale = jnp.exp((parts[:, 0] - peak) * 0.5)
    return jnp.stack(
        [
            peak,
            jnp.sum(parts[:, 1] * (scale * scale), axis=0),
            jnp.sum(parts[:, 2] * scale, axis=0),
            jnp.sum(parts[:, 3], axis=0),
        ]
    )


def place_kernel(count, places_ref, *refs):
    blocks, out_ref, sems = refs[:count], refs[count], refs[count + 1]
    rows = blocks[0].shape[0]
    copies = []
    for i, block in enumerate(blocks):
        at = pl.multiple_of(places_ref[i] * rows, rows)
        copies.append(pltpu.make_async_copy(block, out_ref.at[pl.ds(at, rows), :], sems.at[i]))
    for copy in copies:
        copy.start()
    for copy in copies:
        copy.wait()


def place_blocks(places, *blocks):
    count = len(blocks)
    rows, width = blocks[0].shape
    return pl.pallas_call(
        functools.partial(place_kernel, count),
        out_shape=jax.ShapeDtypeStruct((count * rows, width), blocks[0].dtype),
        grid_spec=pltpu.PrefetchScalarGridSpec(
            num_scalar_prefetch=1,
            grid=(1,),
            in_specs=[pl.BlockSpec(memory_space=pl.ANY)] * count,
            out_specs=pl.BlockSpec(memory_space=pl.ANY),
            scratch_shapes=[pltpu.SemaphoreType.DMA((count,))],
        ),
        compiler_params=pltpu.CompilerParams(vmem_limit_bytes=2 << 20),
        cost_estimate=pl.CostEstimate(flops=0, bytes_accessed=2 * count * blocks[0].size * 2, transcendentals=0),
    )(places, *blocks)


def ring_gather(block, axis):
    size = lax.axis_size(axis)
    here = lax.axis_index(axis)
    blocks = [block]
    for step in range(1, size):
        blocks.append(lax.ppermute(block, axis, [(i, (i + step) % size) for i in range(size)]))
    return place_blocks((here + size - jnp.arange(size, dtype=jnp.int32)) % size, *blocks)


def everywhere(value, axes, count):
    copies = jnp.broadcast_to(value, (count,) + value.shape)
    return lax.all_to_all(copies, axes, 0, 0, tiled=True)


def local(teacher_hidden, teacher_head, student_hidden, student_head, target_ids):
    core = lax.axis_index("c")
    chips = lax.axis_size(WALK)
    stripes = teacher_head.shape[1]
    voc = teacher_head.shape[2]
    rows = teacher_hidden.shape[0]
    width = student_head.shape[0]
    base = lax.axis_index(TOK + VOC) * voc
    pair = [(0, 1), (1, 0)]

    partial = jnp.einsum("rd,dsv->srv", teacher_hidden, teacher_head, preferred_element_type=jnp.float32)
    words = encode(partial)
    words = words.reshape((2, 2, 2) + words.shape[1:]).transpose(2, 1, 0, 3, 4).reshape(words.shape)
    words = lax.all_to_all(words, STRIPES, 0, 0, tiled=True)

    plane = jnp.swapaxes(student_hidden, 0, 1).reshape(4, width)
    plane = everywhere(plane, ("yh", "yl", "xh", "xl"), 16).reshape(64, width)

    own = ring_gather(plane, "z")
    other = lax.ppermute(own, "c", pair)

    scalars = jnp.stack([core, base])
    ids = target_ids.T.astype(jnp.float32)
    own_scores, own_stats = student_half(0, scalars, own, student_head, ids)
    other_scores, other_stats = student_half(1, scalars, other, student_head, ids)
    own_stats, other_stats = own_stats[:4], other_stats[:4]
    stats = jnp.stack(
        [jnp.where(core == 0, own_stats, other_stats), jnp.where(core == 0, other_stats, own_stats)], axis=1
    ).reshape(4, 2 * rows)
    around = [stats] + [lax.ppermute(stats, "z", [(i, (i + j) % 4) for i in range(4)]) for j in (1, 2, 3)]
    stats = merge(jnp.stack(around)).reshape(4, 4, rows // 2)
    stats = lax.dynamic_index_in_dim(stats, lax.axis_index("z"), 1, False)
    stats = stats + 0.0 * words[0, 0, 0].astype(jnp.float32)
    stats = merge(jnp.stack([stats, lax.ppermute(stats, "c", pair)]))

    own_teacher, other_teacher, tile = teacher_sum(scalars, words, own_scores, other_scores)
    copies = chip_copies(scalars, tile, lax.ppermute(tile, "c", pair), stats, chips)
    hidden = place_blocks(jnp.arange(2, dtype=jnp.int32), own, other)
    copies, hidden = lax.optimization_barrier((copies, hidden))
    shares = lax.all_to_all(copies, EXCHANGE, 0, 0, tiled=True)
    own_grad, other_grad, objective = slopes(
        scalars, shares, ids, own_scores, other_scores, own_teacher, other_teacher
    )

    contract = (((1,), (1,)), ((), ()))
    give = lax.dot_general(other_grad, student_head, contract, preferred_element_type=jnp.float32)
    taken = lax.ppermute(give, "c", pair)
    keep = lax.dot_general(own_grad, student_head, contract, preferred_element_type=jnp.float32)
    grad = jnp.concatenate([own_grad, other_grad], axis=0)
    grad_head = lax.dot_general(
        hidden, grad, (((0,), (0,)), ((), ())), preferred_element_type=jnp.float32
    ).astype(jnp.bfloat16)
    objective = objective[:2].T

    share = (keep + taken).astype(jnp.bfloat16).reshape(chips, 4, width)
    share, grad_head, objective = lax.optimization_barrier((share, grad_head, objective))
    share = lax.all_to_all(share, WALK, 0, 0, tiled=True)
    grad_hidden = jnp.sum(share.astype(jnp.float32), axis=0).astype(jnp.bfloat16)
    grad_hidden = jnp.swapaxes(grad_hidden.reshape(2, 2, width), 0, 1)
    return objective, grad_hidden, grad_head


def solution(mesh):
    fine = Mesh(mesh.devices.reshape(SIZES), TOK + VOC)
    return jax.shard_map(
        local,
        mesh=fine,
        in_specs=(
            P(None, TOK),
            P(TOK, None, VOC),
            P(TOK + VOC, None, None),
            P(None, TOK + VOC),
            P(),
        ),
        out_specs=(P(), P(TOK + VOC, None, None), P(None, TOK + VOC)),
        check_vma=False,
    )
```

```python
import functools

import jax
import jax.numpy as jnp
from jax import lax
from jax.experimental import pallas as pl
from jax.experimental.pallas import tpu as pltpu
from jax.sharding import Mesh
from jax.sharding import PartitionSpec as P

TOK = ("xh", "xl", "yh")
VOC = ("yl", "z", "c")
SIZES = (2, 2, 2, 2, 4, 2)
GRANT = 14
STRIPES = ("yh", "xl", "xh")
WALK = ("z", "yh", "yl", "xh", "xl")
EXCHANGE = ("z", "yh", "xh", "yl", "xl")


def encode(partial):
    stripes, rows, width = partial.shape
    half = width // 2
    peak = jnp.maximum(jnp.max(jnp.abs(partial), axis=2), 1e-30)
    level = jnp.ceil(jnp.log2(peak) * 256.0)
    scale = jnp.exp2(-level / 256.0) * 32766.0
    code = jnp.clip(jnp.round(partial * scale[:, :, None]), -32767.0, 32767.0).astype(jnp.int32)
    words = (code[:, :, :half] << 16) | (code[:, :, half:] & 0xFFFF)
    tail = jnp.zeros((stripes, 8, half), jnp.int32).at[:, 0, :rows].set(level.astype(jnp.int32))
    return jnp.concatenate([words, tail], axis=1)


def row_of(place, core):
    head = (place >> 1) & 1
    row = ((place >> 2) & 3) * 64 + ((place >> 4) & 3) * 16 + (place >> 6) * 4 + core * 2 + (place & 1)
    return row, head


def teacher_kernel(core_ref, words_ref, mine_ref, theirs_ref, mine_out, theirs_out, tile_out, sum_ref):
    rows, width = sum_ref.shape
    senders = words_ref.shape[0]
    half = width // 2
    step = 32
    level = jnp.concatenate([words_ref[j, rows : rows + 1, :rows] for j in range(senders)], axis=0)
    scale = jnp.transpose(jnp.exp2(level.astype(jnp.float32) * (1.0 / 256.0)) * (0.5 / 32766.0))
    peaks, totals = [], []
    for at in range(0, rows, step):
        here = pl.ds(at, step)
        low = jnp.zeros((step, half), jnp.float32)
        high = jnp.zeros((step, half), jnp.float32)
        for j in range(senders):
            body = words_ref[j, here, :]
            by = scale[at : at + step, j : j + 1]
            high = high + (body >> 16).astype(jnp.float32) * by
            low = low + ((body << 16) >> 16).astype(jnp.float32) * by
        sum_ref[here, :half] = high
        sum_ref[here, half:] = low
        peak = jnp.maximum(jnp.max(high, axis=1, keepdims=True), jnp.max(low, axis=1, keepdims=True))
        total = jnp.sum(jnp.exp(high - peak), axis=1, keepdims=True)
        total = total + jnp.sum(jnp.exp(low - peak), axis=1, keepdims=True)
        peaks.append(peak)
        totals.append(total)
    peak = jnp.concatenate(peaks, axis=0)
    total = jnp.concatenate(totals, axis=0)
    lane = lax.broadcasted_iota(jnp.int32, (rows, rows), 1)
    place = lax.broadcasted_iota(jnp.int32, (rows, rows), 0)
    eye = lane == place
    first = sum_ref[...].astype(jnp.bfloat16)
    rest = sum_ref[...] - first.astype(jnp.float32)
    second = rest.astype(jnp.bfloat16)
    third = (rest - second.astype(jnp.float32)).astype(jnp.bfloat16)
    crosses = [jnp.zeros((1, rows), jnp.float32), jnp.zeros((1, rows), jnp.float32)]
    for side, scores, out in ((0, mine_ref, mine_out), (1, theirs_ref, theirs_out)):
        core = jnp.where(side == 0, core_ref[0], 1 - core_ref[0])
        row, head = row_of(place, core)
        chosen = lane == jnp.minimum(row + head, rows - 1)
        pick = jnp.where(chosen, 1.0, 0.0).astype(jnp.bfloat16)
        moved = jnp.dot(pick, first, preferred_element_type=jnp.float32)
        moved = moved + jnp.dot(pick, second, preferred_element_type=jnp.float32)
        out[...] = moved + jnp.dot(pick, third, preferred_element_type=jnp.float32)
        parts = []
        for at in range(0, rows, step):
            here = pl.ds(at, step)
            logits = out[here, :]
            weight = jnp.exp(logits - jnp.max(logits, axis=1, keepdims=True))
            parts.append(jnp.sum(weight * (logits - 0.5 * scores[here, :]), axis=1, keepdims=True))
        cross = jnp.concatenate(parts, axis=0)
        for k in (0, 1):
            inside = (lane == row + k) & (head == k)
            crosses[k] = crosses[k] + jnp.sum(jnp.where(inside, cross, 0.0), axis=0, keepdims=True)
    lines = [jnp.sum(jnp.where(eye, column, 0.0), axis=0, keepdims=True) for column in (peak, total)] + crosses
    edge = rows // 2
    tile_out[...] = jnp.concatenate([line[:, at : at + edge] for line in lines for at in (0, edge)], axis=0)


def chosen_id(ids_ref, place, row, head):
    lane = lax.broadcasted_iota(jnp.int32, place.shape, 1)
    ids = jnp.where(head == 0, ids_ref[0:1, :], ids_ref[1:2, :])
    return jnp.sum(jnp.where(lane == row, ids, 0.0), axis=1, keepdims=True)


def student_kernel(side, core_ref, hidden_ref, head_ref, ids_ref, scores_out, lines_out):
    rows, width = scores_out.shape
    step = 32
    for at in range(0, width, 256):
        scores_out[:, at : at + 256] = jnp.dot(
            hidden_ref[...], head_ref[:, at : at + 256], preferred_element_type=jnp.float32
        )
    lane = lax.broadcasted_iota(jnp.int32, (rows, rows), 1)
    place = lax.broadcasted_iota(jnp.int32, (rows, rows), 0)
    core = jnp.where(side == 0, core_ref[0], 1 - core_ref[0])
    row, head = row_of(place, core)
    ids = chosen_id(ids_ref, place, row, head)
    columns = (lax.broadcasted_iota(jnp.int32, (step, width), 1) + core_ref[1]).astype(jnp.float32)
    found = [[], [], [], []]
    for at in range(0, rows, step):
        scores = scores_out[at : at + step, :]
        peak = jnp.max(scores, axis=1, keepdims=True)
        power = jnp.exp((scores - peak) * 0.5)
        found[0].append(peak)
        found[1].append(jnp.sum(power * power, axis=1, keepdims=True))
        found[2].append(jnp.sum(power, axis=1, keepdims=True))
        found[3].append(jnp.sum(jnp.where(columns == ids[at : at + step], scores, 0.0), axis=1, keepdims=True))
    eye = lane == place
    lines = [jnp.sum(jnp.where(eye, jnp.concatenate(f, axis=0), 0.0), axis=0, keepdims=True) for f in found]
    lines_out[...] = jnp.concatenate(lines + [jnp.zeros((4, rows), jnp.float32)], axis=0)


def copy_kernel(core_ref, mine_ref, theirs_ref, stats_ref, copies_out):
    mine, theirs = mine_ref[...], theirs_ref[...]
    top = jnp.maximum(mine[0:2], theirs[0:2])
    both = [jnp.exp(a[0:2] - top) for a in (mine, theirs)]
    both = [jnp.concatenate([b, b, b, b], axis=0) for b in both]
    tile = mine * both[0] + theirs * both[1]
    tile = jnp.concatenate([top, tile[2:8]], axis=0)
    rest = jnp.concatenate([stats_ref[...], jnp.zeros_like(stats_ref)], axis=0)
    copies_out[:, 0:8, :] = jnp.broadcast_to(tile[None], copies_out[:, 0:8, :].shape)
    copies_out[:, 8:16, :] = jnp.broadcast_to(rest[None], copies_out[:, 8:16, :].shape)


def whole(shape):
    return pl.BlockSpec(shape, lambda *_: (0,) * len(shape), pipeline_mode=pl.Buffered(1))


def call(kernel, scalars, operands, results, grant, cost, scratch=()):
    return pl.pallas_call(
        kernel,
        out_shape=tuple(results),
        grid_spec=pltpu.PrefetchScalarGridSpec(
            num_scalar_prefetch=1,
            grid=(1,),
            in_specs=[whole(a.shape) for a in operands],
            out_specs=tuple(whole(a.shape) for a in results),
            scratch_shapes=scratch,
        ),
        compiler_params=pltpu.CompilerParams(vmem_limit_bytes=grant << 20),
        cost_estimate=pl.CostEstimate(flops=cost[0], bytes_accessed=cost[1], transcendentals=cost[2]),
    )(scalars, *operands)


def teacher_sum(scalars, words, mine, theirs):
    rows, width = mine.shape
    area = rows * width
    tile = jax.ShapeDtypeStruct((8, rows // 2), jnp.float32)
    half = jax.ShapeDtypeStruct(mine.shape, jnp.float32)
    scratch = [pltpu.VMEM((rows, width), jnp.float32)]
    operands = (words, mine, theirs)
    return call(teacher_kernel, scalars, operands, (half, half, tile), GRANT, (12 * rows * area, 40 * area, 3 * area), scratch)


def student_half(side, scalars, hidden, head, ids):
    rows, width = hidden.shape[0], head.shape[1]
    area = rows * width
    results = (jax.ShapeDtypeStruct((rows, width), jnp.float32), jax.ShapeDtypeStruct((8, rows), jnp.float32))
    cost = (2 * area * hidden.shape[1], 4 * area + 2 * head.size, area)
    return call(functools.partial(student_kernel, side), scalars, (hidden, head, ids), results, GRANT, cost)


def chip_copies(scalars, mine, theirs, stats, chips):
    copies = jax.ShapeDtypeStruct((chips, 16, mine.shape[1]), jnp.float32)
    return call(copy_kernel, scalars, (mine, theirs, stats), (copies,), GRANT, (mine.size, 4 * copies.size, mine.size))[0]


def slope_kernel(core_ref, shares_ref, ids_ref, mine_ref, theirs_ref, mine_t_ref, theirs_t_ref, mine_out, theirs_out, objective_out):
    devices = shares_ref.shape[0]
    rows, width = mine_ref.shape
    edge = rows // 2
    step = 32
    batch = 16
    four = lambda a: jnp.concatenate([a, a, a, a], axis=1)
    top = jnp.max(shares_ref[0:batch, 0:8, :], axis=0)
    for at in range(batch, devices, batch):
        top = jnp.maximum(top, jnp.max(shares_ref[at : at + batch, 0:8, :], axis=0))
    top = jnp.concatenate([top[0:2]] * 4, axis=0)
    sums = jnp.zeros((8, edge), jnp.float32)
    for at in range(0, devices, batch):
        part = shares_ref[at : at + batch, 0:8, :]
        sums = sums + jnp.sum(jnp.exp(four(part[:, 0:2]) - top[None]) * part, axis=0)
    line = lambda a: jnp.concatenate([a[0:1], a[1:2]], axis=1)
    t_total = sums[2:4]
    t_lse = line(top[0:2] + jnp.log(t_total))
    cross = [line(sums[4:6] / t_total), line(sums[6:8] / t_total)]

    ones, taus, targets = [], [], []
    quarter = devices // 4
    kind = lax.broadcasted_iota(jnp.int32, (batch, 8, edge), 1)
    for q in range(4):
        peak = jnp.max(shares_ref[q * quarter : (q + 1) * quarter, 8:16, :], axis=0)[0:1]
        total = jnp.zeros((8, edge), jnp.float32)
        for at in range(q * quarter, (q + 1) * quarter, batch):
            part = shares_ref[at : at + batch, 8:16, :]
            scale = jnp.exp(0.5 * (part[:, 0:1] - peak[None]))
            scale = jnp.broadcast_to(scale, part.shape)
            scale = jnp.where(kind == 1, scale * scale, jnp.where(kind == 2, scale, 1.0))
            total = total + jnp.sum(scale * part, axis=0)
        ones.append(peak + jnp.log(total[1:2]))
        taus.append(0.5 * peak + jnp.log(total[2:3]))
        targets.append(total[3:4])
    norms = jnp.transpose(jnp.concatenate(ones + taus + targets + targets, axis=0))

    lane = lax.broadcasted_iota(jnp.int32, (rows, rows), 1)
    place = lax.broadcasted_iota(jnp.int32, (rows, rows), 0)
    objective = [jnp.zeros((1, rows), jnp.float32), jnp.zeros((1, rows), jnp.float32)]
    base = core_ref[1]
    columns = (lax.broadcasted_iota(jnp.int32, (step, width), 1) + base).astype(jnp.float32)
    for side, scores, teacher, out in ((0, mine_ref, mine_t_ref, mine_out), (1, theirs_ref, theirs_t_ref, theirs_out)):
        first = (core_ref[0] == 0) == (side == 0)
        core = jnp.where(first, 0, 1)

        def column(n):
            low = jnp.concatenate([norms[:, n : n + 1], norms[:, n + 1 : n + 2]], axis=0)
            high = jnp.concatenate([norms[:, n + 2 : n + 3], norms[:, n + 3 : n + 4]], axis=0)
            return jnp.where(first, low, high)

        one, tau, target = column(0), column(4), column(8)
        row, head = row_of(place, core)
        chosen = lane == jnp.minimum(row + head, rows - 1)
        lse = jnp.sum(jnp.where(chosen, t_lse, 0.0), axis=1, keepdims=True)
        mixed = jnp.where(head == 0, cross[0], cross[1])
        mixed = jnp.sum(jnp.where(chosen, mixed, 0.0), axis=1, keepdims=True)
        weight = jnp.where((head[:, 0:1] == 1) & (row[:, 0:1] == rows - 1), 0.0, 1.0)
        loss = weight * (2.0 * (mixed - lse + tau) + 0.5 * (one - target))
        for k in (0, 1):
            inside = (lane == row) & (head == k)
            objective[k] = objective[k] + jnp.sum(jnp.where(inside, loss, 0.0), axis=0, keepdims=True)
        ids = chosen_id(ids_ref, place, row, head)
        for at in range(0, rows, step):
            here = pl.ds(at, step)
            part = slice(at, at + step)
            score = scores[here, :]
            grad = jnp.exp(0.5 * score - tau[part]) - jnp.exp(teacher[here, :] - lse[part])
            hit = jnp.where(columns == ids[part], 1.0, 0.0)
            grad = weight[part] * (grad + 0.5 * (jnp.exp(score - one[part]) - hit))
            out[here, :] = grad.astype(jnp.bfloat16)
    objective_out[...] = jnp.concatenate(objective + [jnp.zeros((6, rows), jnp.float32)], axis=0)


def slopes(scalars, *operands):
    half = jax.ShapeDtypeStruct(operands[2].shape, jnp.bfloat16)
    lines = jax.ShapeDtypeStruct((8, half.shape[0]), jnp.float32)
    area = operands[2].size
    return call(slope_kernel, scalars, operands, (half, half, lines), GRANT, (40 * area, 24 * area, 6 * area))


def merge(parts):
    peak = jnp.max(parts[:, 0], axis=0)
    scale = jnp.exp((parts[:, 0] - peak) * 0.5)
    return jnp.stack(
        [
            peak,
            jnp.sum(parts[:, 1] * (scale * scale), axis=0),
            jnp.sum(parts[:, 2] * scale, axis=0),
            jnp.sum(parts[:, 3], axis=0),
        ]
    )


def place_kernel(count, places_ref, *refs):
    blocks, out_ref = refs[:count], refs[count]
    rows = blocks[0].shape[0]
    for i, block in enumerate(blocks):
        at = pl.multiple_of(places_ref[i] * rows, rows)
        out_ref[pl.ds(at, rows), :] = block[...]


def place_blocks(places, *blocks):
    count = len(blocks)
    rows, width = blocks[0].shape
    result = jax.ShapeDtypeStruct((count * rows, width), blocks[0].dtype)
    cost = (0, 4 * result.size, 0)
    return call(functools.partial(place_kernel, count), places, blocks, (result,), GRANT, cost)[0]


def ring_gather(block, axis):
    size = lax.axis_size(axis)
    here = lax.axis_index(axis)
    blocks = [block]
    for step in range(1, size):
        blocks.append(lax.ppermute(block, axis, [(i, (i + step) % size) for i in range(size)]))
    return place_blocks((here + size - jnp.arange(size, dtype=jnp.int32)) % size, *blocks)


def everywhere(value, axes, count):
    copies = jnp.broadcast_to(value, (count,) + value.shape)
    return lax.all_to_all(copies, axes, 0, 0, tiled=True)


def local(teacher_hidden, teacher_head, student_hidden, student_head, target_ids):
    core = lax.axis_index("c")
    chips = lax.axis_size(WALK)
    stripes = teacher_head.shape[1]
    voc = teacher_head.shape[2]
    rows = teacher_hidden.shape[0]
    width = student_head.shape[0]
    base = lax.axis_index(TOK + VOC) * voc
    pair = [(0, 1), (1, 0)]

    partial = jnp.einsum("rd,dsv->srv", teacher_hidden, teacher_head, preferred_element_type=jnp.float32)
    words = encode(partial)
    words = words.reshape((2, 2, 2) + words.shape[1:]).transpose(2, 1, 0, 3, 4).reshape(words.shape)
    words = lax.all_to_all(words, STRIPES, 0, 0, tiled=True)

    plane = jnp.swapaxes(student_hidden, 0, 1).reshape(4, width)
    plane = everywhere(plane, ("yh", "yl", "xh", "xl"), 16).reshape(64, width)

    own = ring_gather(plane, "z")
    other = lax.ppermute(own, "c", pair)

    scalars = jnp.stack([core, base])
    ids = target_ids.T.astype(jnp.float32)
    own_scores, own_stats = student_half(0, scalars, own, student_head, ids)
    other_scores, other_stats = student_half(1, scalars, other, student_head, ids)
    own_stats, other_stats = own_stats[:4], other_stats[:4]
    stats = jnp.stack(
        [jnp.where(core == 0, own_stats, other_stats), jnp.where(core == 0, other_stats, own_stats)], axis=1
    ).reshape(4, 2 * rows)
    around = [stats] + [lax.ppermute(stats, "z", [(i, (i + j) % 4) for i in range(4)]) for j in (1, 2, 3)]
    stats = merge(jnp.stack(around)).reshape(4, 4, rows // 2)
    stats = lax.dynamic_index_in_dim(stats, lax.axis_index("z"), 1, False)
    stats = stats + 0.0 * words[0, 0, 0].astype(jnp.float32)
    stats = merge(jnp.stack([stats, lax.ppermute(stats, "c", pair)]))

    own_teacher, other_teacher, tile = teacher_sum(scalars, words, own_scores, other_scores)
    copies = chip_copies(scalars, tile, lax.ppermute(tile, "c", pair), stats, chips)
    hidden = place_blocks(jnp.arange(2, dtype=jnp.int32), own, other)
    copies, hidden = lax.optimization_barrier((copies, hidden))
    shares = lax.all_to_all(copies, EXCHANGE, 0, 0, tiled=True)
    own_grad, other_grad, objective = slopes(
        scalars, shares, ids, own_scores, other_scores, own_teacher, other_teacher
    )

    contract = (((1,), (1,)), ((), ()))
    give = lax.dot_general(other_grad, student_head, contract, preferred_element_type=jnp.float32)
    taken = lax.ppermute(give, "c", pair)
    keep = lax.dot_general(own_grad, student_head, contract, preferred_element_type=jnp.float32)
    grad = jnp.concatenate([own_grad, other_grad], axis=0)
    grad_head = lax.dot_general(
        hidden, grad, (((0,), (0,)), ((), ())), preferred_element_type=jnp.float32
    ).astype(jnp.bfloat16)
    objective = objective[:2].T

    share = (keep + taken).astype(jnp.bfloat16).reshape(chips, 4, width)
    share, grad_head, objective = lax.optimization_barrier((share, grad_head, objective))
    share = lax.all_to_all(share, WALK, 0, 0, tiled=True)
    grad_hidden = jnp.sum(share.astype(jnp.float32), axis=0).astype(jnp.bfloat16)
    grad_hidden = jnp.swapaxes(grad_hidden.reshape(2, 2, width), 0, 1)
    return objective, grad_hidden, grad_head


def solution(mesh):
    fine = Mesh(mesh.devices.reshape(SIZES), TOK + VOC)
    return jax.shard_map(
        local,
        mesh=fine,
        in_specs=(
            P(None, TOK),
            P(TOK, None, VOC),
            P(TOK + VOC, None, None),
            P(None, TOK + VOC),
            P(),
        ),
        out_specs=(P(), P(TOK + VOC, None, None), P(None, TOK + VOC)),
        check_vma=False,
    )
```

```python
import functools

import jax
import jax.numpy as jnp
from jax import lax
from jax.experimental import pallas as pl
from jax.experimental.pallas import tpu as pltpu
from jax.sharding import Mesh
from jax.sharding import PartitionSpec as P

TOK = ("xh", "xl", "yh")
VOC = ("yl", "z", "c")
SIZES = (2, 2, 2, 2, 4, 2)
GRANT = 14
STRIPES = ("yh", "xl", "xh")
WALK = ("z", "yh", "yl", "xh", "xl")
EXCHANGE = ("z", "yh", "xh", "yl", "xl")


def encode(partial):
    stripes, rows, width = partial.shape
    half = width // 2
    peak = jnp.maximum(jnp.max(jnp.abs(partial), axis=2), 1e-30)
    level = jnp.ceil(jnp.log2(peak) * 256.0)
    scale = jnp.exp2(-level / 256.0) * 32766.0
    code = jnp.clip(jnp.round(partial * scale[:, :, None]), -32767.0, 32767.0).astype(jnp.int32)
    words = (code[:, :, :half] << 16) | (code[:, :, half:] & 0xFFFF)
    tail = jnp.zeros((stripes, 8, half), jnp.int32).at[:, 0, :rows].set(level.astype(jnp.int32))
    return jnp.concatenate([words, tail], axis=1)


def row_of(place, core):
    head = (place >> 1) & 1
    row = ((place >> 2) & 3) * 64 + ((place >> 4) & 3) * 16 + (place >> 6) * 4 + core * 2 + (place & 1)
    return row, head


def teacher_kernel(core_ref, words_ref, mine_ref, theirs_ref, mine_out, theirs_out, tile_out, sum_ref):
    rows, width = sum_ref.shape
    senders = words_ref.shape[0]
    half = width // 2
    step = 32
    level = jnp.concatenate([words_ref[j, rows : rows + 1, :rows] for j in range(senders)], axis=0)
    scale = jnp.transpose(jnp.exp2(level.astype(jnp.float32) * (1.0 / 256.0)) * (0.5 / 32766.0))
    peaks, totals = [], []
    for at in range(0, rows, step):
        here = pl.ds(at, step)
        low = jnp.zeros((step, half), jnp.float32)
        high = jnp.zeros((step, half), jnp.float32)
        for j in range(senders):
            body = words_ref[j, here, :]
            by = scale[at : at + step, j : j + 1]
            high = high + (body >> 16).astype(jnp.float32) * by
            low = low + ((body << 16) >> 16).astype(jnp.float32) * by
        sum_ref[here, :half] = high
        sum_ref[here, half:] = low
        peak = jnp.maximum(jnp.max(high, axis=1, keepdims=True), jnp.max(low, axis=1, keepdims=True))
        total = jnp.sum(jnp.exp(high - peak), axis=1, keepdims=True)
        total = total + jnp.sum(jnp.exp(low - peak), axis=1, keepdims=True)
        peaks.append(peak)
        totals.append(total)
    peak = jnp.concatenate(peaks, axis=0)
    total = jnp.concatenate(totals, axis=0)
    lane = lax.broadcasted_iota(jnp.int32, (rows, rows), 1)
    place = lax.broadcasted_iota(jnp.int32, (rows, rows), 0)
    eye = lane == place
    first = sum_ref[...].astype(jnp.bfloat16)
    rest = sum_ref[...] - first.astype(jnp.float32)
    second = rest.astype(jnp.bfloat16)
    third = (rest - second.astype(jnp.float32)).astype(jnp.bfloat16)
    crosses = [jnp.zeros((1, rows), jnp.float32), jnp.zeros((1, rows), jnp.float32)]
    for side, scores, out in ((0, mine_ref, mine_out), (1, theirs_ref, theirs_out)):
        core = jnp.where(side == 0, core_ref[0], 1 - core_ref[0])
        row, head = row_of(place, core)
        chosen = lane == jnp.minimum(row + head, rows - 1)
        pick = jnp.where(chosen, 1.0, 0.0).astype(jnp.bfloat16)
        moved = jnp.dot(pick, first, preferred_element_type=jnp.float32)
        moved = moved + jnp.dot(pick, second, preferred_element_type=jnp.float32)
        out[...] = moved + jnp.dot(pick, third, preferred_element_type=jnp.float32)
        parts = []
        for at in range(0, rows, step):
            here = pl.ds(at, step)
            logits = out[here, :]
            weight = jnp.exp(logits - jnp.max(logits, axis=1, keepdims=True))
            parts.append(jnp.sum(weight * (logits - 0.5 * scores[here, :]), axis=1, keepdims=True))
        cross = jnp.concatenate(parts, axis=0)
        for k in (0, 1):
            inside = (lane == row + k) & (head == k)
            crosses[k] = crosses[k] + jnp.sum(jnp.where(inside, cross, 0.0), axis=0, keepdims=True)
    lines = [jnp.sum(jnp.where(eye, column, 0.0), axis=0, keepdims=True) for column in (peak, total)] + crosses
    edge = rows // 2
    tile_out[...] = jnp.concatenate([line[:, at : at + edge] for line in lines for at in (0, edge)], axis=0)


def chosen_id(ids_ref, place, row, head):
    lane = lax.broadcasted_iota(jnp.int32, place.shape, 1)
    ids = jnp.where(head == 0, ids_ref[0:1, :], ids_ref[1:2, :])
    return jnp.sum(jnp.where(lane == row, ids, 0.0), axis=1, keepdims=True)


def student_kernel(side, core_ref, hidden_ref, head_ref, ids_ref, scores_out, lines_out):
    rows, width = scores_out.shape
    step = 32
    for at in range(0, width, 256):
        scores_out[:, at : at + 256] = jnp.dot(
            hidden_ref[...], head_ref[:, at : at + 256], preferred_element_type=jnp.float32
        )
    lane = lax.broadcasted_iota(jnp.int32, (rows, rows), 1)
    place = lax.broadcasted_iota(jnp.int32, (rows, rows), 0)
    core = jnp.where(side == 0, core_ref[0], 1 - core_ref[0])
    row, head = row_of(place, core)
    ids = chosen_id(ids_ref, place, row, head)
    columns = (lax.broadcasted_iota(jnp.int32, (step, width), 1) + core_ref[1]).astype(jnp.float32)
    found = [[], [], [], []]
    for at in range(0, rows, step):
        scores = scores_out[at : at + step, :]
        peak = jnp.max(scores, axis=1, keepdims=True)
        power = jnp.exp((scores - peak) * 0.5)
        found[0].append(peak)
        found[1].append(jnp.sum(power * power, axis=1, keepdims=True))
        found[2].append(jnp.sum(power, axis=1, keepdims=True))
        found[3].append(jnp.sum(jnp.where(columns == ids[at : at + step], scores, 0.0), axis=1, keepdims=True))
    eye = lane == place
    lines = [jnp.sum(jnp.where(eye, jnp.concatenate(f, axis=0), 0.0), axis=0, keepdims=True) for f in found]
    lines_out[...] = jnp.concatenate(lines + [jnp.zeros((4, rows), jnp.float32)], axis=0)


def copy_kernel(core_ref, mine_ref, theirs_ref, stats_ref, copies_out):
    mine, theirs = mine_ref[...], theirs_ref[...]
    top = jnp.maximum(mine[0:2], theirs[0:2])
    both = [jnp.exp(a[0:2] - top) for a in (mine, theirs)]
    both = [jnp.concatenate([b, b, b, b], axis=0) for b in both]
    tile = mine * both[0] + theirs * both[1]
    tile = jnp.concatenate([top, tile[2:8]], axis=0)
    rest = jnp.concatenate([stats_ref[...], jnp.zeros_like(stats_ref)], axis=0)
    copies_out[:, 0:8, :] = jnp.broadcast_to(tile[None], copies_out[:, 0:8, :].shape)
    copies_out[:, 8:16, :] = jnp.broadcast_to(rest[None], copies_out[:, 8:16, :].shape)


def whole(shape):
    return pl.BlockSpec(shape, lambda *_: (0,) * len(shape), pipeline_mode=pl.Buffered(1))


def call(kernel, scalars, operands, results, grant, cost, scratch=()):
    return pl.pallas_call(
        kernel,
        out_shape=tuple(results),
        grid_spec=pltpu.PrefetchScalarGridSpec(
            num_scalar_prefetch=1,
            grid=(1,),
            in_specs=[whole(a.shape) for a in operands],
            out_specs=tuple(whole(a.shape) for a in results),
            scratch_shapes=scratch,
        ),
        compiler_params=pltpu.CompilerParams(vmem_limit_bytes=grant << 20),
        cost_estimate=pl.CostEstimate(flops=cost[0], bytes_accessed=cost[1], transcendentals=cost[2]),
    )(scalars, *operands)


def teacher_sum(scalars, words, mine, theirs):
    rows, width = mine.shape
    area = rows * width
    tile = jax.ShapeDtypeStruct((8, rows // 2), jnp.float32)
    half = jax.ShapeDtypeStruct(mine.shape, jnp.float32)
    scratch = [pltpu.VMEM((rows, width), jnp.float32)]
    operands = (words, mine, theirs)
    return call(teacher_kernel, scalars, operands, (half, half, tile), GRANT, (12 * rows * area, 40 * area, 3 * area), scratch)


def student_half(side, scalars, hidden, head, ids):
    rows, width = hidden.shape[0], head.shape[1]
    area = rows * width
    results = (jax.ShapeDtypeStruct((rows, width), jnp.float32), jax.ShapeDtypeStruct((8, rows), jnp.float32))
    cost = (2 * area * hidden.shape[1], 4 * area + 2 * head.size, area)
    return call(functools.partial(student_kernel, side), scalars, (hidden, head, ids), results, GRANT, cost)


def chip_copies(scalars, mine, theirs, stats, chips):
    copies = jax.ShapeDtypeStruct((chips, 16, mine.shape[1]), jnp.float32)
    return call(copy_kernel, scalars, (mine, theirs, stats), (copies,), GRANT, (mine.size, 4 * copies.size, mine.size))[0]


def slope_kernel(core_ref, shares_ref, ids_ref, mine_ref, theirs_ref, mine_t_ref, theirs_t_ref, mine_out, theirs_out, objective_out):
    devices = shares_ref.shape[0]
    rows, width = mine_ref.shape
    edge = rows // 2
    step = 32
    batch = 16
    four = lambda a: jnp.concatenate([a, a, a, a], axis=1)
    top = jnp.max(shares_ref[0:batch, 0:8, :], axis=0)
    for at in range(batch, devices, batch):
        top = jnp.maximum(top, jnp.max(shares_ref[at : at + batch, 0:8, :], axis=0))
    top = jnp.concatenate([top[0:2]] * 4, axis=0)
    sums = jnp.zeros((8, edge), jnp.float32)
    for at in range(0, devices, batch):
        part = shares_ref[at : at + batch, 0:8, :]
        sums = sums + jnp.sum(jnp.exp(four(part[:, 0:2]) - top[None]) * part, axis=0)
    line = lambda a: jnp.concatenate([a[0:1], a[1:2]], axis=1)
    t_total = sums[2:4]
    t_lse = line(top[0:2] + jnp.log(t_total))
    cross = [line(sums[4:6] / t_total), line(sums[6:8] / t_total)]

    ones, taus, targets = [], [], []
    quarter = devices // 4
    kind = lax.broadcasted_iota(jnp.int32, (batch, 8, edge), 1)
    for q in range(4):
        peak = jnp.max(shares_ref[q * quarter : (q + 1) * quarter, 8:16, :], axis=0)[0:1]
        total = jnp.zeros((8, edge), jnp.float32)
        for at in range(q * quarter, (q + 1) * quarter, batch):
            part = shares_ref[at : at + batch, 8:16, :]
            scale = jnp.exp(0.5 * (part[:, 0:1] - peak[None]))
            scale = jnp.broadcast_to(scale, part.shape)
            scale = jnp.where(kind == 1, scale * scale, jnp.where(kind == 2, scale, 1.0))
            total = total + jnp.sum(scale * part, axis=0)
        ones.append(peak + jnp.log(total[1:2]))
        taus.append(0.5 * peak + jnp.log(total[2:3]))
        targets.append(total[3:4])
    norms = jnp.transpose(jnp.concatenate(ones + taus + targets + targets, axis=0))

    lane = lax.broadcasted_iota(jnp.int32, (rows, rows), 1)
    place = lax.broadcasted_iota(jnp.int32, (rows, rows), 0)
    objective = [jnp.zeros((1, rows), jnp.float32), jnp.zeros((1, rows), jnp.float32)]
    base = core_ref[1]
    columns = (lax.broadcasted_iota(jnp.int32, (step, width), 1) + base).astype(jnp.float32)
    for side, scores, teacher, out in ((0, mine_ref, mine_t_ref, mine_out), (1, theirs_ref, theirs_t_ref, theirs_out)):
        first = (core_ref[0] == 0) == (side == 0)
        core = jnp.where(first, 0, 1)

        def column(n):
            low = jnp.concatenate([norms[:, n : n + 1], norms[:, n + 1 : n + 2]], axis=0)
            high = jnp.concatenate([norms[:, n + 2 : n + 3], norms[:, n + 3 : n + 4]], axis=0)
            return jnp.where(first, low, high)

        one, tau, target = column(0), column(4), column(8)
        row, head = row_of(place, core)
        chosen = lane == jnp.minimum(row + head, rows - 1)
        lse = jnp.sum(jnp.where(chosen, t_lse, 0.0), axis=1, keepdims=True)
        mixed = jnp.where(head == 0, cross[0], cross[1])
        mixed = jnp.sum(jnp.where(chosen, mixed, 0.0), axis=1, keepdims=True)
        weight = jnp.where((head[:, 0:1] == 1) & (row[:, 0:1] == rows - 1), 0.0, 1.0)
        loss = weight * (2.0 * (mixed - lse + tau) + 0.5 * (one - target))
        for k in (0, 1):
            inside = (lane == row) & (head == k)
            objective[k] = objective[k] + jnp.sum(jnp.where(inside, loss, 0.0), axis=0, keepdims=True)
        ids = chosen_id(ids_ref, place, row, head)
        for at in range(0, rows, step):
            here = pl.ds(at, step)
            part = slice(at, at + step)
            score = scores[here, :]
            grad = jnp.exp(0.5 * score - tau[part]) - jnp.exp(teacher[here, :] - lse[part])
            hit = jnp.where(columns == ids[part], 1.0, 0.0)
            grad = weight[part] * (grad + 0.5 * (jnp.exp(score - one[part]) - hit))
            out[here, :] = grad.astype(jnp.bfloat16)
    objective_out[...] = jnp.concatenate(objective + [jnp.zeros((6, rows), jnp.float32)], axis=0)


def slopes(scalars, *operands):
    half = jax.ShapeDtypeStruct(operands[2].shape, jnp.bfloat16)
    lines = jax.ShapeDtypeStruct((8, half.shape[0]), jnp.float32)
    area = operands[2].size
    return call(slope_kernel, scalars, operands, (half, half, lines), GRANT, (40 * area, 24 * area, 6 * area))


def merge(parts):
    peak = jnp.max(parts[:, 0], axis=0)
    scale = jnp.exp((parts[:, 0] - peak) * 0.5)
    return jnp.stack(
        [
            peak,
            jnp.sum(parts[:, 1] * (scale * scale), axis=0),
            jnp.sum(parts[:, 2] * scale, axis=0),
            jnp.sum(parts[:, 3], axis=0),
        ]
    )


def place_kernel(count, places_ref, *refs):
    blocks, out_ref = refs[:count], refs[count]
    rows = blocks[0].shape[0]
    for i, block in enumerate(blocks):
        at = pl.multiple_of(places_ref[i] * rows, rows)
        out_ref[pl.ds(at, rows), :] = block[...]


def place_blocks(places, *blocks):
    count = len(blocks)
    rows, width = blocks[0].shape
    result = jax.ShapeDtypeStruct((count * rows, width), blocks[0].dtype)
    cost = (0, 4 * result.size, 0)
    return call(functools.partial(place_kernel, count), places, blocks, (result,), GRANT, cost)[0]


def ring_gather(block, axis):
    size = lax.axis_size(axis)
    here = lax.axis_index(axis)
    blocks = [block]
    for step in range(1, size):
        blocks.append(lax.ppermute(block, axis, [(i, (i + step) % size) for i in range(size)]))
    return place_blocks((here + size - jnp.arange(size, dtype=jnp.int32)) % size, *blocks)


def everywhere(value, axes, count):
    copies = jnp.broadcast_to(value, (count,) + value.shape)
    return lax.all_to_all(copies, axes, 0, 0, tiled=True)


def local(teacher_hidden, teacher_head, student_hidden, student_head, target_ids):
    core = lax.axis_index("c")
    chips = lax.axis_size(WALK)
    stripes = teacher_head.shape[1]
    voc = teacher_head.shape[2]
    rows = teacher_hidden.shape[0]
    width = student_head.shape[0]
    base = lax.axis_index(TOK + VOC) * voc
    pair = [(0, 1), (1, 0)]

    partial = jnp.einsum("rd,dsv->srv", teacher_hidden, teacher_head, preferred_element_type=jnp.float32)
    words = encode(partial)
    words = words.reshape((2, 2, 2) + words.shape[1:]).transpose(2, 1, 0, 3, 4).reshape(words.shape)
    words = lax.all_to_all(words, STRIPES, 0, 0, tiled=True)

    plane = jnp.swapaxes(student_hidden, 0, 1).reshape(4, width)
    plane = everywhere(plane, ("yh", "yl", "xh", "xl"), 16).reshape(64, width)

    own = ring_gather(plane, "z")
    other = lax.ppermute(own, "c", pair)

    scalars = jnp.stack([core, base])
    ids = target_ids.T.astype(jnp.float32)
    own_scores, own_stats = student_half(0, scalars, own, student_head, ids)
    other_scores, other_stats = student_half(1, scalars, other, student_head, ids)
    own_stats, other_stats = own_stats[:4], other_stats[:4]
    stats = jnp.stack(
        [jnp.where(core == 0, own_stats, other_stats), jnp.where(core == 0, other_stats, own_stats)], axis=1
    ).reshape(4, 2 * rows)
    around = [stats] + [lax.ppermute(stats, "z", [(i, (i + j) % 4) for i in range(4)]) for j in (1, 2, 3)]
    stats = merge(jnp.stack(around)).reshape(4, 4, rows // 2)
    stats = lax.dynamic_index_in_dim(stats, lax.axis_index("z"), 1, False)
    stats = stats + 0.0 * words[0, 0, 0].astype(jnp.float32)
    stats = merge(jnp.stack([stats, lax.ppermute(stats, "c", pair)]))

    own_teacher, other_teacher, tile = teacher_sum(scalars, words, own_scores, other_scores)
    copies = chip_copies(scalars, tile, lax.ppermute(tile, "c", pair), stats, chips)
    shares = lax.all_to_all(copies, EXCHANGE, 0, 0, tiled=True)
    own_grad, other_grad, objective = slopes(
        scalars, shares, ids, own_scores, other_scores, own_teacher, other_teacher
    )

    contract = (((1,), (1,)), ((), ()))
    give = lax.dot_general(other_grad, student_head, contract, preferred_element_type=jnp.float32)
    taken = lax.ppermute(give, "c", pair)
    keep = lax.dot_general(own_grad, student_head, contract, preferred_element_type=jnp.float32)
    grad = jnp.concatenate([own_grad, other_grad], axis=0)
    late = (jnp.abs(own_grad[0, 0].astype(jnp.float32)) > 3e38).astype(jnp.int32)
    hidden = place_blocks(jnp.arange(2, dtype=jnp.int32) + late, own, other)
    grad_head = lax.dot_general(
        hidden, grad, (((0,), (0,)), ((), ())), preferred_element_type=jnp.float32
    ).astype(jnp.bfloat16)
    objective = objective[:2].T

    share = (keep + taken).astype(jnp.bfloat16).reshape(chips, 4, width)
    share, grad_head, objective = lax.optimization_barrier((share, grad_head, objective))
    share = lax.all_to_all(share, WALK, 0, 0, tiled=True)
    grad_hidden = jnp.sum(share.astype(jnp.float32), axis=0).astype(jnp.bfloat16)
    grad_hidden = jnp.swapaxes(grad_hidden.reshape(2, 2, width), 0, 1)
    return objective, grad_hidden, grad_head


def solution(mesh):
    fine = Mesh(mesh.devices.reshape(SIZES), TOK + VOC)
    return jax.shard_map(
        local,
        mesh=fine,
        in_specs=(
            P(None, TOK),
            P(TOK, None, VOC),
            P(TOK + VOC, None, None),
            P(None, TOK + VOC),
            P(),
        ),
        out_specs=(P(), P(TOK + VOC, None, None), P(None, TOK + VOC)),
        check_vma=False,
    )
```

```python
import functools

import jax
import jax.numpy as jnp
from jax import lax
from jax.experimental import pallas as pl
from jax.experimental.pallas import tpu as pltpu
from jax.sharding import Mesh
from jax.sharding import PartitionSpec as P

TOK = ("xh", "xl", "yh")
VOC = ("yl", "z", "c")
SIZES = (2, 2, 2, 2, 4, 2)
GRANT = 14
STRIPES = ("yh", "xl", "xh")
WALK = ("z", "yh", "yl", "xh", "xl")
EXCHANGE = ("z", "yh", "xh", "yl", "xl")


def encode(partial):
    stripes, rows, width = partial.shape
    half = width // 2
    peak = jnp.maximum(jnp.max(jnp.abs(partial), axis=2), 1e-30)
    level = jnp.ceil(jnp.log2(peak) * 256.0)
    scale = jnp.exp2(-level / 256.0) * 32766.0
    code = jnp.clip(jnp.round(partial * scale[:, :, None]), -32767.0, 32767.0).astype(jnp.int32)
    words = (code[:, :, :half] << 16) | (code[:, :, half:] & 0xFFFF)
    tail = jnp.zeros((stripes, 8, half), jnp.int32).at[:, 0, :rows].set(level.astype(jnp.int32))
    return jnp.concatenate([words, tail], axis=1)


def row_of(place, core):
    head = (place >> 1) & 1
    row = ((place >> 2) & 3) * 64 + ((place >> 4) & 3) * 16 + (place >> 6) * 4 + core * 2 + (place & 1)
    return row, head


def teacher_kernel(core_ref, words_ref, mine_ref, theirs_ref, mine_out, theirs_out, tile_out, sum_ref):
    rows, width = sum_ref.shape
    senders = words_ref.shape[0]
    half = width // 2
    step = 32
    level = jnp.concatenate([words_ref[j, rows : rows + 1, :rows] for j in range(senders)], axis=0)
    scale = jnp.transpose(jnp.exp2(level.astype(jnp.float32) * (1.0 / 256.0)) * (0.5 / 32766.0))
    peaks, totals = [], []
    for at in range(0, rows, step):
        here = pl.ds(at, step)
        low = jnp.zeros((step, half), jnp.float32)
        high = jnp.zeros((step, half), jnp.float32)
        for j in range(senders):
            body = words_ref[j, here, :]
            by = scale[at : at + step, j : j + 1]
            high = high + (body >> 16).astype(jnp.float32) * by
            low = low + ((body << 16) >> 16).astype(jnp.float32) * by
        sum_ref[here, :half] = high
        sum_ref[here, half:] = low
        peak = jnp.maximum(jnp.max(high, axis=1, keepdims=True), jnp.max(low, axis=1, keepdims=True))
        total = jnp.sum(jnp.exp(high - peak), axis=1, keepdims=True)
        total = total + jnp.sum(jnp.exp(low - peak), axis=1, keepdims=True)
        peaks.append(peak)
        totals.append(total)
    peak = jnp.concatenate(peaks, axis=0)
    total = jnp.concatenate(totals, axis=0)
    lane = lax.broadcasted_iota(jnp.int32, (rows, rows), 1)
    place = lax.broadcasted_iota(jnp.int32, (rows, rows), 0)
    eye = lane == place
    first = sum_ref[...].astype(jnp.bfloat16)
    rest = sum_ref[...] - first.astype(jnp.float32)
    second = rest.astype(jnp.bfloat16)
    third = (rest - second.astype(jnp.float32)).astype(jnp.bfloat16)
    crosses = [jnp.zeros((1, rows), jnp.float32), jnp.zeros((1, rows), jnp.float32)]
    for side, scores, out in ((0, mine_ref, mine_out), (1, theirs_ref, theirs_out)):
        core = jnp.where(side == 0, core_ref[0], 1 - core_ref[0])
        row, head = row_of(place, core)
        chosen = lane == jnp.minimum(row + head, rows - 1)
        pick = jnp.where(chosen, 1.0, 0.0).astype(jnp.bfloat16)
        moved = jnp.dot(pick, first, preferred_element_type=jnp.float32)
        moved = moved + jnp.dot(pick, second, preferred_element_type=jnp.float32)
        out[...] = moved + jnp.dot(pick, third, preferred_element_type=jnp.float32)
        parts = []
        for at in range(0, rows, step):
            here = pl.ds(at, step)
            logits = out[here, :]
            weight = jnp.exp(logits - jnp.max(logits, axis=1, keepdims=True))
            parts.append(jnp.sum(weight * (logits - 0.5 * scores[here, :]), axis=1, keepdims=True))
        cross = jnp.concatenate(parts, axis=0)
        for k in (0, 1):
            inside = (lane == row + k) & (head == k)
            crosses[k] = crosses[k] + jnp.sum(jnp.where(inside, cross, 0.0), axis=0, keepdims=True)
    lines = [jnp.sum(jnp.where(eye, column, 0.0), axis=0, keepdims=True) for column in (peak, total)] + crosses
    edge = rows // 2
    tile_out[...] = jnp.concatenate([line[:, at : at + edge] for line in lines for at in (0, edge)], axis=0)


def chosen_id(ids_ref, place, row, head):
    lane = lax.broadcasted_iota(jnp.int32, place.shape, 1)
    ids = jnp.where(head == 0, ids_ref[0:1, :], ids_ref[1:2, :])
    return jnp.sum(jnp.where(lane == row, ids, 0.0), axis=1, keepdims=True)


def student_kernel(side, core_ref, hidden_ref, head_ref, ids_ref, scores_out, lines_out):
    rows, width = scores_out.shape
    step = 32
    for at in range(0, width, 256):
        scores_out[:, at : at + 256] = jnp.dot(
            hidden_ref[...], head_ref[:, at : at + 256], preferred_element_type=jnp.float32
        )
    lane = lax.broadcasted_iota(jnp.int32, (rows, rows), 1)
    place = lax.broadcasted_iota(jnp.int32, (rows, rows), 0)
    core = jnp.where(side == 0, core_ref[0], 1 - core_ref[0])
    row, head = row_of(place, core)
    ids = chosen_id(ids_ref, place, row, head)
    columns = (lax.broadcasted_iota(jnp.int32, (step, width), 1) + core_ref[1]).astype(jnp.float32)
    found = [[], [], [], []]
    for at in range(0, rows, step):
        scores = scores_out[at : at + step, :]
        peak = jnp.max(scores, axis=1, keepdims=True)
        power = jnp.exp((scores - peak) * 0.5)
        found[0].append(peak)
        found[1].append(jnp.sum(power * power, axis=1, keepdims=True))
        found[2].append(jnp.sum(power, axis=1, keepdims=True))
        found[3].append(jnp.sum(jnp.where(columns == ids[at : at + step], scores, 0.0), axis=1, keepdims=True))
    eye = lane == place
    lines = [jnp.sum(jnp.where(eye, jnp.concatenate(f, axis=0), 0.0), axis=0, keepdims=True) for f in found]
    lines_out[...] = jnp.concatenate(lines + [jnp.zeros((4, rows), jnp.float32)], axis=0)


def copy_kernel(core_ref, mine_ref, theirs_ref, stats_ref, copies_out):
    mine, theirs = mine_ref[...], theirs_ref[...]
    top = jnp.maximum(mine[0:2], theirs[0:2])
    both = [jnp.exp(a[0:2] - top) for a in (mine, theirs)]
    both = [jnp.concatenate([b, b, b, b], axis=0) for b in both]
    tile = mine * both[0] + theirs * both[1]
    tile = jnp.concatenate([top, tile[2:8]], axis=0)
    rest = jnp.concatenate([stats_ref[...], jnp.zeros_like(stats_ref)], axis=0)
    copies_out[:, 0:8, :] = jnp.broadcast_to(tile[None], copies_out[:, 0:8, :].shape)
    copies_out[:, 8:16, :] = jnp.broadcast_to(rest[None], copies_out[:, 8:16, :].shape)


def whole(shape):
    return pl.BlockSpec(shape, lambda *_: (0,) * len(shape), pipeline_mode=pl.Buffered(1))


def call(kernel, scalars, operands, results, grant, cost, scratch=()):
    return pl.pallas_call(
        kernel,
        out_shape=tuple(results),
        grid_spec=pltpu.PrefetchScalarGridSpec(
            num_scalar_prefetch=1,
            grid=(1,),
            in_specs=[whole(a.shape) for a in operands],
            out_specs=tuple(whole(a.shape) for a in results),
            scratch_shapes=scratch,
        ),
        compiler_params=pltpu.CompilerParams(vmem_limit_bytes=grant << 20),
        cost_estimate=pl.CostEstimate(flops=cost[0], bytes_accessed=cost[1], transcendentals=cost[2]),
    )(scalars, *operands)


def teacher_sum(scalars, words, mine, theirs):
    rows, width = mine.shape
    area = rows * width
    tile = jax.ShapeDtypeStruct((8, rows // 2), jnp.float32)
    half = jax.ShapeDtypeStruct(mine.shape, jnp.float32)
    scratch = [pltpu.VMEM((rows, width), jnp.float32)]
    operands = (words, mine, theirs)
    return call(teacher_kernel, scalars, operands, (half, half, tile), GRANT, (12 * rows * area, 40 * area, 3 * area), scratch)


def student_half(side, scalars, hidden, head, ids):
    rows, width = hidden.shape[0], head.shape[1]
    area = rows * width
    results = (jax.ShapeDtypeStruct((rows, width), jnp.float32), jax.ShapeDtypeStruct((8, rows), jnp.float32))
    cost = (2 * area * hidden.shape[1], 4 * area + 2 * head.size, area)
    return call(functools.partial(student_kernel, side), scalars, (hidden, head, ids), results, GRANT, cost)


def chip_copies(scalars, mine, theirs, stats, chips):
    copies = jax.ShapeDtypeStruct((chips, 16, mine.shape[1]), jnp.float32)
    return call(copy_kernel, scalars, (mine, theirs, stats), (copies,), GRANT, (mine.size, 4 * copies.size, mine.size))[0]


def slope_kernel(core_ref, shares_ref, ids_ref, mine_ref, theirs_ref, mine_t_ref, theirs_t_ref, mine_out, theirs_out, objective_out):
    devices = shares_ref.shape[0]
    rows, width = mine_ref.shape
    edge = rows // 2
    step = 32
    batch = 16
    four = lambda a: jnp.concatenate([a, a, a, a], axis=1)
    top = jnp.max(shares_ref[0:batch, 0:8, :], axis=0)
    for at in range(batch, devices, batch):
        top = jnp.maximum(top, jnp.max(shares_ref[at : at + batch, 0:8, :], axis=0))
    top = jnp.concatenate([top[0:2]] * 4, axis=0)
    sums = jnp.zeros((8, edge), jnp.float32)
    for at in range(0, devices, batch):
        part = shares_ref[at : at + batch, 0:8, :]
        sums = sums + jnp.sum(jnp.exp(four(part[:, 0:2]) - top[None]) * part, axis=0)
    line = lambda a: jnp.concatenate([a[0:1], a[1:2]], axis=1)
    t_total = sums[2:4]
    t_lse = line(top[0:2] + jnp.log(t_total))
    cross = [line(sums[4:6] / t_total), line(sums[6:8] / t_total)]

    ones, taus, targets = [], [], []
    quarter = devices // 4
    kind = lax.broadcasted_iota(jnp.int32, (batch, 8, edge), 1)
    for q in range(4):
        peak = jnp.max(shares_ref[q * quarter : (q + 1) * quarter, 8:16, :], axis=0)[0:1]
        total = jnp.zeros((8, edge), jnp.float32)
        for at in range(q * quarter, (q + 1) * quarter, batch):
            part = shares_ref[at : at + batch, 8:16, :]
            scale = jnp.exp(0.5 * (part[:, 0:1] - peak[None]))
            scale = jnp.broadcast_to(scale, part.shape)
            scale = jnp.where(kind == 1, scale * scale, jnp.where(kind == 2, scale, 1.0))
            total = total + jnp.sum(scale * part, axis=0)
        ones.append(peak + jnp.log(total[1:2]))
        taus.append(0.5 * peak + jnp.log(total[2:3]))
        targets.append(total[3:4])
    norms = jnp.transpose(jnp.concatenate(ones + taus + targets + targets, axis=0))

    lane = lax.broadcasted_iota(jnp.int32, (rows, rows), 1)
    place = lax.broadcasted_iota(jnp.int32, (rows, rows), 0)
    objective = [jnp.zeros((1, rows), jnp.float32), jnp.zeros((1, rows), jnp.float32)]
    base = core_ref[1]
    columns = (lax.broadcasted_iota(jnp.int32, (step, width), 1) + base).astype(jnp.float32)
    for side, scores, teacher, out in ((0, mine_ref, mine_t_ref, mine_out), (1, theirs_ref, theirs_t_ref, theirs_out)):
        first = (core_ref[0] == 0) == (side == 0)
        core = jnp.where(first, 0, 1)

        def column(n):
            low = jnp.concatenate([norms[:, n : n + 1], norms[:, n + 1 : n + 2]], axis=0)
            high = jnp.concatenate([norms[:, n + 2 : n + 3], norms[:, n + 3 : n + 4]], axis=0)
            return jnp.where(first, low, high)

        one, tau, target = column(0), column(4), column(8)
        row, head = row_of(place, core)
        chosen = lane == jnp.minimum(row + head, rows - 1)
        lse = jnp.sum(jnp.where(chosen, t_lse, 0.0), axis=1, keepdims=True)
        mixed = jnp.where(head == 0, cross[0], cross[1])
        mixed = jnp.sum(jnp.where(chosen, mixed, 0.0), axis=1, keepdims=True)
        weight = jnp.where((head[:, 0:1] == 1) & (row[:, 0:1] == rows - 1), 0.0, 1.0)
        loss = weight * (2.0 * (mixed - lse + tau) + 0.5 * (one - target))
        for k in (0, 1):
            inside = (lane == row) & (head == k)
            objective[k] = objective[k] + jnp.sum(jnp.where(inside, loss, 0.0), axis=0, keepdims=True)
        ids = chosen_id(ids_ref, place, row, head)
        for at in range(0, rows, step):
            here = pl.ds(at, step)
            part = slice(at, at + step)
            score = scores[here, :]
            grad = jnp.exp(0.5 * score - tau[part]) - jnp.exp(teacher[here, :] - lse[part])
            hit = jnp.where(columns == ids[part], 1.0, 0.0)
            grad = weight[part] * (grad + 0.5 * (jnp.exp(score - one[part]) - hit))
            out[here, :] = grad.astype(jnp.bfloat16)
    objective_out[...] = jnp.concatenate(objective + [jnp.zeros((6, rows), jnp.float32)], axis=0)


def slopes(scalars, *operands):
    half = jax.ShapeDtypeStruct(operands[2].shape, jnp.bfloat16)
    lines = jax.ShapeDtypeStruct((8, half.shape[0]), jnp.float32)
    area = operands[2].size
    return call(slope_kernel, scalars, operands, (half, half, lines), GRANT, (40 * area, 24 * area, 6 * area))


def merge(parts):
    peak = jnp.max(parts[:, 0], axis=0)
    scale = jnp.exp((parts[:, 0] - peak) * 0.5)
    return jnp.stack(
        [
            peak,
            jnp.sum(parts[:, 1] * (scale * scale), axis=0),
            jnp.sum(parts[:, 2] * scale, axis=0),
            jnp.sum(parts[:, 3], axis=0),
        ]
    )


def place_kernel(count, places_ref, *refs):
    blocks, out_ref = refs[:count], refs[count]
    rows = blocks[0].shape[0]
    for i, block in enumerate(blocks):
        at = pl.multiple_of(places_ref[i] * rows, rows)
        out_ref[pl.ds(at, rows), :] = block[...]


def place_blocks(places, *blocks):
    count = len(blocks)
    rows, width = blocks[0].shape
    result = jax.ShapeDtypeStruct((count * rows, width), blocks[0].dtype)
    cost = (0, 4 * result.size, 0)
    return call(functools.partial(place_kernel, count), places, blocks, (result,), GRANT, cost)[0]


def ring_gather(block, axis):
    size = lax.axis_size(axis)
    here = lax.axis_index(axis)
    blocks = [block]
    for step in range(1, size):
        blocks.append(lax.ppermute(block, axis, [(i, (i + step) % size) for i in range(size)]))
    return place_blocks((here + size - jnp.arange(size, dtype=jnp.int32)) % size, *blocks)


def everywhere(value, axes, count):
    copies = jnp.broadcast_to(value, (count,) + value.shape)
    return lax.all_to_all(copies, axes, 0, 0, tiled=True)


def local(teacher_hidden, teacher_head, student_hidden, student_head, target_ids):
    core = lax.axis_index("c")
    chips = lax.axis_size(WALK)
    stripes = teacher_head.shape[1]
    voc = teacher_head.shape[2]
    rows = teacher_hidden.shape[0]
    width = student_head.shape[0]
    base = lax.axis_index(TOK + VOC) * voc
    pair = [(0, 1), (1, 0)]

    partial = jnp.einsum("rd,dsv->srv", teacher_hidden, teacher_head, preferred_element_type=jnp.float32)
    words = encode(partial)
    words = words.reshape((2, 2, 2) + words.shape[1:]).transpose(2, 1, 0, 3, 4).reshape(words.shape)
    words = lax.all_to_all(words, STRIPES, 0, 0, tiled=True)

    plane = jnp.swapaxes(student_hidden, 0, 1).reshape(4, width)
    plane = everywhere(plane, ("yh", "yl", "xh", "xl"), 16).reshape(64, width)

    own = ring_gather(plane, "z")
    other = lax.ppermute(own, "c", pair)

    scalars = jnp.stack([core, base])
    ids = target_ids.T.astype(jnp.float32)
    own_scores, own_stats = student_half(0, scalars, own, student_head, ids)
    other_scores, other_stats = student_half(1, scalars, other, student_head, ids)
    own_stats, other_stats = own_stats[:4], other_stats[:4]
    stats = jnp.stack(
        [jnp.where(core == 0, own_stats, other_stats), jnp.where(core == 0, other_stats, own_stats)], axis=1
    ).reshape(4, 2 * rows)
    around = [stats] + [lax.ppermute(stats, "z", [(i, (i + j) % 4) for i in range(4)]) for j in (1, 2, 3)]
    stats = merge(jnp.stack(around)).reshape(4, 4, rows // 2)
    stats = lax.dynamic_index_in_dim(stats, lax.axis_index("z"), 1, False)
    stats = stats + 0.0 * words[0, 0, 0].astype(jnp.float32)
    stats = merge(jnp.stack([stats, lax.ppermute(stats, "c", pair)]))

    own_teacher, other_teacher, tile = teacher_sum(scalars, words, own_scores, other_scores)
    copies = chip_copies(scalars, tile, lax.ppermute(tile, "c", pair), stats, chips)
    shares = lax.all_to_all(copies, EXCHANGE, 0, 0, tiled=True)
    own_grad, other_grad, objective = slopes(
        scalars, shares, ids, own_scores, other_scores, own_teacher, other_teacher
    )

    contract = (((1,), (1,)), ((), ()))
    give = lax.dot_general(other_grad, student_head, contract, preferred_element_type=jnp.float32)
    taken = lax.ppermute(give, "c", pair)
    keep = lax.dot_general(own_grad, student_head, contract, preferred_element_type=jnp.float32)
    grad = jnp.concatenate([own_grad, other_grad], axis=0)
    objective = objective[:2].T

    share = (keep + taken).astype(jnp.bfloat16).reshape(chips, 4, width)
    late = (jnp.abs(share[0, 0, 0].astype(jnp.float32)) > 3e38).astype(jnp.int32)
    hidden = place_blocks(jnp.arange(2, dtype=jnp.int32) + late, own, other)
    grad_head = lax.dot_general(
        hidden, grad, (((0,), (0,)), ((), ())), preferred_element_type=jnp.float32
    ).astype(jnp.bfloat16)
    share = lax.all_to_all(share, WALK, 0, 0, tiled=True)
    grad_hidden = jnp.sum(share.astype(jnp.float32), axis=0).astype(jnp.bfloat16)
    grad_hidden = jnp.swapaxes(grad_hidden.reshape(2, 2, width), 0, 1)
    return objective, grad_hidden, grad_head


def solution(mesh):
    fine = Mesh(mesh.devices.reshape(SIZES), TOK + VOC)
    return jax.shard_map(
        local,
        mesh=fine,
        in_specs=(
            P(None, TOK),
            P(TOK, None, VOC),
            P(TOK + VOC, None, None),
            P(None, TOK + VOC),
            P(),
        ),
        out_specs=(P(), P(TOK + VOC, None, None), P(None, TOK + VOC)),
        check_vma=False,
    )
```
